32 devices in a mesh: fsdp: 32 (over z, y, x, core).
Axes of the slice: x: 2, y: 2, z: 4, core: 2. Of those that a mesh axis runs over, the one named last changes fastest.
Arguments:
- slow_in: bfloat16 [512, 14, 14, 1024], P('fsdp'), may hold values from -6 to 6
- fast_in: bfloat16 [2048, 14, 14, 128], P('fsdp'), may hold values from -6 to 6
- clip_ids: int32 [32, 16], P('fsdp'), may hold values from 0 to 7, never falling along the last dimension, each value on 1 to 8 neighbouring positions
- lateral_weight: bfloat16 [640, 256], P(None, 'fsdp'), may hold values from -0.25 to 0.25
- first_weight: bfloat16 [3840, 256], P('fsdp'), may hold values from -0.09375 to 0.09375
- middle_weight: bfloat16 [2304, 256], P('fsdp'), may hold values from -0.125 to 0.125
- last_weight: bfloat16 [256, 1024], P('fsdp'), may hold values from -0.375 to 0.375
- proj_weight: bfloat16 [1280, 1024], P('fsdp'), may hold values from -0.15625 to 0.15625
- lat_norm: bfloat16 [2, 256], P(None, 'fsdp'), may hold values from 0.099609375 to 1.8984375
- one_norm: bfloat16 [2, 256], P(None, 'fsdp'), may hold values from 0.099609375 to 1.8984375
- two_norm: bfloat16 [2, 256], P(None, 'fsdp'), may hold values from 0.099609375 to 1.8984375
- out_norm: bfloat16 [2, 1024], P(None, 'fsdp'), may hold values from 0.099609375 to 1.8984375
- proj_norm: bfloat16 [2, 1024], P(None, 'fsdp'), may hold values from 0.099609375 to 1.8984375
- fast_first: bfloat16 [384, 32], replicated, may hold values from -0.3125 to 0.3125
- fast_middle: bfloat16 [288, 32], replicated, may hold values from -0.375 to 0.375
- fast_last: bfloat16 [32, 128], replicated, may hold values from -1 to 1
- fast_proj: bfloat16 [128, 128], replicated, may hold values from -0.5 to 0.5
- fast_mid_norm: bfloat16 [2, 2, 32], replicated, may hold values from 0.099609375 to 1.8984375
- fast_out_norm: bfloat16 [2, 2, 128], replicated, may hold values from 0.099609375 to 1.8984375
- slow_cot: bfloat16 [512, 14, 14, 1024], P('fsdp'), may hold values from -6 to 6
- fast_cot: bfloat16 [2048, 14, 14, 128], P('fsdp'), may hold values from -6 to 6
Outputs:
- slow_out: bfloat16 [512, 14, 14, 1024], P('fsdp')
- fast_out: bfloat16 [2048, 14, 14, 128], P('fsdp')
- slow_in_grad: bfloat16 [512, 14, 14, 1024], P('fsdp')
- fast_in_grad: bfloat16 [2048, 14, 14, 128], P('fsdp')
- lateral_grad: float32 [640, 256], P(None, 'fsdp')
- first_grad: float32 [3840, 256], P('fsdp')
- middle_grad: float32 [2304, 256], P('fsdp')
- last_grad: float32 [256, 1024], P('fsdp')
- proj_grad: float32 [1280, 1024], P('fsdp')
- lat_norm_grad: float32 [2, 256], P(None, 'fsdp')
- one_norm_grad: float32 [2, 256], P(None, 'fsdp')
- two_norm_grad: float32 [2, 256], P(None, 'fsdp')
- out_norm_grad: float32 [2, 1024], P(None, 'fsdp')
- proj_norm_grad: float32 [2, 1024], P(None, 'fsdp')
- fast_first_grad: float32 [384, 32], replicated
- fast_middle_grad: float32 [288, 32], replicated
- fast_last_grad: float32 [32, 128], replicated
- fast_proj_grad: float32 [128, 128], replicated
- fast_mid_norm_grad: float32 [2, 2, 32], replicated
- fast_out_norm_grad: float32 [2, 2, 128], replicated
The draws below stay inside these ranges and needn't reach their ends.
Inputs may be any that keep to these rules, and one draw needn't show every extreme that they name: `clip_ids`: each row holds the slow frames of one device in 8 clips; clip numbers never fall along a row and a clip never continues into the next row; each clip has 1 to 8 frames, and every row holds at least one clip of exactly 8 frames.
All inputs are finite; a program needn't handle non-finite values.
Results may differ from the reference program's by a relative error of at most 0.0089.
Values may be sent and summed in bfloat16 or wider, within the bound.
A program may use at most 384 MiB of HBM per device.

```python
import math
import jax
import jax.numpy as jnp
import numpy as np
from jax import lax

CS_IN = 1024
CL = 256
CS_MID = 256
CF = 128
CF_MID = 32
SIDE = 14
FR = 16
FRAMES = 512
N_FSDP = 32


def block_scale(key, dims, split, smallest, high):
    factor_of = 1.0
    for position, shards_of in split:
        draws = jax.random.uniform(jax.random.fold_in(jax.random.fold_in(key, 6), position), (shards_of,), jnp.float32, smallest / len(split), high / len(split))
        factor_of = factor_of * jnp.repeat(jnp.exp(draws), dims[position] // shards_of).reshape((-1,) + (1,) * (len(dims) - 1 - position))
    return factor_of


def length_profile(count, total, bound, slope):
    loads = [(1 << 20) // math.isqrt(standing ** slope) + 1 for standing in range(2, count + 1)]
    surplus, counts = total - bound - (count - 1), [1] * (count - 1)
    while surplus > 0:
        movable = [i for i in range(count - 1) if counts[i] < bound]
        mass, remaining = sum([loads[i] for i in movable]), surplus
        for i in movable:
            more = min(bound - counts[i], max(1, remaining * loads[i] // mass), surplus)
            counts[i] = counts[i] + more
            surplus = surplus - more
    return np.array([bound] + counts)


def uneven_parts(own_key, number_of, total, most, lean):
    if number_of == 2:
        one = jax.random.randint(own_key, (), max(1, total - most), min(most, total - 1) + 1)
        return jnp.stack([one, total - one])
    tallies = jnp.asarray(length_profile(number_of, total, most, lean), jnp.int32)
    pairs = (number_of - 1) // 2
    source_of, sink = tallies[1:1 + 2 * pairs:2], tallies[2:2 + 2 * pairs:2]
    slack = jnp.minimum(source_of - 1, most - sink)
    passed = jax.random.randint(jax.random.fold_in(own_key, 1), (pairs,), 0, 1 << 20) % (slack + 1)
    tallies = tallies.at[1:1 + 2 * pairs:2].set(source_of - passed).at[2:2 + 2 * pairs:2].set(sink + passed)
    return tallies[jax.random.permutation(jax.random.fold_in(own_key, 2), number_of)]


def scatter_about(key, dims, spread, most, cuts=(), held_as=jnp.bfloat16):
    result = spread * jax.random.normal(key, dims, jnp.float32)
    if cuts:
        result = result * block_scale(key, dims, cuts, -0.22, 0.18)
    return jnp.clip(result, -most, most).astype(held_as)


def setup_inputs(seed: int = 0) -> dict:
    arg_keys = jax.random.split(jax.random.key(seed), 22)
    slow_in = scatter_about(arg_keys[0], (FRAMES, SIDE, SIDE, CS_IN), 1.0, 6.0, ((0, 32),))
    fast_in = scatter_about(arg_keys[1], (4 * FRAMES, SIDE, SIDE, CF), 1.0, 6.0, ((0, 32),))
    clip_ids = jax.vmap(lambda own: jnp.searchsorted(jnp.cumsum(uneven_parts(own, (FR + 1) // 2, FR, max(FR // 2, 2), 2)), jnp.arange(FR), side="right"))(jax.random.split(arg_keys[2], N_FSDP)).reshape((N_FSDP, FR)).astype(jnp.int32)
    lateral_weight = scatter_about(arg_keys[3], (5 * CF, CL), (5 * CF) ** -0.5, 0.25, ((1, 32),))
    first_weight = scatter_about(arg_keys[4], (3 * (CS_IN + CL), CS_MID), (3 * (CS_IN + CL)) ** -0.5, 0.09375, ((0, 32),))
    middle_weight = scatter_about(arg_keys[5], (9 * CS_MID, CS_MID), (9 * CS_MID) ** -0.5, 0.125, ((0, 32),))
    last_weight = scatter_about(arg_keys[6], (CS_MID, CS_IN), CS_MID ** -0.5, 0.375, ((0, 32),))
    proj_weight = scatter_about(arg_keys[7], (CS_IN + CL, CS_IN), (CS_IN + CL) ** -0.5, 0.15625, ((0, 32),))
    lat_norm = jnp.clip(1.0 + 0.18 * jax.random.normal(arg_keys[8], (2, CL), jnp.float32), 0.099609375, 1.8984375).astype(jnp.bfloat16)
    one_norm = jnp.clip(1.0 + 0.18 * jax.random.normal(arg_keys[9], (2, CS_MID), jnp.float32), 0.099609375, 1.8984375).astype(jnp.bfloat16)
    two_norm = jnp.clip(1.0 + 0.18 * jax.random.normal(arg_keys[10], (2, CS_MID), jnp.float32), 0.099609375, 1.8984375).astype(jnp.bfloat16)
    out_norm = jnp.clip(1.0 + 0.18 * jax.random.normal(arg_keys[11], (2, CS_IN), jnp.float32), 0.099609375, 1.8984375).astype(jnp.bfloat16)
    proj_norm = jnp.clip(1.0 + 0.18 * jax.random.normal(arg_keys[12], (2, CS_IN), jnp.float32), 0.099609375, 1.8984375).astype(jnp.bfloat16)
    fast_first = scatter_about(arg_keys[13], (3 * CF, CF_MID), (3 * CF) ** -0.5, 0.3125)
    fast_middle = scatter_about(arg_keys[14], (9 * CF_MID, CF_MID), (9 * CF_MID) ** -0.5, 0.375)
    fast_last = scatter_about(arg_keys[15], (CF_MID, CF), CF_MID ** -0.5, 1.0)
    fast_proj = scatter_about(arg_keys[16], (CF, CF), CF ** -0.5, 0.5)
    fast_mid_norm = jnp.clip(1.0 + 0.18 * jax.random.normal(arg_keys[17], (2, 2, CF_MID), jnp.float32), 0.099609375, 1.8984375).astype(jnp.bfloat16)
    fast_out_norm = jnp.clip(1.0 + 0.18 * jax.random.normal(arg_keys[18], (2, 2, CF), jnp.float32), 0.099609375, 1.8984375).astype(jnp.bfloat16)
    slow_cot = scatter_about(arg_keys[19], (FRAMES, SIDE, SIDE, CS_IN), 1.0, 6.0, ((0, 32),))
    fast_cot = scatter_about(arg_keys[20], (4 * FRAMES, SIDE, SIDE, CF), 1.0, 6.0, ((0, 32),))
    return dict(slow_in=slow_in, fast_in=fast_in, clip_ids=clip_ids, lateral_weight=lateral_weight, first_weight=first_weight, middle_weight=middle_weight, last_weight=last_weight, proj_weight=proj_weight, lat_norm=lat_norm, one_norm=one_norm, two_norm=two_norm, out_norm=out_norm, proj_norm=proj_norm, fast_first=fast_first, fast_middle=fast_middle, fast_last=fast_last, fast_proj=fast_proj, fast_mid_norm=fast_mid_norm, fast_out_norm=fast_out_norm, slow_cot=slow_cot, fast_cot=fast_cot)


@jax.custom_vjp
def low(v):
    return lax.optimization_barrier(v.astype(jnp.bfloat16)).astype(jnp.float32)

@jax.custom_vjp
def low_back(v):
    return v

def low_keep(v):
    return (low(v), None)

def low_pass(kept, grad):
    return (grad,)

def back_keep(v):
    return (v, None)

def back_low(kept, grad):
    return (low(grad),)
low.defvjp(low_keep, low_pass)
low_back.defvjp(back_keep, back_low)
EPSILON = 1e-05

def matmul(operand, weight):
    return jnp.einsum('fhwc,cd->fhwd', operand, weight, precision=lax.Precision.HIGHEST)

def clip_edges(clip_ids):
    same = clip_ids[:, 1:] == clip_ids[:, :-1]
    closed = jnp.zeros((clip_ids.shape[0], 1), dtype=bool)
    has_prev = jnp.concatenate([closed, same], axis=1).reshape(-1)
    has_next = jnp.concatenate([same, closed], axis=1).reshape(-1)
    return (has_prev, has_next)

def fast_edges(has_prev, has_next):
    within = jnp.arange(4)
    fast_prev = ((within[None, :] != 0) | has_prev[:, None]).reshape(-1)
    fast_next = ((within[None, :] != 3) | has_next[:, None]).reshape(-1)
    return (fast_prev, fast_next)

def masked(field, keep_mask):
    return jnp.where(keep_mask[:, None, None, None], field, jnp.zeros_like(field))

def shift_down(field):
    return jnp.concatenate([jnp.zeros_like(field[:1]), field[:-1]], axis=0)

def shift_up(field):
    return jnp.concatenate([field[1:], jnp.zeros_like(field[:1])], axis=0)

def temporal_cols(field, has_prev, has_next):
    return jnp.concatenate([masked(shift_down(field), has_prev), field, masked(shift_up(field), has_next)], axis=-1)

def spatial_cols(field):
    extent = field.shape[1]
    padded = jnp.pad(field, ((0, 0), (1, 1), (1, 1), (0, 0)))
    pieces = []
    for row_off in range(3):
        for col_off in range(3):
            pieces.append(padded[:, row_off:row_off + extent, col_off:col_off + extent, :])
    return jnp.concatenate(pieces, axis=-1)

def lateral_cols(fast, has_prev):
    frames = fast.shape[0] // 4
    grouped = fast.reshape((frames, 4) + fast.shape[1:])
    return jnp.concatenate([masked(shift_down(grouped[:, 2]), has_prev), masked(shift_down(grouped[:, 3]), has_prev), grouped[:, 0], grouped[:, 1], grouped[:, 2]], axis=-1)

def batch_norm(field, norm_pair):
    average = lax.optimization_barrier(jnp.mean(field, axis=(0, 1, 2)))
    variance = lax.optimization_barrier(jnp.mean(jnp.square(field - average), axis=(0, 1, 2)))
    return (field - average) * lax.rsqrt(variance + EPSILON) * norm_pair[0] + norm_pair[1]

def reference(slow_in, fast_in, clip_ids, lateral_weight, first_weight, middle_weight, last_weight, proj_weight, lat_norm, one_norm, two_norm, out_norm, proj_norm, fast_first, fast_middle, fast_last, fast_proj, fast_mid_norm, fast_out_norm, slow_cot, fast_cot):
    has_prev, has_next = clip_edges(clip_ids)
    fast_prev, fast_next = fast_edges(has_prev, has_next)

    def forward(params):
        slow_x, fast_x, weight_lat, weight_one, weight_two, weight_three, weight_proj, gain_lat, gain_one, gain_two, gain_out, gain_proj, fast_one, fast_two, fast_three, fast_skip, gain_fmid, gain_fout = params
        lat_pre = low_back(matmul(lateral_cols(fast_x, has_prev), weight_lat))
        lateral = low(jax.nn.silu(batch_norm(lat_pre, gain_lat)))
        joined = jnp.concatenate([slow_x, lateral], axis=-1)
        one_pre = low_back(matmul(temporal_cols(joined, has_prev, has_next), weight_one))
        one_act = low(jax.nn.silu(batch_norm(one_pre, gain_one)))
        two_pre = low_back(matmul(spatial_cols(one_act), weight_two))
        two_act = low(jax.nn.silu(batch_norm(two_pre, gain_two)))
        three_pre = low_back(matmul(two_act, weight_three))
        proj_pre = low_back(matmul(joined, weight_proj))
        slow_out = jax.nn.silu(batch_norm(three_pre, gain_out) + batch_norm(proj_pre, gain_proj))
        fone_pre = low_back(matmul(temporal_cols(fast_x, fast_prev, fast_next), fast_one))
        fone_act = low(jax.nn.silu(batch_norm(fone_pre, gain_fmid[0])))
        ftwo_pre = low_back(matmul(spatial_cols(fone_act), fast_two))
        ftwo_act = low(jax.nn.silu(batch_norm(ftwo_pre, gain_fmid[1])))
        fthree_pre = low_back(matmul(ftwo_act, fast_three))
        fskip_pre = low_back(matmul(fast_x, fast_skip))
        fast_out = jax.nn.silu(batch_norm(fthree_pre, gain_fout[0]) + batch_norm(fskip_pre, gain_fout[1]))
        return (slow_out, fast_out)
    inputs = (slow_in, fast_in, lateral_weight, first_weight, middle_weight, last_weight, proj_weight, lat_norm, one_norm, two_norm, out_norm, proj_norm, fast_first, fast_middle, fast_last, fast_proj, fast_mid_norm, fast_out_norm)
    params = tuple((item.astype(jnp.float32) for item in inputs))
    (slow_out, fast_out), pullback = jax.vjp(forward, params)
    grads = pullback((slow_cot.astype(jnp.float32), fast_cot.astype(jnp.float32)))[0]
    return (slow_out.astype(jnp.bfloat16), fast_out.astype(jnp.bfloat16), grads[0].astype(jnp.bfloat16), grads[1].astype(jnp.bfloat16), grads[2], grads[3], grads[4], grads[5], grads[6], grads[7], grads[8], grads[9], grads[10], grads[11], grads[12], grads[13], grads[14], grads[15], grads[16], grads[17])
```

```python
import functools

import jax
import jax.numpy as jnp
from jax import lax
from jax.experimental import pallas as pl
from jax.experimental.pallas import tpu as pltpu
from jax.sharding import PartitionSpec as P

EPSILON = 1e-05

MESH = pl.DeviceIdType.MESH

def exch_kernel(n, inner, count, centred, x_ref, o_ref, near, far, mid, near_send, near_recv, far_send, far_recv):
    me = lax.axis_index("fsdp")
    outer = n // inner
    mi = lax.rem(me, inner)
    mo = lax.div(me, inner)
    barrier = pltpu.get_barrier_semaphore()
    for k in range(1, inner):
        pl.semaphore_signal(barrier, inc=1, device_id=(mo * inner + lax.rem(mi + k, inner),), device_id_type=MESH)
    for k in range(1, outer):
        pl.semaphore_signal(barrier, inc=1, device_id=(lax.rem(mo + k, outer) * inner + mi,), device_id_type=MESH)
    pl.semaphore_wait(barrier, inner - 1 + outer - 1)

    def swap(src, slots, sends, recvs, mine, size, peer):
        copies = []
        for k in range(1, size):
            c = pltpu.make_async_remote_copy(src_ref=src, dst_ref=slots.at[mine], send_sem=sends.at[k], recv_sem=recvs.at[k],
                device_id=(peer(k),), device_id_type=MESH)
            c.start()
            copies.append(c)
        slots[mine] = src[...]
        for c in copies:
            c.wait()

    def merge(slots, size, weight):
        if not centred:
            t = slots[0]
            for k in range(1, size):
                t = t + slots[k]
            return t
        m = slots[0, 0:1]
        for k in range(1, size):
            m = m + slots[k, 0:1]
        m = m * (1.0 / size)
        s = None
        for k in range(size):
            d = slots[k, 0:1] - m
            v = slots[k, 1:2] + d * d * weight
            s = v if s is None else s + v
        return jnp.concatenate([m, s], axis=0)

    swap(x_ref, near, near_send, near_recv, mi, inner, lambda k: mo * inner + lax.rem(mi + k, inner))
    mid[...] = merge(near, inner, float(count))
    if outer > 1:
        swap(mid, far, far_send, far_recv, mo, outer, lambda k: lax.rem(mo + k, outer) * inner + mi)
        o_ref[...] = merge(far, outer, float(count * inner))
    else:
        o_ref[...] = mid[...]

def exchange(x, n, inner, cid, count=1.0, centred=False):
    outer = n // inner
    return pl.pallas_call(
        functools.partial(exch_kernel, n, inner, count, centred),
        out_shape=jax.ShapeDtypeStruct(x.shape, x.dtype),
        in_specs=[pl.BlockSpec(memory_space=pltpu.VMEM)],
        out_specs=pl.BlockSpec(memory_space=pltpu.VMEM),
        scratch_shapes=[pltpu.VMEM((inner,) + x.shape, x.dtype), pltpu.VMEM((outer,) + x.shape, x.dtype), pltpu.VMEM(x.shape, x.dtype),
            pltpu.SemaphoreType.DMA((inner,)), pltpu.SemaphoreType.DMA((inner,)),
            pltpu.SemaphoreType.DMA((outer,)), pltpu.SemaphoreType.DMA((outer,))],
        compiler_params=pltpu.CompilerParams(collective_id=cid, has_side_effects=True),
    )(x)

def places(n):
    me = lax.axis_index("fsdp")
    z = lax.div(me, 8)
    y = lax.rem(lax.div(me, 4), 2)
    x = lax.rem(lax.div(me, 2), 2)
    c = lax.rem(me, 2)
    return z, y, x, c

def flat(z, y, x, c):
    return ((z * 2 + y) * 2 + x) * 2 + c

def meet(n):
    z, y, x, c = places(n)
    depth = n // 8
    barrier = pltpu.get_barrier_semaphore()
    peers = [flat(lax.rem(z + k, depth), y, x, c) for k in range(1, depth)]
    peers += [flat(z, y, x, 1 - c), flat(z, y, 1 - x, c), flat(z, 1 - y, x, c)]
    for peer in peers:
        pl.semaphore_signal(barrier, inc=1, device_id=(peer,), device_id_type=MESH)
    pl.semaphore_wait(barrier, len(peers))

def gather_kernel(n, turns, *refs):
    k = len(turns)
    ins, outs = refs[:k], refs[k:2 * k]
    own_sem, z_send, z_recv, p_send, p_recv, c_send, c_recv = refs[2 * k:]
    depth = n // 8
    z, y, x, c = places(n)
    meet(n)
    def start(src, dst, ss, rs, dev):
        d = pltpu.make_async_remote_copy(src_ref=src, dst_ref=dst, send_sem=ss, recv_sem=rs, device_id=(dev,), device_id_type=MESH)
        d.start()
        return d
    core = flat(z, y, x, 1 - c)
    tail = []
    zc, own = [], []
    for i in range(k):
        o = pltpu.make_async_copy(ins[i], outs[i].at[z, y, x, c], own_sem.at[i])
        o.start()
        own.append(o)
        zc.append([start(ins[i], outs[i].at[z, y, x, c], z_send.at[i, s], z_recv.at[i, s], flat(lax.rem(z + s, depth), y, x, c)) for s in range(1, depth)])
    pc = []
    for i in range(k):
        own[i].wait()
        for d in zc[i]:
            d.wait()
        dev = flat(z, y, 1 - x, c) if turns[i] == 0 else flat(z, 1 - y, x, c)
        part = outs[i].at[:, y, x, c]
        pc.append(start(part, part, p_send.at[i, 0], p_recv.at[i, 0], dev))
        tail.append(start(part, part, c_send.at[i, 0], c_recv.at[i, 0], core))
    qc = []
    for i in range(k):
        pc[i].wait()
        if turns[i] == 0:
            part, new, dev = outs[i].at[:, y, :, c], outs[i].at[:, y, 1 - x, c], flat(z, 1 - y, x, c)
        else:
            part, new, dev = outs[i].at[:, :, x, c], outs[i].at[:, 1 - y, x, c], flat(z, y, 1 - x, c)
        qc.append(start(part, part, p_send.at[i, 1], p_recv.at[i, 1], dev))
        tail.append(start(new, new, c_send.at[i, 1], c_recv.at[i, 1], core))
    for i in range(k):
        qc[i].wait()
        new = outs[i].at[:, 1 - y, :, c] if turns[i] == 0 else outs[i].at[:, :, 1 - x, c]
        tail.append(start(new, new, c_send.at[i, 2], c_recv.at[i, 2], core))
    for d in tail:
        d.wait()

def gather_all(arrays, turns, n, cid):
    k = len(arrays)
    depth = n // 8
    DS = pltpu.SemaphoreType.DMA
    outs = pl.pallas_call(
        functools.partial(gather_kernel, n, turns),
        out_shape=[jax.ShapeDtypeStruct((depth, 2, 2, 2) + a.shape, a.dtype) for a in arrays],
        in_specs=[pl.BlockSpec(memory_space=pl.ANY)] * k,
        out_specs=[pl.BlockSpec(memory_space=pl.ANY)] * k,
        scratch_shapes=[DS((k,)), DS((k, depth)), DS((k, depth)), DS((k, 2)), DS((k, 2)), DS((k, 3)), DS((k, 3))],
        compiler_params=pltpu.CompilerParams(collective_id=cid, has_side_effects=True),
    )(*arrays)
    return [o.reshape((n,) + a.shape) for o, a in zip(outs, arrays)]

def scatter_kernel(n, turns, *refs):
    k = len(turns)
    ins, outs = refs[:k], refs[k:2 * k]
    rest = refs[2 * k:]
    half, r1, r2, r3, r4 = (rest[j * k:(j + 1) * k] for j in range(5))
    own_sem, c_sem, p_sem, q_sem, z_send, z_recv = rest[5 * k:]
    depth = n // 8
    z, y, x, c = places(n)
    meet(n)
    def start(src, dst, ss, rs, dev):
        d = pltpu.make_async_remote_copy(src_ref=src, dst_ref=dst, send_sem=ss, recv_sem=rs, device_id=(dev,), device_id_type=MESH)
        d.start()
        return d
    def add(target, other):
        target[...] = (target[...].astype(jnp.float32) + other[...].astype(jnp.float32)).astype(target.dtype)
    def pairs(i):
        if turns[i] == 0:
            return (lambda zz, o: half[i].at[zz, o, x]), (lambda zz: half[i].at[zz, y, x])
        return (lambda zz, o: half[i].at[zz, y, o]), (lambda zz: half[i].at[zz, y, x])
    own, cc, pc, qc, zc = [], [], [], [], []
    for i in range(k):
        o = pltpu.make_async_copy(ins[i].at[:, :, :, c], half[i], own_sem.at[i])
        o.start()
        own.append(o)
        cc.append(start(ins[i].at[:, :, :, 1 - c], r1[i], c_sem.at[i, 0], c_sem.at[i, 1], flat(z, y, x, 1 - c)))
    for i in range(k):
        own[i].wait()
        cc[i].wait()
        @pl.loop(0, depth)
        def _(zz):
            for a in range(2):
                for b in range(2):
                    add(half[i].at[zz, a, b], r1[i].at[zz, a, b])
        if turns[i] == 0:
            src, dev = half[i].at[:, :, 1 - x], flat(z, y, 1 - x, c)
        else:
            src, dev = half[i].at[:, 1 - y], flat(z, 1 - y, x, c)
        pc.append(start(src, r2[i], p_sem.at[i, 0], p_sem.at[i, 1], dev))
    for i in range(k):
        pc[i].wait()
        view, last = pairs(i)
        @pl.loop(0, depth)
        def _(zz):
            for o in range(2):
                add(view(zz, o), r2[i].at[zz, o])
        if turns[i] == 0:
            src, dev = half[i].at[:, 1 - y, x], flat(z, 1 - y, x, c)
        else:
            src, dev = half[i].at[:, y, 1 - x], flat(z, y, 1 - x, c)
        qc.append(start(src, r3[i], q_sem.at[i, 0], q_sem.at[i, 1], dev))
    for i in range(k):
        qc[i].wait()
        view, last = pairs(i)
        @pl.loop(0, depth)
        def _(zz):
            add(last(zz), r3[i].at[zz])
        for s in range(1, depth):
            zz = lax.rem(z + s, depth)
            zc.append((i, s, start(last(zz), r4[i].at[s], z_send.at[i, s], z_recv.at[i, s], flat(zz, y, x, c))))
    for i in range(k):
        view, last = pairs(i)
        outs[i][...] = last(z)[...].astype(jnp.float32)
        for j, s, d in zc:
            if j == i:
                d.wait()
                outs[i][...] += r4[i][s].astype(jnp.float32)

def scatter_all(arrays, turns, n, cid):
    k = len(arrays)
    depth = n // 8
    DS = pltpu.SemaphoreType.DMA
    six = [a.reshape((depth, 2, 2, 2) + a.shape[1:]) for a in arrays]
    def buf(lead):
        return [pltpu.VMEM(lead + a.shape[1:], a.dtype) for a in arrays]
    return pl.pallas_call(
        functools.partial(scatter_kernel, n, turns),
        out_shape=[jax.ShapeDtypeStruct(a.shape[1:], jnp.float32) for a in arrays],
        in_specs=[pl.BlockSpec(memory_space=pl.ANY)] * k,
        out_specs=[pl.BlockSpec(memory_space=pltpu.VMEM)] * k,
        scratch_shapes=buf((depth, 2, 2)) + buf((depth, 2, 2)) + buf((depth, 2)) + buf((depth,)) + buf((depth,))
        + [DS((k,)), DS((k, 2)), DS((k, 2)), DS((k, 2)), DS((k, depth)), DS((k, depth))],
        compiler_params=pltpu.CompilerParams(collective_id=cid, has_side_effects=True, vmem_limit_bytes=60 * 1024 * 1024),
    )(*six)


def product(operand, weight):
    return jnp.einsum("fhwc,cd->fhwd", operand, weight, preferred_element_type=jnp.float32)


def back_product(gradient, weight):
    return jnp.einsum("fhwd,cd->fhwc", gradient, weight, preferred_element_type=jnp.float32)


def weight_term(columns, gradient):
    return jnp.einsum("fhwc,fhwd->cd", columns, gradient, preferred_element_type=jnp.float32)


def clip_edges(clip_ids):
    same = clip_ids[:, 1:] == clip_ids[:, :-1]
    closed = jnp.zeros((clip_ids.shape[0], 1), dtype=bool)
    has_prev = jnp.concatenate([closed, same], axis=1).reshape(-1)
    has_next = jnp.concatenate([same, closed], axis=1).reshape(-1)
    return (has_prev, has_next)


def fast_edges(has_prev, has_next):
    within = jnp.arange(4)
    fast_prev = ((within[None, :] != 0) | has_prev[:, None]).reshape(-1)
    fast_next = ((within[None, :] != 3) | has_next[:, None]).reshape(-1)
    return (fast_prev, fast_next)


def masked(field, keep_mask):
    return jnp.where(keep_mask[:, None, None, None], field, jnp.zeros_like(field))


def shift_down(field):
    return jnp.concatenate([jnp.zeros_like(field[:1]), field[:-1]], axis=0)


def shift_up(field):
    return jnp.concatenate([field[1:], jnp.zeros_like(field[:1])], axis=0)


def temporal_cols(field, has_prev, has_next):
    return jnp.concatenate(
        [masked(shift_down(field), has_prev), field, masked(shift_up(field), has_next)], axis=-1
    )


def temporal_back(grad_cols, has_prev, has_next):
    width = grad_cols.shape[-1] // 3
    before = masked(grad_cols[..., :width], has_prev)
    after = masked(grad_cols[..., 2 * width :], has_next)
    return grad_cols[..., width : 2 * width] + shift_up(before) + shift_down(after)


def spatial_cols(field):
    extent = field.shape[1]
    padded = jnp.pad(field, ((0, 0), (1, 1), (1, 1), (0, 0)))
    pieces = []
    for row_off in range(3):
        for col_off in range(3):
            pieces.append(padded[:, row_off : row_off + extent, col_off : col_off + extent, :])
    return jnp.concatenate(pieces, axis=-1)


def spatial_back(grad_cols):
    width = grad_cols.shape[-1] // 9
    extent = grad_cols.shape[1]
    total = None
    for position in range(9):
        row_off = position // 3
        col_off = position % 3
        piece = grad_cols[..., position * width : (position + 1) * width]
        placed = jnp.pad(piece, ((0, 0), (row_off, 2 - row_off), (col_off, 2 - col_off), (0, 0)))
        total = placed if total is None else total + placed
    return total[:, 1 : 1 + extent, 1 : 1 + extent, :]


def lateral_cols(fast, has_prev):
    frames = fast.shape[0] // 4
    grouped = fast.reshape((frames, 4) + fast.shape[1:])
    return jnp.concatenate(
        [
            masked(shift_down(grouped[:, 2]), has_prev),
            masked(shift_down(grouped[:, 3]), has_prev),
            grouped[:, 0],
            grouped[:, 1],
            grouped[:, 2],
        ],
        axis=-1,
    )


def lateral_back(grad_cols, has_prev):
    width = grad_cols.shape[-1] // 5
    parts = [grad_cols[..., tap * width : (tap + 1) * width] for tap in range(5)]
    from_two = shift_up(masked(parts[0], has_prev))
    from_three = shift_up(masked(parts[1], has_prev))
    grouped = jnp.stack([parts[2], parts[3], parts[4] + from_two, from_three], axis=1)
    return grouped.reshape((grouped.shape[0] * 4,) + grouped.shape[2:])


def widen(row):
    short = -row.shape[-1] % 128
    return jnp.pad(row, ((0, 0), (0, short)))


def gather_stats(fields, call):
    devices = lax.axis_size("fsdp")
    widths = [field.shape[-1] for field in fields]
    rows = []
    for field in fields:
        own = jnp.mean(field, axis=(0, 1, 2))
        rows.append(widen(jnp.stack([own, jnp.mean(jnp.square(field - own), axis=(0, 1, 2))])))
    merged = exchange(jnp.concatenate(rows, axis=1), devices, 8, call, 1.0, True) / jnp.array([[1.0], [devices]])
    result, offset = [], 0
    for width, row in zip(widths, rows):
        part = merged[:, offset : offset + width]
        result.append((part[0], lax.rsqrt(part[1] + EPSILON)))
        offset += row.shape[1]
    return result


def reduce_norms(pairs, call):
    devices = lax.axis_size("fsdp")
    rows = [
        widen(jnp.stack([jnp.sum(grad_out, axis=(0, 1, 2)), jnp.sum(grad_out * normed, axis=(0, 1, 2))]))
        for grad_out, normed in pairs
    ]
    merged = exchange(jnp.concatenate(rows, axis=1), devices, 8, call)
    result, offset = [], 0
    for (grad_out, normed), row in zip(pairs, rows):
        width = grad_out.shape[-1]
        result.append((merged[0, offset : offset + width], merged[1, offset : offset + width]))
        offset += row.shape[1]
    return result


def normalize(field, stats):
    average, inverse = stats
    return (field - average) * inverse


def affine(normed, norm_pair):
    pair = norm_pair.astype(jnp.float32)
    return normed * pair[0] + pair[1]


def silu_slope(field):
    sigma = jax.nn.sigmoid(field)
    return sigma * (1.0 + field * (1.0 - sigma))


def norm_input_grad(grad_out, normed, norm_pair, inverse, totals, count):
    sum_grad, sum_cross = totals
    gain = norm_pair[0].astype(jnp.float32)
    return (gain * inverse * (grad_out - sum_grad / count - normed * (sum_cross / count))).astype(
        jnp.bfloat16
    )


def pair_grad(totals):
    return jnp.stack([totals[1], totals[0]])


def own_columns(full_grad):
    share = full_grad.shape[1] // lax.axis_size("fsdp")
    return lax.dynamic_slice_in_dim(full_grad, lax.axis_index("fsdp") * share, share, 1)


def shards(
    slow_in,
    fast_in,
    clip_ids,
    lateral_weight,
    first_weight,
    middle_weight,
    last_weight,
    proj_weight,
    lat_norm,
    one_norm,
    two_norm,
    out_norm,
    proj_norm,
    fast_first,
    fast_middle,
    fast_last,
    fast_proj,
    fast_mid_norm,
    fast_out_norm,
    slow_cot,
    fast_cot,
):
    devices = lax.axis_size("fsdp")
    norms = jnp.concatenate([lat_norm, one_norm, two_norm, out_norm, proj_norm], axis=1).astype(jnp.float32)
    norms = jnp.pad(norms, ((0, 6), (0, 128 - norms.shape[1])))
    lateral_full, first_full, middle_full, last_full, proj_full, norms_full = gather_all(
        [lateral_weight.T, first_weight, middle_weight, last_weight, proj_weight, norms], (0, 1, 1, 0, 0, 0), devices, 1
    )
    lateral_full = lateral_full.reshape(-1, lateral_weight.shape[0]).T
    first_full = first_full.reshape(-1, first_weight.shape[1])
    middle_full = middle_full.reshape(-1, middle_weight.shape[1])
    last_full = last_full.reshape(-1, last_weight.shape[1])
    proj_full = proj_full.reshape(-1, proj_weight.shape[1])
    gains, offset = [], 0
    for pair in (lat_norm, one_norm, two_norm, out_norm, proj_norm):
        width = pair.shape[1]
        gains.append(norms_full[:, :2, offset : offset + width].transpose(1, 0, 2).reshape(2, -1))
        offset += width
    gain_lat, gain_one, gain_two, gain_out, gain_proj = gains
    has_prev, has_next = clip_edges(clip_ids)
    fast_prev, fast_next = fast_edges(has_prev, has_next)
    slow_count = slow_in.shape[0] * slow_in.shape[1] * slow_in.shape[2] * devices
    fast_count = 4 * slow_count
    lat_cols = lateral_cols(fast_in, has_prev)
    lat_pre = product(lat_cols, lateral_full)
    fone_cols = temporal_cols(fast_in, fast_prev, fast_next)
    fone_pre = product(fone_cols, fast_first)
    fproj_pre = product(fast_in, fast_proj)
    lat_stats, fone_stats, fproj_stats = gather_stats([lat_pre, fone_pre, fproj_pre], 2)
    lat_hat = normalize(lat_pre, lat_stats)
    lat_act = affine(lat_hat, gain_lat)
    lateral = jax.nn.silu(lat_act).astype(jnp.bfloat16)
    fone_hat = normalize(fone_pre, fone_stats)
    fone_act = affine(fone_hat, fast_mid_norm[0])
    fone = jax.nn.silu(fone_act).astype(jnp.bfloat16)
    fproj_hat = normalize(fproj_pre, fproj_stats)
    joined = jnp.concatenate([slow_in, lateral], axis=-1)
    one_cols = temporal_cols(joined, has_prev, has_next)
    one_pre = product(one_cols, first_full)
    proj_pre = product(joined, proj_full)
    ftwo_cols = spatial_cols(fone)
    ftwo_pre = product(ftwo_cols, fast_middle)
    one_stats, proj_stats, ftwo_stats = gather_stats([one_pre, proj_pre, ftwo_pre], 3)
    one_hat = normalize(one_pre, one_stats)
    one_act = affine(one_hat, gain_one)
    one = jax.nn.silu(one_act).astype(jnp.bfloat16)
    proj_hat = normalize(proj_pre, proj_stats)
    ftwo_hat = normalize(ftwo_pre, ftwo_stats)
    ftwo_act = affine(ftwo_hat, fast_mid_norm[1])
    ftwo = jax.nn.silu(ftwo_act).astype(jnp.bfloat16)
    two_cols = spatial_cols(one)
    two_pre = product(two_cols, middle_full)
    fthree_pre = product(ftwo, fast_last)
    two_stats, fthree_stats = gather_stats([two_pre, fthree_pre], 4)
    two_hat = normalize(two_pre, two_stats)
    two_act = affine(two_hat, gain_two)
    two = jax.nn.silu(two_act).astype(jnp.bfloat16)
    fthree_hat = normalize(fthree_pre, fthree_stats)
    three_pre = product(two, last_full)
    three_stats = gather_stats([three_pre], 5)[0]
    three_hat = normalize(three_pre, three_stats)
    slow_sum = affine(three_hat, gain_out) + affine(proj_hat, gain_proj)
    slow_out = jax.nn.silu(slow_sum).astype(jnp.bfloat16)
    fast_sum = affine(fthree_hat, fast_out_norm[0]) + affine(fproj_hat, fast_out_norm[1])
    fast_out = jax.nn.silu(fast_sum).astype(jnp.bfloat16)
    slow_delta = slow_cot.astype(jnp.float32) * silu_slope(slow_sum)
    fast_delta = fast_cot.astype(jnp.float32) * silu_slope(fast_sum)
    outer = reduce_norms(
        [
            (slow_delta, three_hat),
            (slow_delta, proj_hat),
            (fast_delta, fthree_hat),
            (fast_delta, fproj_hat),
        ],
        6,
    )
    three_d = norm_input_grad(slow_delta, three_hat, gain_out, three_stats[1], outer[0], slow_count)
    proj_d = norm_input_grad(slow_delta, proj_hat, gain_proj, proj_stats[1], outer[1], slow_count)
    fthree_d = norm_input_grad(
        fast_delta, fthree_hat, fast_out_norm[0], fthree_stats[1], outer[2], fast_count
    )
    fproj_d = norm_input_grad(
        fast_delta, fproj_hat, fast_out_norm[1], fproj_stats[1], outer[3], fast_count
    )
    last_term = weight_term(two, three_d)
    proj_term = weight_term(joined, proj_d)
    fthree_term = weight_term(ftwo, fthree_d)
    fproj_term = weight_term(fast_in, fproj_d)
    two_delta = back_product(three_d, last_full) * silu_slope(two_act)
    ftwo_delta = back_product(fthree_d, fast_last) * silu_slope(ftwo_act)
    middle_sums = reduce_norms([(two_delta, two_hat), (ftwo_delta, ftwo_hat)], 7)
    two_d = norm_input_grad(two_delta, two_hat, gain_two, two_stats[1], middle_sums[0], slow_count)
    ftwo_d = norm_input_grad(
        ftwo_delta, ftwo_hat, fast_mid_norm[1], ftwo_stats[1], middle_sums[1], fast_count
    )
    middle_term = weight_term(two_cols, two_d)
    fmiddle_term = weight_term(ftwo_cols, ftwo_d)
    one_delta = spatial_back(back_product(two_d, middle_full)) * silu_slope(one_act)
    fone_delta = spatial_back(back_product(ftwo_d, fast_middle)) * silu_slope(fone_act)
    inner_sums = reduce_norms([(one_delta, one_hat), (fone_delta, fone_hat)], 8)
    one_d = norm_input_grad(one_delta, one_hat, gain_one, one_stats[1], inner_sums[0], slow_count)
    fone_d = norm_input_grad(
        fone_delta, fone_hat, fast_mid_norm[0], fone_stats[1], inner_sums[1], fast_count
    )
    first_term = weight_term(one_cols, one_d)
    ffirst_term = weight_term(fone_cols, fone_d)
    joined_grad = temporal_back(back_product(one_d, first_full), has_prev, has_next) + back_product(
        proj_d, proj_full
    )
    width_in = slow_in.shape[-1]
    slow_in_grad = joined_grad[..., :width_in].astype(jnp.bfloat16)
    lat_delta = joined_grad[..., width_in:] * silu_slope(lat_act)
    lat_sums = reduce_norms([(lat_delta, lat_hat)], 9)
    lat_d = norm_input_grad(lat_delta, lat_hat, gain_lat, lat_stats[1], lat_sums[0], slow_count)
    lateral_term = weight_term(lat_cols, lat_d)
    fast_in_grad = (
        lateral_back(back_product(lat_d, lateral_full), has_prev)
        + temporal_back(back_product(fone_d, fast_first), fast_prev, fast_next)
        + back_product(fproj_d, fast_proj)
    ).astype(jnp.bfloat16)
    shares = scatter_all(
        [
            lateral_term.T.astype(jnp.bfloat16).reshape(devices, -1, lateral_weight.shape[0]),
            first_term.astype(jnp.bfloat16).reshape(devices, -1, first_weight.shape[1]),
            middle_term.astype(jnp.bfloat16).reshape(devices, -1, middle_weight.shape[1]),
            last_term.astype(jnp.bfloat16).reshape(devices, -1, last_weight.shape[1]),
            proj_term.astype(jnp.bfloat16).reshape(devices, -1, proj_weight.shape[1]),
        ],
        (0, 1, 1, 0, 0),
        devices,
        10,
    )
    lateral_grad, first_grad, middle_grad, last_grad, proj_grad = shares
    lateral_grad = lateral_grad.T
    terms = (ffirst_term, fmiddle_term, fthree_term, fproj_term)
    fast_total = exchange(jnp.concatenate([term.reshape(-1, 128) for term in terms]), devices, 8, 11)
    fast_shares, offset = [], 0
    for term in terms:
        rows = term.size // 128
        fast_shares.append(fast_total[offset : offset + rows].reshape(term.shape))
        offset += rows
    lat_norm_grad = own_columns(pair_grad(lat_sums[0]))
    one_norm_grad = own_columns(pair_grad(inner_sums[0]))
    two_norm_grad = own_columns(pair_grad(middle_sums[0]))
    out_norm_grad = own_columns(pair_grad(outer[0]))
    proj_norm_grad = own_columns(pair_grad(outer[1]))
    fast_mid_norm_grad = jnp.stack([pair_grad(inner_sums[1]), pair_grad(middle_sums[1])])
    fast_out_norm_grad = jnp.stack([pair_grad(outer[2]), pair_grad(outer[3])])
    return (
        slow_out,
        fast_out,
        slow_in_grad,
        fast_in_grad,
        lateral_grad,
        first_grad,
        middle_grad,
        last_grad,
        proj_grad,
        lat_norm_grad,
        one_norm_grad,
        two_norm_grad,
        out_norm_grad,
        proj_norm_grad,
        fast_shares[0],
        fast_shares[1],
        fast_shares[2],
        fast_shares[3],
        fast_mid_norm_grad,
        fast_out_norm_grad,
    )


def solution(mesh):
    in_specs = (
        P("fsdp", None, None, None),
        P("fsdp", None, None, None),
        P("fsdp", None),
        P(None, "fsdp"),
        P("fsdp", None),
        P("fsdp", None),
        P("fsdp", None),
        P("fsdp", None),
        P(None, "fsdp"),
        P(None, "fsdp"),
        P(None, "fsdp"),
        P(None, "fsdp"),
        P(None, "fsdp"),
        P(),
        P(),
        P(),
        P(),
        P(),
        P(),
        P("fsdp", None, None, None),
        P("fsdp", None, None, None),
    )
    out_specs = (
        P("fsdp", None, None, None),
        P("fsdp", None, None, None),
        P("fsdp", None, None, None),
        P("fsdp", None, None, None),
        P(None, "fsdp"),
        P("fsdp", None),
        P("fsdp", None),
        P("fsdp", None),
        P("fsdp", None),
        P(None, "fsdp"),
        P(None, "fsdp"),
        P(None, "fsdp"),
        P(None, "fsdp"),
        P(None, "fsdp"),
        P(),
        P(),
        P(),
        P(),
        P(),
        P(),
    )
    return jax.shard_map(shards, mesh=mesh, in_specs=in_specs, out_specs=out_specs, check_vma=False)
```

```python
import functools

import jax
import jax.numpy as jnp
import numpy as np
from jax import lax
from jax.experimental import pallas as pl
from jax.experimental.pallas import tpu as pltpu
from jax.sharding import PartitionSpec as P

EPSILON = 1e-05


MESH = pl.DeviceIdType.MESH


f32 = jnp.float32
bf16 = jnp.bfloat16
STEPS = 7
STRIP = 32


def dot(a, b):
    return lax.dot_general(a, b, (((1,), (0,)), ((), ())), preferred_element_type=f32)


def dot_nt(a, b):
    return lax.dot_general(a, b, (((1,), (1,)), ((), ())), preferred_element_type=f32)


def dot_tn(a, b):
    return lax.dot_general(a, b, (((0,), (0,)), ((), ())), preferred_element_type=f32)


def shift(v, mask, by):
    rows = v.shape[0]
    moved = pltpu.roll(v, by % rows, 0)
    return masked(moved, mask)


def masked(v, mask):
    return (v.reshape(-1, mask.shape[0], v.shape[1]) * mask[None, :, : v.shape[1]]).reshape(v.shape)


def sigma(x):
    return 0.5 + 0.5 * jnp.tanh(0.5 * x)


def silu(x):
    return x * sigma(x)


def slope(x):
    s = sigma(x)
    return s * (1.0 + x * (1.0 - s))


def normed(z, n):
    return (z - n[0:1]) * n[1:2]


def scaled(hat, n):
    return hat * n[2:3] + n[3:4]


def acted(z, n):
    return scaled(normed(z, n), n)


def input_grad(e, hat, n, s_mean, s_cross):
    return ((n[2:3] * n[1:2]) * (e - s_mean - hat * s_cross)).astype(bf16)


def eighth(v):
    return jnp.sum(v.reshape(-1, 8, v.shape[1]), axis=0)


def clear_first(step, *refs):
    @pl.when(step == 0)
    def _():
        for ref in refs:
            ref[...] = jnp.zeros(ref.shape, ref.dtype)


def add_moments(step, acc, lo, z):
    hi = lo + z.shape[1]
    high = z.shape[0] // 8
    deep = z.reshape(high, 8, hi - lo)
    own = jnp.sum(deep, axis=0) * (1.0 / high)
    off = deep - own[None]
    spread_of = jnp.sum(off * off, axis=0)
    past = step.astype(f32)
    share = 1.0 / (past + 1.0)
    gap = own - acc[0, :, lo:hi]
    acc[0, :, lo:hi] += gap * share
    acc[1, :, lo:hi] += spread_of + gap * gap * (past * share * high)


def add_sums(step, acc, lo, parts):
    hi = lo + parts[0].shape[1]
    for k, part in enumerate(parts):
        acc[k, :, lo:hi] += part


def split_fours(raw, wide):
    rows = wide.shape[0]
    wide[...] = raw[...].astype(f32).reshape(rows, 128)
    return jnp.concatenate([wide[pl.ds(k, rows // 4, stride=4), :] for k in range(4)], axis=1)


def join_fours(value, wide, raw):
    rows = wide.shape[0]
    for k in range(4):
        wide[pl.ds(k, rows // 4, stride=4), :] = value[:, 128 * k : 128 * (k + 1)]
    raw[...] = wide[...].astype(bf16).reshape(raw.shape)


def clear(grid):
    grid[...] = jnp.zeros(grid.shape, grid.dtype)


def fill(grid, side, value, block):
    per = side // STEPS
    line = value.shape[0] // per
    frames = line // side
    for r in range(per):
        at = ((block * per + r + 1) * (side + 2) + 1) * frames
        grid[pl.ds(pl.multiple_of(at, 16), line), :] = value[r * line : (r + 1) * line]


def tap_columns(grid, side, step, rows, flip):
    per = side // STEPS
    line = rows // per
    frames = line // side
    lines = []
    for r in range(per):
        pieces = []
        for a in range(3):
            for b in range(3):
                ra, rb = (2 - a, 2 - b) if flip else (a, b)
                at = ((step * per + r + ra) * (side + 2) + rb) * frames
                pieces.append(grid[pl.ds(pl.multiple_of(at, 16), line), :])
        lines.append(jnp.concatenate(pieces, axis=1))
    return jnp.concatenate(lines, axis=0)


INNER = 8


def greet(n):
    me = lax.axis_index("fsdp")
    mi, mo, depth = lax.rem(me, INNER), lax.div(me, INNER), n // INNER
    barrier = pltpu.get_barrier_semaphore()
    for k in range(1, INNER):
        pl.semaphore_signal(barrier, inc=1, device_id=(mo * INNER + lax.rem(mi + k, INNER),), device_id_type=MESH)
    for k in range(1, depth):
        pl.semaphore_signal(barrier, inc=1, device_id=(lax.rem(mo + k, depth) * INNER + mi,), device_id_type=MESH)


def greeted(n):
    pl.semaphore_wait(pltpu.get_barrier_semaphore(), INNER - 1 + n // INNER - 1)


def total_of(n, centred, own, near, far, mid, near_send, near_recv, far_send, far_recv):
    me = lax.axis_index("fsdp")
    mi, mo, depth = lax.rem(me, INNER), lax.div(me, INNER), n // INNER

    def swap(src, slots, sends, recvs, mine, size, peer):
        copies = []
        for k in range(1, size):
            copy = pltpu.make_async_remote_copy(
                src_ref=src, dst_ref=slots.at[mine], send_sem=sends.at[k], recv_sem=recvs.at[k],
                device_id=(peer(k),), device_id_type=MESH)
            copy.start()
            copies.append(copy)
        slots[mine] = src[...]
        for copy in copies:
            copy.wait()

    def merge(slots, size):
        if not centred:
            return sum(slots[k] for k in range(1, size)) + slots[0]
        mean = sum(slots[k, 0:1] for k in range(size)) * (1.0 / size)
        off = [slots[k, 0:1] - mean for k in range(size)]
        return jnp.concatenate([mean, sum(slots[k, 1:2] + off[k] * off[k] for k in range(size)) * (1.0 / size)], axis=0)

    swap(own, near, near_send, near_recv, mi, INNER, lambda k: mo * INNER + lax.rem(mi + k, INNER))
    mid[...] = merge(near, INNER)
    if depth == 1:
        return mid[...]
    swap(mid, far, far_send, far_recv, mo, depth, lambda k: lax.rem(mo + k, depth) * INNER + mi)
    return merge(far, depth)


def over_groups(part, width):
    lanes = part.shape[1]
    if width < 128:
        wide = jnp.broadcast_to(part, (8, lanes))
        total = wide
        for k in range(1, lanes // width):
            total = total + pltpu.roll(wide, k * width, 1)
        return total[0:1]
    total = sum(part[:, k : k + width] for k in range(0, lanes, width))
    return jnp.concatenate([total] * (lanes // width), axis=1)


def norm_pack(total, pairs, out, folds):
    out[0:2] = total
    for lo, hi, width in folds:
        groups = width / (hi - lo)
        mean = over_groups(total[0:1, lo:hi], width) * groups
        off = total[0:1, lo:hi] - mean
        out[0:1, lo:hi] = mean
        out[1:2, lo:hi] = over_groups(total[1:2, lo:hi] + off * off, width) * groups
    out[1:2] = lax.rsqrt(out[1:2] + EPSILON)
    at = 0
    for pair, lo, hi in pairs:
        out[2:4, at : at + hi - lo] = pair[:, lo:hi]
        at += hi - lo


def sum_pack(total, out, folds):
    out[...] = total
    for lo, hi, width in folds:
        for k in range(out.shape[0]):
            out[k : k + 1, lo:hi] = over_groups(total[k : k + 1, lo:hi], width)


def swap_scratch(shape, n):
    DS, depth = pltpu.SemaphoreType.DMA, n // INNER
    return [pltpu.VMEM((INNER,) + shape, f32), pltpu.VMEM((depth,) + shape, f32), pltpu.VMEM(shape, f32),
        DS((INNER,)), DS((INNER,)), DS((depth,)), DS((depth,))]


def run(body, rows, ins, outs, scratch, n=1, swap=None, call=None, same=None):
    def spec(shape, how):
        if how == "any":
            return pl.BlockSpec(memory_space=pl.ANY)
        if how == "rows":
            return pl.BlockSpec((shape[0] // STEPS,) + tuple(shape[1:]), lambda i, d=len(shape): (i,) + (0,) * (d - 1))
        return pl.BlockSpec(tuple(shape), lambda i, d=len(shape): (0,) * d, pipeline_mode=pl.Buffered(1))
    def out_spec(shape, how):
        if how in ("rows", "any"):
            return spec(shape, how)
        return pl.BlockSpec(tuple(shape), lambda i, d=len(shape): (0,) * d)
    extra = {}
    if swap is not None:
        scratch = scratch + [pltpu.VMEM(swap, f32)]
    if n > 1 and swap is not None:
        scratch = scratch + swap_scratch(swap, n)
    if n > 1 and call is not None:
        extra = dict(collective_id=call, has_side_effects=True)
    return pl.pallas_call(
        body,
        grid=(STEPS,),
        in_specs=[spec(a.shape, how) for a, how in ins],
        out_specs=[out_spec(shape, how) for shape, _, how in outs],
        out_shape=[jax.ShapeDtypeStruct(shape, kind) for shape, kind, _ in outs],
        scratch_shapes=scratch,
        input_output_aliases=same or {},
        compiler_params=pltpu.CompilerParams(dimension_semantics=("arbitrary",), vmem_limit_bytes=58 * 1024 * 1024, **extra),
    )(*[a for a, _ in ins])


def close_moments(step, acc, pairs, out, count, folds, n, ticks, own, *links):
    @pl.when(step == STEPS - 1)
    def _():
        mean = jnp.mean(acc[0], axis=0, keepdims=True)
        off = acc[0] - mean
        own[0:1] = mean
        own[1:2] = jnp.sum(acc[1], axis=0, keepdims=True) * (1.0 / count) + jnp.mean(off * off, axis=0, keepdims=True)
        if n > 1:
            ticks[3]()
            norm_pack(total_of(n, True, own, *links), pairs, out, folds)
            ticks[4]()
        else:
            norm_pack(own[...], pairs, out, folds)


def close_sums(step, acc, out, folds, n, ticks, own, *links):
    if n > 1 and not ticks:
        @pl.when(step == 0)
        def _():
            greet(n)

    @pl.when(step == STEPS - 1)
    def _():
        for k in range(acc.shape[0]):
            own[k : k + 1] = jnp.sum(acc[k], axis=0, keepdims=True)
        if n > 1:
            if ticks:
                ticks[3]()
            else:
                greeted(n)
            sum_pack(total_of(n, False, own, *links), out, folds)
            if ticks:
                ticks[4]()
        else:
            sum_pack(own[...], out, folds)


def places():
    me = lax.axis_index("fsdp")
    return lax.div(me, 8), lax.rem(lax.div(me, 4), 2), lax.rem(lax.div(me, 2), 2), lax.rem(me, 2)


def flat(z, y, x, c):
    return ((z * 2 + y) * 2 + x) * 2 + c


def six(term, n):
    return term.reshape((n // 8, 2, 2, 2, term.shape[0] // n) + term.shape[1:])


def halves(width):
    if width < 256:
        return ((0, width),)
    middle = width // 256 * 128
    return ((0, middle), (middle, width))


def scatter_scratch(parts, n):
    depth, k, DS = n // 8, len(parts), pltpu.SemaphoreType.DMA
    def buf(lead):
        return [pltpu.VMEM(lead + part, bf16) for part in parts]
    return (buf((depth, 2, 2)) + buf((depth, 2, 2)) + buf((depth, 2)) + buf((depth,)) + buf((depth,))
        + [DS((k,)), DS((k, 2)), DS((k, 2, 2)), DS((k, 2, 2)), DS((k, depth)), DS((k, depth))])


def scatter_ticks(n, ins, outs, rest):
    k, depth = len(ins), n // 8
    half, r1, r2, r3, r4 = (rest[j * k : (j + 1) * k] for j in range(5))
    own_sem, c_sem, p_sem, q_sem, z_send, z_recv = rest[5 * k :]
    z, y, x, c = places()
    core, over_x, over_y = flat(z, y, x, 1 - c), flat(z, y, 1 - x, c), flat(z, 1 - y, x, c)
    line = [flat(lax.rem(z + s, depth), y, x, c) for s in range(depth)]
    spots = [lax.rem(z + s, depth) for s in range(depth)]

    def remote(src, dst, send, recv, peer):
        return pltpu.make_async_remote_copy(
            src_ref=src, dst_ref=dst, send_sem=send, recv_sem=recv, device_id=(peer,), device_id_type=MESH)
    def sides(i):
        return tuple(enumerate(halves(half[i].shape[-1])))
    def own(i):
        return pltpu.make_async_copy(ins[i].at[:, :, :, c], half[i], own_sem.at[i])
    def to_core(i):
        return remote(ins[i].at[:, :, :, 1 - c], r1[i], c_sem.at[i, 0], c_sem.at[i, 1], core)
    def to_first(i, t, lo, hi):
        src, peer = (half[i].at[:, :, 1 - x, :, lo:hi], over_x) if t == 0 else (half[i].at[:, 1 - y, :, :, lo:hi], over_y)
        return remote(src, r2[i].at[:, :, :, lo:hi], p_sem.at[i, t, 0], p_sem.at[i, t, 1], peer)
    def to_second(i, t, lo, hi):
        src, peer = (half[i].at[:, 1 - y, x, :, lo:hi], over_y) if t == 0 else (half[i].at[:, y, 1 - x, :, lo:hi], over_x)
        return remote(src, r3[i].at[:, :, lo:hi], q_sem.at[i, t, 0], q_sem.at[i, t, 1], peer)
    def to_line(i, s):
        return remote(half[i].at[spots[s], y, x], r4[i].at[s], z_send.at[i, s], z_recv.at[i, s], line[s])
    def add(target, other):
        target[...] = (target[...].astype(f32) + other[...].astype(f32)).astype(target.dtype)

    def begin():
        for i in range(k):
            own(i).start()
            to_core(i).start()
    def first():
        for i in range(k):
            own(i).wait()
            to_core(i).wait()
            @pl.loop(0, depth)
            def _(zz, i=i):
                for a in range(2):
                    for b in range(2):
                        add(half[i].at[zz, a, b], r1[i].at[zz, a, b])
            for t, (lo, hi) in sides(i):
                to_first(i, t, lo, hi).start()
    def second():
        for i in range(k):
            for t, (lo, hi) in sides(i):
                to_first(i, t, lo, hi).wait()
                @pl.loop(0, depth)
                def _(zz, i=i, t=t, lo=lo, hi=hi):
                    for o in range(2):
                        target = half[i].at[zz, o, x] if t == 0 else half[i].at[zz, y, o]
                        add(target.at[:, lo:hi], r2[i].at[zz, o, :, lo:hi])
                to_second(i, t, lo, hi).start()
    def third():
        for i in range(k):
            for t, (lo, hi) in sides(i):
                to_second(i, t, lo, hi).wait()
            @pl.loop(0, depth)
            def _(zz, i=i):
                add(half[i].at[zz, y, x], r3[i].at[zz])
            for s in range(1, depth):
                to_line(i, s).start()
    def finish():
        for i in range(k):
            outs[i][...] = half[i][z, y, x].astype(f32)
            for s in range(1, depth):
                to_line(i, s).wait()
                outs[i][...] += r4[i][s].astype(f32)
    return begin, first, second, third, finish


GATHER_SEMS = 9


def gather_scratch(k, n):
    DS, depth = pltpu.SemaphoreType.DMA, n // 8
    return [DS((1,)), DS((depth,)), DS((depth,)), DS((2, 2)), DS((2, 2)), DS((2, 3)), DS((2, 3)), DS((8,)), DS((8,))] * k


class Moves:
    def __init__(self, n, shard, whole, sems):
        self.n, self.shard, self.whole, self.sems = n, shard, whole, sems
        self.at = places()
        self.sides = tuple(enumerate(halves(whole.shape[-1])))

    def remote(self, src, dst, send, recv, *peer):
        return pltpu.make_async_remote_copy(
            src_ref=src, dst_ref=dst, send_sem=send, recv_sem=recv, device_id=(flat(*peer),), device_id_type=MESH)

    def part(self, name, t, lo, hi):
        z, y, x, c = self.at
        index = {
            "p": (slice(None), y, x, c),
            "q": (slice(None), y, slice(None), c) if t == 0 else (slice(None), slice(None), x, c),
            "c1": (slice(None), y, 1 - x, c) if t == 0 else (slice(None), 1 - y, x, c),
            "c2": (slice(None), 1 - y, slice(None), c) if t == 0 else (slice(None), slice(None), 1 - x, c),
        }["p" if name == "c0" else name]
        return self.whole.at[index + (slice(None), slice(lo, hi))]

    def copies(self, name):
        z, y, x, c = self.at
        own, z_send, z_recv, p, q, c_send, c_recv, d_send, d_recv = self.sems
        depth = self.n // 8
        if name == "z":
            mine = self.whole.at[z, y, x, c]
            return [pltpu.make_async_copy(self.shard, mine, own.at[0])] + [
                self.remote(self.shard, mine, z_send.at[s], z_recv.at[s], lax.rem(z + s, depth), y, x, c) for s in range(1, depth)]
        if name == "d":
            mine = self.whole.at[:, y, x, c]
            found = []
            for k in range(1, 8):
                other = lax.rem((y * 2 + x) * 2 + c + k, 8)
                found.append(self.remote(mine, mine, d_send.at[k], d_recv.at[k], z, 0, 0, other))
            return found
        found = []
        for t, (lo, hi) in self.sides:
            src = self.part(name, t, lo, hi)
            if name[0] == "c":
                j = int(name[1])
                found.append(self.remote(src, src, c_send.at[t, j], c_recv.at[t, j], z, y, x, 1 - c))
                continue
            sem = p if name == "p" else q
            peer = (z, y, 1 - x, c) if (t == 0) == (name == "p") else (z, 1 - y, x, c)
            found.append(self.remote(src, src, sem.at[t, 0], sem.at[t, 1], *peer))
        return found

    def start(self, *names):
        for name in names:
            for copy in self.copies(name):
                copy.start()

    def wait(self, *names):
        for name in names:
            for copy in self.copies(name):
                copy.wait()


def moves(n, shards, wholes, rest):
    return [Moves(n, shard, whole, rest[GATHER_SEMS * i : GATHER_SEMS * (i + 1)]) for i, (shard, whole) in enumerate(zip(shards, wholes))]


def spread_shapes(shards, n):
    return [((n // 8, 2, 2, 2) + v.shape, v.dtype, "any") for v in shards]


def whole_shapes(wholes):
    return [(v.shape, v.dtype, "any") for v in wholes]


def gathered(v, n):
    return v.reshape((n * v.shape[4],) + v.shape[5:])


def body0(n, *refs):
    lat, norms, first = moves(n, refs[:3], refs[3:6], refs[6:])
    greet(n)
    greeted(n)
    for m in (lat, norms, first):
        m.start("z")
    for m in (lat, norms):
        m.wait("z")
        m.start("d")
    first.wait("z")
    first.start("p", "c0")
    lat.wait("d")
    norms.wait("d")
    first.wait("p", "c0")


def stage0(shards, n):
    return pl.pallas_call(
        functools.partial(body0, n),
        in_specs=[pl.BlockSpec(memory_space=pl.ANY)] * len(shards),
        out_specs=[pl.BlockSpec(memory_space=pl.ANY)] * len(shards),
        out_shape=[jax.ShapeDtypeStruct(shape, kind) for shape, kind, _ in spread_shapes(shards, n)],
        scratch_shapes=gather_scratch(len(shards), n),
        compiler_params=pltpu.CompilerParams(collective_id=1, has_side_effects=True),
    )(*shards)


def run_ticks(step, n, ticks, at):
    @pl.when(step == 0)
    def _():
        greet(n)
    for j in range(3):
        @pl.when(step == at[j])
        def _(j=j):
            if j == 0:
                greeted(n)
            ticks[j]()


def strips(rows, width, body, init):
    return lax.fori_loop(0, rows // STRIP, lambda k, carry: body(pl.ds(pl.multiple_of(k * STRIP, STRIP), STRIP), carry), init, unroll=True)


FOLDS1 = ((256, 384, 32), (384, 896, 128))
FOLDS2 = ((256, 384, 32),)
FOLDS3 = ((256, 768, 128),)


def body1(n, raw, lat, band, fproj, mask, spair, fpair, held, *refs):
    shards, (fast4, lat_pre, fone_pre, n1), wholes, (wide, acc), rest = refs[:2], refs[2:6], refs[6:9], refs[9:11], refs[11:]
    step = pl.program_id(0)
    clear_first(step, acc)
    ticks, swap = (), rest
    if n > 1:
        first, *others = moves(n, (None,) + tuple(shards), wholes, rest)
        swap = rest[3 * GATHER_SEMS :]

        def begin():
            first.start("q", "c1")
            for m in others:
                m.start("z")
        def middle():
            first.wait("q")
            first.start("c2")
        def finish():
            first.wait("c1", "c2")
            for m in others:
                m.wait("z")
        ticks = (begin, middle, lambda: None, lambda: None, finish)
        run_ticks(step, n, ticks, (1, 4, 6))
    f = split_fours(raw, wide).astype(bf16)
    fast4[...] = f
    prev, nxt = mask[0], mask[1]
    z = dot_nt(f[:, :384], lat[:, 256:]) + shift(dot_nt(f[:, 256:], lat[:, :256]), prev, 1)
    lat_pre[...] = z
    add_moments(step, acc, 0, z)
    y = dot(f, band[...])
    z = y[:, :128] + shift(y[:, 128:256], prev, 1) + shift(y[:, 256:], nxt, -1)
    fone_pre[...] = z
    add_moments(step, acc, 256, z)
    z = jnp.concatenate([dot(f[:, :256], fproj[...]), dot(f[:, 256:], fproj[...])], axis=1)
    add_moments(step, acc, 384, z)
    close_moments(step, acc, ((spair, 0, 256), (fpair, 0, 128), (fpair, 768, 1280)), n1, f.shape[0] * STEPS, FOLDS1, n, ticks, *swap)


def stage1(raw, lat, band, fproj, mask, spair, fpair, held, shards_of, n):
    rows = raw.shape[0] * raw.shape[1] // 4
    return run(functools.partial(body1, n), rows,
        [(raw, "rows")] + [(v, "all") for v in (lat, band, fproj, mask, spair, fpair)] + [(v, "any") for v in (held,) + tuple(shards_of)],
        [((rows, 512), bf16, "rows"), ((rows, 256), f32, "rows"), ((rows, 128), f32, "rows"), ((4, 896), f32, "all")] + whole_shapes([held]) + spread_shapes(shards_of, n),
        [pltpu.VMEM((rows * 4 // STEPS, 128), f32), pltpu.VMEM((2, 8, 896), f32)] + (gather_scratch(3, n) if n > 1 else []), n, (2, 896), 2, {7: 4})


def body2(n, side, slow, lat_pre, fone_pre, n1, first, fmid, mask, spair, fpair, held_a, held_b, shard,
          lateral, one_pre, ftwo_pre, n2, whole_a, whole_b, whole_c, grid, acc, *rest):
    step = pl.program_id(0)
    rows = slow.shape[0]
    n_lat, n_fone = n1[:, :256], n1[:, 256:384]
    ticks, swap = (), rest
    if n > 1:
        middle, last, proj = moves(n, (None, None, shard), (whole_a, whole_b, whole_c), rest)
        swap = rest[3 * GATHER_SEMS :]

        def begin():
            middle.start("p", "c0")
            last.start("p", "c0")
            proj.start("z")
        def half():
            middle.wait("p")
            middle.start("q", "c1")
        def late():
            proj.wait("z")
            proj.start("p", "c0")
        def close():
            middle.wait("q")
            middle.start("c2")
        def finish():
            last.wait("p", "c0")
            proj.wait("p", "c0")
            middle.wait("c0", "c1", "c2")
        ticks = (begin, half, late, close, finish)
        run_ticks(step, n, ticks, (1, 3, 5))

    def put(block):
        part = fone_pre[pl.ds(pl.multiple_of(block * rows, 16), rows), :]
        fill(grid, side, silu(acted(part, n_fone)).astype(bf16), block)

    @pl.when(step == 0)
    def _():
        clear(grid)
        clear(acc)
        put(0)

    put(jnp.minimum(step + 1, STEPS - 1))
    lat = silu(acted(lat_pre[...], n_lat)).astype(bf16)
    lateral[...] = lat
    joined = jnp.concatenate([slow[...], lat], axis=1)
    z = dot(joined, first[1]) + shift(dot(joined, first[0]), mask[0], 1) + shift(dot(joined, first[2]), mask[1], -1)
    one_pre[...] = z
    add_moments(step, acc, 0, z)
    z = dot(tap_columns(grid, side, step, rows, False), fmid[...])
    ftwo_pre[...] = z
    add_moments(step, acc, 256, z)
    close_moments(step, acc, ((spair, 256, 512), (fpair, 128, 256)), n2, rows * STEPS, FOLDS2, n, ticks, *swap)


def stage2(slow, lat_pre, fone_pre, n1, first, fmid, mask, spair, fpair, held, shard, side, n):
    rows = slow.shape[0]
    frames = rows // side**2
    return run(functools.partial(body2, n, side), rows,
        [(slow, "rows"), (lat_pre, "rows")] + [(v, "all") for v in (fone_pre, n1, first, fmid, mask, spair, fpair)] + [(v, "any") for v in tuple(held) + (shard,)],
        [((rows, 256), bf16, "rows"), ((rows, 256), f32, "rows"), ((rows, 128), f32, "rows"), ((4, 384), f32, "all")] + whole_shapes(held) + spread_shapes([shard], n),
        [pltpu.VMEM(((side + 2) ** 2 * frames, 128), bf16), pltpu.VMEM((2, 8, 384), f32)] + (gather_scratch(3, n) if n > 1 else []), n, (2, 384), 3, {9: 4, 10: 5})


def body3(n, side, one_pre, ftwo_pre, n2, middle, flast, spair, fpair, held_a, held_b, two_pre, ftwo, n3, whole_a, whole_b, grid, acc, *rest):
    step = pl.program_id(0)
    rows = two_pre.shape[0]
    n_one, n_ftwo = n2[:, :256], n2[:, 256:]
    ticks, swap = (), rest
    if n > 1:
        both = moves(n, (None, None), (whole_a, whole_b), rest)
        swap = rest[2 * GATHER_SEMS :]

        def begin():
            for m in both:
                m.start("q", "c1")
        def half():
            for m in both:
                m.wait("q")
                m.start("c2")
        def finish():
            for m in both:
                m.wait("c1", "c2")
        ticks = (begin, half, lambda: None, lambda: None, finish)
        run_ticks(step, n, ticks, (1, 5, 6))

    def put(block):
        part = one_pre[pl.ds(pl.multiple_of(block * rows, 16), rows), :]
        fill(grid, side, silu(acted(part, n_one)).astype(bf16), block)

    @pl.when(step == 0)
    def _():
        clear(grid)
        clear(acc)
        put(0)

    put(jnp.minimum(step + 1, STEPS - 1))
    z = dot(tap_columns(grid, side, step, rows, False), middle[...])
    two_pre[...] = z
    add_moments(step, acc, 0, z)
    f = silu(acted(ftwo_pre[...], n_ftwo)).astype(bf16)
    ftwo[...] = f
    for k in range(2):
        add_moments(step, acc, 256 * (k + 1), dot(f, flast[:, 256 * k : 256 * (k + 1)]))
    close_moments(step, acc, ((spair, 512, 768), (fpair, 256, 768)), n3, rows * STEPS, FOLDS3, n, ticks, *swap)


def stage3(one_pre, ftwo_pre, n2, middle, flast, spair, fpair, held, side, n):
    rows = one_pre.shape[0]
    frames = rows // side**2
    return run(functools.partial(body3, n, side), rows,
        [(one_pre, "all"), (ftwo_pre, "rows")] + [(v, "all") for v in (n2, middle, flast, spair, fpair)] + [(v, "any") for v in held],
        [((rows, 256), f32, "rows"), ((rows, 128), bf16, "rows"), ((4, 768), f32, "all")] + whole_shapes(held),
        [pltpu.VMEM(((side + 2) ** 2 * frames, 256), bf16), pltpu.VMEM((2, 8, 768), f32)] + (gather_scratch(2, n) if n > 1 else []), n, (2, 768), 4, {7: 3, 8: 4})


def body4(n, two_pre, slow, lateral, n3, last, proj, spair, two, proj_pre, n4, acc, *swap):
    step = pl.program_id(0)
    clear_first(step, acc)
    v = silu(acted(two_pre[...], n3[:, :256])).astype(bf16)
    two[...] = v
    for k in range(4):
        add_moments(step, acc, 256 * k, dot(v, last[:, 256 * k : 256 * (k + 1)]))
    joined = jnp.concatenate([slow[...], lateral[...]], axis=1)
    for k in range(4):
        z = dot(joined, proj[:, 256 * k : 256 * (k + 1)])
        proj_pre[:, 256 * k : 256 * (k + 1)] = z.astype(proj_pre.dtype)
        add_moments(step, acc, 1024 + 256 * k, z)
    if n > 1:
        @pl.when(step == 0)
        def _():
            greet(n)
    close_moments(step, acc, ((spair, 768, 2816),), n4, v.shape[0] * STEPS, (), n,
        (None, None, None, lambda: greeted(n), lambda: None), *swap)


def stage4(two_pre, slow, lateral, n3, last, proj, spair, n):
    rows = two_pre.shape[0]
    return run(functools.partial(body4, n), rows,
        [(v, "rows") for v in (two_pre, slow, lateral)] + [(v, "all") for v in (n3, last, proj, spair)],
        [((rows, 256), bf16, "rows"), ((rows, 1024), f32, "rows"), ((4, 2048), f32, "all")], [pltpu.VMEM((2, 8, 2048), f32)], n, (2, 2048), 5)


def body5(two, proj_pre, cot, fast4, ftwo, fcot, n1, n3, n4, last, fproj, flast,
          slow_out, fast_out, delta, fdelta, sums, wide, three, fthree, fskip, fgrad, fout, acc):
    step = pl.program_id(0)
    rows = two.shape[0]
    clear_first(step, acc)
    fgrad[...] = split_fours(fcot, wide)
    three[...] = dot(two[...], last[...])
    fthree[...] = dot(ftwo[...], flast[...])
    for k in range(2):
        fskip[:, 256 * k : 256 * (k + 1)] = dot(fast4[:, 256 * k : 256 * (k + 1)], fproj[...])

    def side_of(za, zb, grad, na, nb, out, keep, lo, lanes):
        ga, gb, base = 0.5 * na[1:2] * na[2:3], 0.5 * nb[1:2] * nb[2:3], 0.5 * (na[3:4] + nb[3:4])
        ma, mb = na[0:1], nb[0:1]
        def one(at, carry):
            ha = za[at, lanes].astype(f32) - ma
            hb = zb[at, lanes].astype(f32) - mb
            h = ha * ga + hb * gb + base
            th = jnp.tanh(h)
            u = 1.0 + th
            out[at, lanes] = (h * u).astype(out.dtype)
            d = (0.5 * grad[at, lanes].astype(f32)) * (u * (1.0 + h * (1.0 - th)))
            keep[at, lanes] = d
            return carry[0] + eighth(d), carry[1] + eighth(d * ha), carry[2] + eighth(d * hb)
        zero = jnp.zeros((8, 256), f32)
        add_sums(step, acc, lo, strips(rows, 256, one, (zero, zero, zero)))

    for k in range(4):
        lanes = slice(256 * k, 256 * (k + 1))
        side_of(three, proj_pre, cot, n4[:, lanes], n4[:, 1024 + 256 * k : 1280 + 256 * k], slow_out, delta, 256 * k, lanes)
    for k in range(2):
        lanes = slice(256 * k, 256 * (k + 1))
        side_of(fthree, fskip, fgrad, n3[:, 256 + 256 * k : 512 + 256 * k], n1[:, 384 + 256 * k : 640 + 256 * k], fout, fdelta, 1024 + 256 * k, lanes)
    join_fours(fout[...], wide, fast_out)

    @pl.when(step == STEPS - 1)
    def _():
        scales = (1.0, jnp.concatenate([n4[1:2, :1024], n3[1:2, 256:]], axis=1), jnp.concatenate([n4[1:2, 1024:], n1[1:2, 384:]], axis=1))
        for k in range(3):
            sums[k : k + 1] = jnp.sum(acc[k], axis=0, keepdims=True) * scales[k]


def stage5(two, proj_pre, cot, fast4, ftwo, fcot, n1, n3, n4, last, fproj, flast):
    rows = two.shape[0]
    part = rows // STEPS
    return run(body5, rows,
        [(two, "rows"), (proj_pre, "rows"), (cot, "rows"), (fast4, "rows"), (ftwo, "rows"), (fcot, "rows"),
         (n1, "all"), (n3, "all"), (n4, "all"), (last, "all"), (fproj, "all"), (flast, "all")],
        [((rows, 1024), bf16, "rows"), (fcot.shape, bf16, "rows"), ((rows, 1024), f32, "rows"), ((rows, 512), f32, "rows"), ((3, 1536), f32, "all")],
        [pltpu.VMEM((part * 4, 128), f32), pltpu.VMEM((part, 1024), f32), pltpu.VMEM((part, 512), f32), pltpu.VMEM((part, 512), f32),
         pltpu.VMEM((part, 512), f32), pltpu.VMEM((part, 512), f32), pltpu.VMEM((3, 8, 1536), f32)])


def body5x(n, own, out, *links):
    greet(n)
    greeted(n)
    sum_pack(total_of(n, False, own, *links), out, ((1024, 1536, 128),))


def stage5x(sums, n):
    return pl.pallas_call(
        functools.partial(body5x, n),
        in_specs=[pl.BlockSpec(memory_space=pltpu.VMEM)],
        out_specs=pl.BlockSpec(memory_space=pltpu.VMEM),
        out_shape=jax.ShapeDtypeStruct(sums.shape, f32),
        scratch_shapes=swap_scratch(sums.shape, n),
        compiler_params=pltpu.CompilerParams(collective_id=6, has_side_effects=True),
    )(sums)


def body6(n, total, two, two_pre, proj_pre, slow, lateral, delta, fast4, ftwo, ftwo_pre, fdelta, n1, n2, n3, n4, s5, last, fproj, flast,
          d_proj, d_fproj, last_term, proj_term, flast_term, e_two, e_ftwo, sums,
          three, fthree, fskip, d_three, d_fthree, acc, last_acc, proj_acc, *swap):
    step = pl.program_id(0)
    rows = two.shape[0]
    clear_first(step, acc, last_acc, proj_acc, flast_term)
    three[...] = dot(two[...], last[...])
    fthree[...] = dot(ftwo[...], flast[...])
    for k in range(2):
        fskip[:, 256 * k : 256 * (k + 1)] = dot(fast4[:, 256 * k : 256 * (k + 1)], fproj[...])

    def side_of(za, zb, e, na, nb, s, da, db, lanes):
        pa, pb = na[2:3] * na[1:2], nb[2:3] * nb[1:2]
        qa, qb = pa * na[1:2] * s[1:2], pb * nb[1:2] * s[2:3]
        ma, mb, base = na[0:1], nb[0:1], s[0:1]
        def one(at, carry):
            d = e[at, lanes] - base
            da[at, lanes] = (d * pa - (za[at, lanes].astype(f32) - ma) * qa).astype(bf16)
            db[at, lanes] = (d * pb - (zb[at, lanes].astype(f32) - mb) * qb).astype(bf16)
            return carry
        strips(rows, 256, one, 0)

    for k in range(4):
        lanes = slice(256 * k, 256 * (k + 1))
        side_of(three, proj_pre, delta, n4[:, lanes], n4[:, 1024 + 256 * k : 1280 + 256 * k], s5[:, lanes] * (1.0 / total), d_three, d_proj, lanes)
    for k in range(2):
        lanes = slice(256 * k, 256 * (k + 1))
        side_of(fthree, fskip, fdelta, n3[:, 256 + 256 * k : 512 + 256 * k], n1[:, 384 + 256 * k : 640 + 256 * k],
                s5[:, 1024 + 256 * k : 1280 + 256 * k] * (0.25 / total), d_fthree, d_fproj, lanes)

    wide = slow.shape[1]
    last_acc[...] += dot_tn(two[...], d_three[...])
    proj_acc[:wide] += dot_tn(slow[...], d_proj[...])
    proj_acc[wide:] += dot_tn(lateral[...], d_proj[...])
    flast_term[...] += dot_tn(ftwo[...], d_fthree[...])
    h = normed(two_pre[...], n3[:, :256])
    e = dot_nt(d_three[...], last[...]) * slope(scaled(h, n3[:, :256]))
    e_two[...] = e
    add_sums(step, acc, 0, (eighth(e), eighth(e * h)))
    h = normed(ftwo_pre[...], n2[:, 256:])
    e = dot_nt(d_fthree[...], flast[...]) * slope(scaled(h, n2[:, 256:]))
    e_ftwo[...] = e
    add_sums(step, acc, 256, (eighth(e), eighth(e * h)))
    close_sums(step, acc, sums, ((256, 384, 32),), n, (), *swap)

    @pl.when(step == STEPS - 1)
    def _():
        last_term[...] = last_acc[...].astype(bf16)
        proj_term[...] = proj_acc[...].astype(bf16)


def stage6(total, two, two_pre, proj_pre, slow, lateral, delta, fast4, ftwo, ftwo_pre, fdelta, n1, n2, n3, n4, s5, last, fproj, flast, n):
    rows = two.shape[0]
    part = rows // STEPS
    return run(functools.partial(body6, n, total), rows,
        [(a, "rows") for a in (two, two_pre, proj_pre, slow, lateral, delta, fast4, ftwo, ftwo_pre, fdelta)]
        + [(a, "all") for a in (n1, n2, n3, n4, s5, last, fproj, flast)],
        [((rows, 1024), bf16, "rows"), ((rows, 512), bf16, "rows"), ((256, 1024), bf16, "all"), ((1280, 1024), bf16, "all"), ((128, 512), f32, "all"),
         ((rows, 256), f32, "rows"), ((rows, 128), f32, "rows"), ((2, 384), f32, "all")],
        [pltpu.VMEM((part, 1024), f32), pltpu.VMEM((part, 512), f32), pltpu.VMEM((part, 512), f32),
         pltpu.VMEM((part, 1024), bf16), pltpu.VMEM((part, 512), bf16), pltpu.VMEM((2, 8, 384), f32),
         pltpu.VMEM((256, 1024), f32), pltpu.VMEM((1280, 1024), f32)], n, (2, 384), 7)


def body7(n, side, total, one_pre, two_pre, e_two, fone_pre, ftwo_pre, e_ftwo, n1, n2, n3, s6, middle, fmid, proj_term,
          middleerm, fmid_term, e_one, e_fone, sums, proj_grad, grid, fgrid, acc, mid_acc, *rest):
    step = pl.program_id(0)
    ticks, swap = (), rest
    if n > 1:
        ticks = scatter_ticks(n, (proj_term,), (proj_grad,), rest[:11])
        swap = rest[11:]
        run_ticks(step, n, ticks, (1, 3, 5))
    rows = one_pre.shape[0]

    def put(block):
        at = pl.ds(pl.multiple_of(block * rows, 16), rows)
        p, s = n3[:, :256], s6[:, :256] * (1.0 / total)
        fill(grid, side, input_grad(e_two[at, :], normed(two_pre[at, :], p), p, s[0:1], s[1:2]), block)
        p, s = n2[:, 256:], s6[:, 256:] * (0.25 / total)
        fill(fgrid, side, input_grad(e_ftwo[at, :], normed(ftwo_pre[at, :], p), p, s[0:1], s[1:2]), block)

    @pl.when(step == 0)
    def _():
        clear(grid)
        clear(fgrid)
        clear(acc)
        put(0)
        mid_acc[...] = jnp.zeros_like(mid_acc)
        fmid_term[...] = jnp.zeros_like(fmid_term)

    put(jnp.minimum(step + 1, STEPS - 1))

    def one_side(pre, p, columns, weight, lo, term, e_out):
        h = normed(pre[...], p)
        act = scaled(h, p)
        s = sigma(act)
        mid = act * s
        term[...] += dot_tn(mid.astype(bf16), columns)
        width = weight.shape[1]
        turned = jnp.concatenate([weight[width * k : width * (k + 1)] for k in range(9)], axis=1)
        e = dot_nt(columns, turned) * (s + mid * (1.0 - s))
        e_out[...] = e
        add_sums(step, acc, lo, (eighth(e), eighth(e * h)))

    one_side(one_pre, n2[:, :256], tap_columns(grid, side, step, rows, True), middle, 0, mid_acc, e_one)
    one_side(fone_pre, n1[:, 256:384], tap_columns(fgrid, side, step, rows, True), fmid, 256, fmid_term, e_fone)
    close_sums(step, acc, sums, ((256, 384, 32),), n, ticks, *swap)

    @pl.when(step == STEPS - 1)
    def _():
        for k in range(9):
            middleerm[k] = mid_acc[:, 256 * k : 256 * (k + 1)].astype(bf16)


def stage7(total, one_pre, two_pre, e_two, fone_pre, ftwo_pre, e_ftwo, n1, n2, n3, s6, middle, fmid, proj_term, side, n):
    terms = [six(v, n) for v in (proj_term,)] if n > 1 else [proj_term]
    parts = [(v.shape[0] // n, v.shape[1]) for v in (proj_term,)]
    rows = one_pre.shape[0]
    frames = rows // side**2
    return run(functools.partial(body7, n, side, total), rows,
        [(one_pre, "rows"), (two_pre, "all"), (e_two, "all"), (fone_pre, "rows"), (ftwo_pre, "all"), (e_ftwo, "all")]
        + [(a, "all") for a in (n1, n2, n3, s6, middle, fmid)] + [(v, "any") for v in terms],
        [((9, 256, 256), bf16, "all"), ((128, 1152), f32, "all"), ((rows, 256), f32, "rows"), ((rows, 128), f32, "rows"), ((2, 384), f32, "all")] + [(part, f32, "all") for part in parts],
        [pltpu.VMEM(((side + 2) ** 2 * frames, 256), bf16), pltpu.VMEM(((side + 2) ** 2 * frames, 128), bf16),
         pltpu.VMEM((2, 8, 384), f32), pltpu.VMEM((256, 2304), f32)] + (scatter_scratch(parts, n) if n > 1 else []), n, (2, 384), 8)


def body8(n, total, slow, lateral, one_pre, e_one, n2, s7, mask, middleerm, first_term, pieces, middle_grad, first_acc, *rest):
    step = pl.program_id(0)
    if n > 1:
        ticks = scatter_ticks(n, (middleerm,), (middle_grad,), rest)
        run_ticks(step, n, ticks, (1, 2, 4))

        @pl.when(step == STEPS - 1)
        def _():
            ticks[3]()
    clear_first(step, first_acc)
    p, s = n2[:, :256], s7[:, :256] * (1.0 / total)
    d = input_grad(e_one[...], normed(one_pre[...], p), p, s[0:1], s[1:2])
    w = d.astype(f32)
    rows = w.shape[0]
    before = pltpu.roll(masked(w, mask[0]), rows - 1, 0).astype(bf16)
    after = pltpu.roll(masked(w, mask[1]), 1, 0).astype(bf16)
    columns = jnp.concatenate([before, d, after], axis=1)
    pieces[...] = columns
    wide = slow.shape[1]
    first_acc[:wide] += dot_tn(slow[...], columns)
    first_acc[wide:] += dot_tn(lateral[...], columns)

    @pl.when(step == STEPS - 1)
    def _():
        for k in range(3):
            first_term[k] = first_acc[:, 256 * k : 256 * (k + 1)].astype(bf16)
        if n > 1:
            ticks[4]()


def stage8(total, slow, lateral, one_pre, e_one, n2, s7, mask, middleerm, n):
    rows = slow.shape[0]
    part = (middleerm.shape[0] // n, middleerm.shape[1])
    return run(functools.partial(body8, n, total), rows,
        [(a, "rows") for a in (slow, lateral, one_pre, e_one)] + [(a, "all") for a in (n2, s7, mask)]
        + [(six(middleerm, n) if n > 1 else middleerm, "any")],
        [((3, 1280, 256), bf16, "all"), ((rows, 768), bf16, "rows"), (part, f32, "all")],
        [pltpu.VMEM((1280, 768), f32)] + (scatter_scratch([part], n) if n > 1 else []), n, None, 12)


def body8b(n, pieces, d_proj, lat_pre, n1, first, proj, last_term, first_term,
           slow_grad, e_lat, sums, last_grad, first_grad, acc, *rest):
    step = pl.program_id(0)
    ticks, swap = (), rest
    if n > 1:
        ticks = scatter_ticks(n, (last_term, first_term), (last_grad, first_grad), rest[:16])
        swap = rest[16:]
        run_ticks(step, n, ticks, (1, 3, 5))
    clear_first(step, acc)
    wide = proj.shape[0] - 256

    def back(lo, hi):
        part = dot_nt(d_proj[...], proj[lo:hi])
        for k in range(3):
            part += dot_nt(pieces[:, 256 * k : 256 * (k + 1)], first[k, lo:hi])
        return part

    for k in range(4):
        slow_grad[:, 256 * k : 256 * (k + 1)] = back(256 * k, 256 * (k + 1)).astype(bf16)
    h = normed(lat_pre[...], n1[:, :256])
    e = back(wide, wide + 256) * slope(scaled(h, n1[:, :256]))
    e_lat[...] = e
    add_sums(step, acc, 0, (eighth(e), eighth(e * h)))
    close_sums(step, acc, sums, (), n, ticks, *swap)


def stage8b(pieces, d_proj, lat_pre, n1, first, proj, last_term, first_term, n):
    rows = pieces.shape[0]
    terms = [six(v, n) if n > 1 else v for v in (last_term, first_term)]
    parts = [(v.shape[0] // n, v.shape[1]) for v in (last_term, first_term)]
    return run(functools.partial(body8b, n), rows,
        [(a, "rows") for a in (pieces, d_proj, lat_pre)] + [(a, "all") for a in (n1, first, proj)] + [(v, "any") for v in terms],
        [((rows, 1024), bf16, "rows"), ((rows, 256), f32, "rows"), ((2, 256), f32, "all")] + [(part, f32, "all") for part in parts],
        [pltpu.VMEM((2, 8, 256), f32)] + (scatter_scratch(parts, n) if n > 1 else []), n, (2, 256), 9)


def lanes_at(v, source, target):
    moved = pltpu.roll(v, (target - source) % 128, 1) if target != source else v
    lane = lax.broadcasted_iota(jnp.int32, v.shape, 1)
    return jnp.where((lane >= target) & (lane < target + 32), moved, 0.0)


def pack_fast(out, band, fproj, flast, fmid):
    places_of = (
        ((0, 0, 1), (0, 1, 2), (0, 2, 3), (1, 3, 0)),
        ((0, 0, 0), (0, 1, 1), (0, 2, 2), (0, 3, 3)),
        ((0, 1, 0), (0, 2, 1), (0, 3, 2), (2, 0, 3)),
    )
    for tap in range(3):
        out[32 * tap : 32 * (tap + 1)] = sum(
            band[128 * part + 32 * j : 128 * part + 32 * (j + 1), 128 * k : 128 * (k + 1)] for part, k, j in places_of[tap])
    out[96:224] = fproj[...]
    out[224:256] = sum(flast[32 * k : 32 * (k + 1), 128 * k : 128 * (k + 1)] for k in range(4))
    for group in range(3):
        total = None
        for tap in range(4 * group, min(4 * group + 4, 9)):
            for k in range(4):
                turned = fmid[:, 128 * tap : 128 * (tap + 1)].T
                v = lanes_at(turned[32 * k : 32 * (k + 1)], 32 * k, 32 * (tap % 4))
                total = v if total is None else total + v
        out[256 + 32 * group : 288 + 32 * group] = total
    out[352:384] = jnp.zeros((32, 128), f32)


def own_pair(out, sums, lo, hi, row):
    share = out.shape[1]
    back = lax.rem(hi - lo - lax.axis_index("fsdp") * share, hi - lo)
    for at, k in enumerate((row, 0)):
        wide = jnp.broadcast_to(sums[k : k + 1, lo:hi], (8, hi - lo))
        out[at : at + 1] = pltpu.roll(wide, back, 1)[0:1, :share]


def body9(n, total, fast4, lat_pre, e_lat, fone_pre, e_fone, d_fproj, ready, n1, s5, s6, s7, s8, lat, band, fproj, mask, flast_term, fmid_term,
          ready_first, ready_middle, ready_last, ready_proj, lat_term, packed, raw, slow_grad, lat_n, one_n, two_n, out_n, proj_n, mid_n, fout_n,
          first_grad, middle_grad, last_grad, proj_grad, wide, lat_acc, whole, band_term, fproj_term):
    step = pl.program_id(0)
    clear_first(step, lat_acc, band_term, fproj_term)
    slow_grad[...] = ready[...]
    rows = fast4.shape[0]
    def backward(e, pre, p, s):
        d = input_grad(e[...], normed(pre[...], p), p, s[0:1], s[1:2])
        w = d.astype(f32)
        return d, pltpu.roll(masked(w, mask[0]), rows - 1, 0).astype(bf16), pltpu.roll(masked(w, mask[1]), 1, 0).astype(bf16)
    d, before, _ = backward(e_lat, lat_pre, n1[:, :256], s8[...] * (1.0 / total))
    f, fbefore, fafter = backward(e_fone, fone_pre, n1[:, 256:384], s7[:, 256:] * (0.25 / total))
    narrow = jnp.concatenate([f, fbefore, fafter], axis=1)
    lat_acc[:, :256] += dot_tn(before, fast4[:, 256:])
    lat_acc[:, 256:] += dot_tn(d, fast4[:, :384])
    band_term[...] += dot_tn(narrow, fast4[...])
    for k in range(4):
        fproj_term[...] += dot_tn(fast4[:, 128 * k : 128 * (k + 1)], d_fproj[:, 128 * k : 128 * (k + 1)])
    base = dot_nt(narrow, band[...])
    skip = jnp.concatenate([dot_nt(d_fproj[:, 256 * k : 256 * (k + 1)], fproj[...]) for k in range(2)], axis=1)
    whole[...] = base + skip
    whole[:, :384] += dot(d, lat[:, 256:])
    whole[:, 256:] += dot(before, lat[:, :256])
    join_fours(whole[...], wide, raw)

    @pl.when(step == STEPS - 1)
    def _():
        lat_term[...] = lat_acc[...].astype(bf16)
        for grad, found in ((first_grad, ready_first), (middle_grad, ready_middle), (last_grad, ready_last), (proj_grad, ready_proj)):
            grad[...] = found[...]
        pack_fast(packed, band_term, fproj_term, flast_term, fmid_term)
        if n > 1:
            own_pair(lat_n, s8, 0, 256, 1)
            own_pair(one_n, s7, 0, 256, 1)
            own_pair(two_n, s6, 0, 256, 1)
            own_pair(out_n, s5, 0, 1024, 1)
            own_pair(proj_n, s5, 0, 1024, 2)
        for j, (sums, lo, row) in enumerate(((s7, 256, 1), (s6, 256, 1))):
            mid_n[j, 0:1] = sums[row : row + 1, lo : lo + 32]
            mid_n[j, 1:2] = sums[0:1, lo : lo + 32]
        for j in range(2):
            fout_n[j, 0:1] = s5[j + 1 : j + 2, 1024:1152]
            fout_n[j, 1:2] = s5[0:1, 1024:1152]


def stage9(total, fast4, lat_pre, e_lat, fone_pre, e_fone, d_fproj, ready, n1, s5, s6, s7, s8, lat, band, fproj, mask, flast_term, fmid_term, grads, n):
    rows = fast4.shape[0]
    part = rows // STEPS
    return run(functools.partial(body9, n, total), rows,
        [(a, "rows") for a in (fast4, lat_pre, e_lat, fone_pre, e_fone, d_fproj, ready)]
        + [(a, "all") for a in (n1, s5, s6, s7, s8, lat, band, fproj, mask, flast_term, fmid_term) + tuple(grads)],
        [((256, 640), bf16, "all"), ((384, 128), f32, "all"), ((rows // 16, 64, 128), bf16, "rows"), (ready.shape, bf16, "rows")]
        + [((2, 256 // n), f32, "all")] * 3 + [((2, 1024 // n), f32, "all")] * 2 + [((2, 2, 32), f32, "all"), ((2, 2, 128), f32, "all")] + [(v.shape, f32, "all") for v in grads],
        [pltpu.VMEM((part * 4, 128), f32), pltpu.VMEM((256, 640), f32), pltpu.VMEM((part, 512), f32),
         pltpu.VMEM((384, 512), f32), pltpu.VMEM((128, 128), f32)])


def body10(n, lat_term, packed, lat_grad, first_t, middle_t, last, proj, sums, slots, line, mine, lat_slots, lat_line, lat_mine,
           a_send, a_recv, b_send, b_recv, g_send, g_recv, l_send, l_recv, m_send, m_recv):
    me = lax.axis_index("fsdp")
    mi, mo, depth = lax.rem(me, INNER), lax.div(me, INNER), n // INNER
    peers = [mo * INNER + lax.rem(mi + k, INNER) for k in range(INNER)]
    spots = [lax.rem(mi + k, INNER) for k in range(INNER)]
    beyond = [lax.rem(mo + k, depth) for k in range(depth)]

    def remote(src, dst, send, recv, peer):
        copy = pltpu.make_async_remote_copy(
            src_ref=src, dst_ref=dst, send_sem=send, recv_sem=recv, device_id=(peer,), device_id_type=MESH)
        copy.start()
        return copy

    greet(n)
    greeted(n)
    fast = [remote(packed.at[spots[k]], slots.at[mi], a_send.at[k], a_recv.at[k], peers[k]) for k in range(1, INNER)]
    slow = [remote(lat_term.at[:, spots[k]], lat_slots.at[mi], l_send.at[k], l_recv.at[k], peers[k]) for k in range(1, INNER)]
    slots[mi] = packed[mi]
    lat_slots[mi] = lat_term[:, mi]
    for copy in fast:
        copy.wait()
    mine[...] = sum(slots[k] for k in range(1, INNER)) + slots[0]
    fast = [remote(mine, line.at[mo], b_send.at[k], b_recv.at[k], beyond[k] * INNER + mi) for k in range(1, depth)]
    line[mo] = mine[...]
    for copy in slow:
        copy.wait()
    lat_mine[...] = sum(lat_slots[k].astype(f32) for k in range(INNER)).astype(bf16)
    slow = [remote(lat_mine.at[beyond[k]], lat_line.at[mo], m_send.at[k], m_recv.at[k], beyond[k] * INNER + mi) for k in range(1, depth)]
    lat_line[mo] = lat_mine[mo]
    for copy in fast:
        copy.wait()
    sums[mi] = sum((line[k] for k in range(1, depth)), line[0])
    fast = [remote(sums.at[mi], sums.at[mi], g_send.at[k], g_recv.at[k], peers[k]) for k in range(1, INNER)]
    for copy in slow:
        copy.wait()
    lat_grad[...] = sum(lat_line[k].astype(f32) for k in range(depth))
    for copy in fast:
        copy.wait()

    high = sums.shape[1]
    def rows_of(lo, hi):
        found = []
        while lo < hi:
            top = min(hi, (lo // high + 1) * high)
            found.append(sums[lo // high, lo % high : lo % high + top - lo])
            lo = top
        return jnp.concatenate(found, axis=0) if len(found) > 1 else found[0]

    for k in range(3):
        first_t[:, 128 * k : 128 * (k + 1)] = rows_of(32 * k, 32 * (k + 1))
        wide = min(128, 288 - 128 * k)
        middle_t[:, 128 * k : 128 * k + wide] = rows_of(256 + 32 * k, 288 + 32 * k)[:, :wide]
    proj[...] = rows_of(96, 224)
    last[...] = rows_of(224, 256)


def stage10(lat_term, packed, n):
    depth, DS = n // INNER, pltpu.SemaphoreType.DMA
    packed = packed.reshape(INNER, -1, 128)
    chunk = packed.shape[1:]
    share = (lat_term.shape[0] // n, lat_term.shape[1])
    lat_grad, first_t, middle_t, last, proj = pl.pallas_call(
        functools.partial(body10, n),
        in_specs=[pl.BlockSpec(memory_space=pltpu.VMEM)] * 2,
        out_specs=[pl.BlockSpec(memory_space=pltpu.VMEM)] * 5,
        out_shape=[jax.ShapeDtypeStruct(shape, f32) for shape in (share, (32, 384), (32, 288), (32, 128), (128, 128))],
        scratch_shapes=[pltpu.VMEM((INNER,) + chunk, f32), pltpu.VMEM((INNER,) + chunk, f32), pltpu.VMEM((depth,) + chunk, f32), pltpu.VMEM(chunk, f32),
            pltpu.VMEM((INNER, depth) + share, bf16), pltpu.VMEM((depth,) + share, bf16), pltpu.VMEM((depth,) + share, bf16)]
        + [DS((INNER,)), DS((INNER,)), DS((depth,)), DS((depth,)), DS((INNER,)), DS((INNER,)), DS((INNER,)), DS((INNER,)), DS((depth,)), DS((depth,))],
        compiler_params=pltpu.CompilerParams(collective_id=10, has_side_effects=True),
    )(lat_term.reshape((depth, INNER) + share), packed)
    return lat_grad, (first_t.T, middle_t.T, last, proj)


def spread(weight, groups):
    eye = jnp.eye(groups, dtype=weight.dtype)
    r, c = weight.shape[-2:]
    wide = eye[:, None, :, None] * weight[..., None, :, None, :]
    return wide.reshape(weight.shape[:-2] + (groups * r, groups * c))


def banded(fast_first):
    table = np.zeros((3, 4, 3, 4), np.float32)
    for tap in range(3):
        for j in range(4):
            k = j + tap - 1
            part = 1 if k < 0 else 2 if k > 3 else 0
            table[tap, k % 4, part, j] = 1
    tap = fast_first.reshape(3, 128, 32)
    total = sum(table[k].astype(tap.dtype)[:, None, :, :, None] * tap[k][None, :, None, None, :] for k in range(3))
    return total.reshape(512, 384)


def shards(slow_in, fast_in, clip_ids, lateral_weight, first_weight, middle_weight, last_weight, proj_weight,
           lat_norm, one_norm, two_norm, out_norm, proj_norm, fast_first, fast_middle, fast_last, fast_proj,
           fast_mid_norm, fast_out_norm, slow_cot, fast_cot):
    n = lax.axis_size("fsdp")
    side = slow_in.shape[1]
    count = slow_in.shape[0] * side * side * n
    norms = jnp.concatenate([lat_norm, one_norm, two_norm, out_norm, proj_norm], axis=1).astype(f32)
    norms = jnp.pad(norms, ((0, 6), (0, 128 - norms.shape[1])))
    lat, norms_full, first = stage0([lateral_weight.T, norms, first_weight], n)
    lat = gathered(lat, n)
    norms_full = norms_full.reshape(n, 8, 128)
    gains, offset = [], 0
    for pair in (lat_norm, one_norm, two_norm, out_norm, proj_norm):
        width = pair.shape[1]
        gains.append(norms_full[:, :2, offset : offset + width].transpose(1, 0, 2).reshape(2, -1))
        offset += width
    spair = jnp.concatenate(gains, axis=1)
    fpair = jnp.concatenate(
        [jnp.tile(pair[k].astype(f32), (1, 4)) for pair in (fast_mid_norm, fast_out_norm) for k in range(2)], axis=1)
    band = banded(fast_first)
    fproj = spread(fast_proj, 2)
    fmid = spread(fast_middle.reshape(9, 32, 32), 4)
    fmid = fmid.reshape(-1, 128)
    flast = spread(fast_last, 4)

    same = (clip_ids[0, 1:] == clip_ids[0, :-1]).astype(f32)
    closed = jnp.zeros((1,), f32)
    mask = jnp.stack([jnp.concatenate([closed, same]), jnp.concatenate([same, closed])])
    mask = jnp.broadcast_to(mask[:, :, None], mask.shape + (256,))

    def rows(v):
        return v.transpose(1, 2, 0, 3).reshape(-1, v.shape[3])
    def unrows(v):
        return v.reshape(side, side, -1, v.shape[1]).transpose(2, 0, 1, 3)
    def raw(v):
        return v.transpose(1, 2, 0, 3).reshape(side * side, -1, v.shape[3])
    def unraw(v):
        return v.reshape((side, side) + v.shape[1:]).transpose(2, 0, 1, 3)

    slow = rows(slow_in)
    fast4, lat_pre, fone_pre, n1, first, *held = stage1(
        raw(fast_in), lat, band, fproj, mask, spair, fpair, first, (middle_weight, last_weight), n)
    first = gathered(first, n).reshape(3, -1, first_weight.shape[1])
    lateral, one_pre, ftwo_pre, n2, middle, last, proj = stage2(
        slow, lat_pre, fone_pre, n1, first, fmid, mask, spair, fpair, held, proj_weight, side, n)
    middle = gathered(middle, n)
    two_pre, ftwo, n3, last, proj = stage3(one_pre, ftwo_pre, n2, middle, flast, spair, fpair, (last, proj), side, n)
    last, proj = gathered(last, n), gathered(proj, n)
    two, proj_pre, n4 = stage4(two_pre, slow, lateral, n3, last, proj, spair, n)
    slow_out, fast_out, delta, fdelta, local = stage5(
        two, proj_pre, rows(slow_cot), fast4, ftwo, raw(fast_cot), n1, n3, n4, last, fproj, flast)
    s5 = stage5x(local, n)
    d_proj, d_fproj, last_term, proj_term, flast_term, e_two, e_ftwo, s6 = stage6(
        count, two, two_pre, proj_pre, slow, lateral, delta, fast4, ftwo, ftwo_pre, fdelta, n1, n2, n3, n4, s5, last, fproj, flast, n)
    middle_term, fmid_term, e_one, e_fone, s7, proj_grad = stage7(
        count, one_pre, two_pre, e_two, fone_pre, ftwo_pre, e_ftwo, n1, n2, n3, s6, middle, fmid, proj_term, side, n)
    first_term, pieces, middle_grad = stage8(count, slow, lateral, one_pre, e_one, n2, s7, mask, middle_term.reshape(-1, 256), n)
    slow_grad, e_lat, s8, last_grad, first_grad = stage8b(
        pieces, d_proj, lat_pre, n1, first, proj, last_term, first_term.reshape(-1, 256), n)
    lat_term, packed, fast_grad, slow_grad, *small = stage9(
        count, fast4, lat_pre, e_lat, fone_pre, e_fone, d_fproj, slow_grad, n1, s5, s6, s7, s8, lat, band, fproj, mask, flast_term, fmid_term,
        (first_grad, middle_grad, last_grad, proj_grad), n)
    lateral_grad, fast_grads = stage10(lat_term, packed, n)
    return (unrows(slow_out), unraw(fast_out), unrows(slow_grad), unraw(fast_grad),
            lateral_grad.T, *small[7:],
            *small[:5], *fast_grads, *small[5:7])


def solution(mesh):
    in_specs = (
        P("fsdp", None, None, None),
        P("fsdp", None, None, None),
        P("fsdp", None),
        P(None, "fsdp"),
        P("fsdp", None),
        P("fsdp", None),
        P("fsdp", None),
        P("fsdp", None),
        P(None, "fsdp"),
        P(None, "fsdp"),
        P(None, "fsdp"),
        P(None, "fsdp"),
        P(None, "fsdp"),
        P(),
        P(),
        P(),
        P(),
        P(),
        P(),
        P("fsdp", None, None, None),
        P("fsdp", None, None, None),
    )
    out_specs = (
        P("fsdp", None, None, None),
        P("fsdp", None, None, None),
        P("fsdp", None, None, None),
        P("fsdp", None, None, None),
        P(None, "fsdp"),
        P("fsdp", None),
        P("fsdp", None),
        P("fsdp", None),
        P("fsdp", None),
        P(None, "fsdp"),
        P(None, "fsdp"),
        P(None, "fsdp"),
        P(None, "fsdp"),
        P(None, "fsdp"),
        P(),
        P(),
        P(),
        P(),
        P(),
        P(),
    )
    return jax.shard_map(shards, mesh=mesh, in_specs=in_specs, out_specs=out_specs, check_vma=False)
```

```python
import functools

import jax
import jax.numpy as jnp
import numpy as np
from jax import lax
from jax.experimental import pallas as pl
from jax.experimental.pallas import tpu as pltpu
from jax.sharding import PartitionSpec as P

EPSILON = 1e-05


MESH = pl.DeviceIdType.MESH


f32 = jnp.float32
bf16 = jnp.bfloat16
STEPS = 7
STRIP = 32


def dot(a, b):
    return lax.dot_general(a, b, (((1,), (0,)), ((), ())), preferred_element_type=f32)


def dot_nt(a, b):
    return lax.dot_general(a, b, (((1,), (1,)), ((), ())), preferred_element_type=f32)


def dot_tn(a, b):
    return lax.dot_general(a, b, (((0,), (0,)), ((), ())), preferred_element_type=f32)


def shift(v, mask, by):
    rows = v.shape[0]
    moved = pltpu.roll(v, by % rows, 0)
    return masked(moved, mask)


def masked(v, mask):
    return (v.reshape(-1, mask.shape[0], v.shape[1]) * mask[None, :, : v.shape[1]]).reshape(v.shape)


def sigma(x):
    return 0.5 + 0.5 * jnp.tanh(0.5 * x)


def silu(x):
    return x * sigma(x)


def slope(x):
    s = sigma(x)
    return s * (1.0 + x * (1.0 - s))


def normed(z, n):
    return (z - n[0:1]) * n[1:2]


def scaled(hat, n):
    return hat * n[2:3] + n[3:4]


def acted(z, n):
    return scaled(normed(z, n), n)


def input_grad(e, hat, n, s_mean, s_cross):
    return ((n[2:3] * n[1:2]) * (e - s_mean - hat * s_cross)).astype(bf16)


def eighth(v):
    return jnp.sum(v.reshape(-1, 8, v.shape[1]), axis=0)


def clear_first(step, *refs):
    @pl.when(step == 0)
    def _():
        for ref in refs:
            ref[...] = jnp.zeros(ref.shape, ref.dtype)


def add_moments(step, acc, lo, z):
    hi = lo + z.shape[1]
    high = z.shape[0] // 8
    deep = z.reshape(high, 8, hi - lo)
    own = jnp.sum(deep, axis=0) * (1.0 / high)
    off = deep - own[None]
    spread_of = jnp.sum(off * off, axis=0)
    past = step.astype(f32)
    share = 1.0 / (past + 1.0)
    gap = own - acc[0, :, lo:hi]
    acc[0, :, lo:hi] += gap * share
    acc[1, :, lo:hi] += spread_of + gap * gap * (past * share * high)


def add_sums(step, acc, lo, parts):
    hi = lo + parts[0].shape[1]
    for k, part in enumerate(parts):
        acc[k, :, lo:hi] += part


def split_fours(raw, wide):
    rows = wide.shape[0]
    wide[...] = raw[...].astype(f32).reshape(rows, 128)
    return jnp.concatenate([wide[pl.ds(k, rows // 4, stride=4), :] for k in range(4)], axis=1)


def join_fours(value, wide, raw):
    rows = wide.shape[0]
    for k in range(4):
        wide[pl.ds(k, rows // 4, stride=4), :] = value[:, 128 * k : 128 * (k + 1)]
    raw[...] = wide[...].astype(bf16).reshape(raw.shape)


def clear(grid):
    grid[...] = jnp.zeros(grid.shape, grid.dtype)


def fill(grid, side, value, block):
    per = side // STEPS
    line = value.shape[0] // per
    frames = line // side
    for r in range(per):
        at = ((block * per + r + 1) * (side + 2) + 1) * frames
        grid[pl.ds(pl.multiple_of(at, 16), line), :] = value[r * line : (r + 1) * line]


def tap_columns(grid, side, step, rows, flip):
    per = side // STEPS
    line = rows // per
    frames = line // side
    lines = []
    for r in range(per):
        pieces = []
        for a in range(3):
            for b in range(3):
                ra, rb = (2 - a, 2 - b) if flip else (a, b)
                at = ((step * per + r + ra) * (side + 2) + rb) * frames
                pieces.append(grid[pl.ds(pl.multiple_of(at, 16), line), :])
        lines.append(jnp.concatenate(pieces, axis=1))
    return jnp.concatenate(lines, axis=0)


INNER = 8


def greet(n):
    me = lax.axis_index("fsdp")
    mi, mo, depth = lax.rem(me, INNER), lax.div(me, INNER), n // INNER
    barrier = pltpu.get_barrier_semaphore()
    for k in range(1, INNER):
        pl.semaphore_signal(barrier, inc=1, device_id=(mo * INNER + lax.rem(mi + k, INNER),), device_id_type=MESH)
    for k in range(1, depth):
        pl.semaphore_signal(barrier, inc=1, device_id=(lax.rem(mo + k, depth) * INNER + mi,), device_id_type=MESH)


def greeted(n):
    pl.semaphore_wait(pltpu.get_barrier_semaphore(), INNER - 1 + n // INNER - 1)


def total_of(n, centred, own, near, far, mid, near_send, near_recv, far_send, far_recv):
    me = lax.axis_index("fsdp")
    mi, mo, depth = lax.rem(me, INNER), lax.div(me, INNER), n // INNER

    def swap(src, slots, sends, recvs, mine, size, peer):
        copies = []
        for k in range(1, size):
            copy = pltpu.make_async_remote_copy(
                src_ref=src, dst_ref=slots.at[mine], send_sem=sends.at[k], recv_sem=recvs.at[k],
                device_id=(peer(k),), device_id_type=MESH)
            copy.start()
            copies.append(copy)
        slots[mine] = src[...]
        for copy in copies:
            copy.wait()

    def merge(slots, size):
        if not centred:
            return sum(slots[k] for k in range(1, size)) + slots[0]
        mean = sum(slots[k, 0:1] for k in range(size)) * (1.0 / size)
        off = [slots[k, 0:1] - mean for k in range(size)]
        return jnp.concatenate([mean, sum(slots[k, 1:2] + off[k] * off[k] for k in range(size)) * (1.0 / size)], axis=0)

    swap(own, near, near_send, near_recv, mi, INNER, lambda k: mo * INNER + lax.rem(mi + k, INNER))
    mid[...] = merge(near, INNER)
    if depth == 1:
        return mid[...]
    swap(mid, far, far_send, far_recv, mo, depth, lambda k: lax.rem(mo + k, depth) * INNER + mi)
    return merge(far, depth)


def over_groups(part, width):
    lanes = part.shape[1]
    if width < 128:
        wide = jnp.broadcast_to(part, (8, lanes))
        total = wide
        for k in range(1, lanes // width):
            total = total + pltpu.roll(wide, k * width, 1)
        return total[0:1]
    total = sum(part[:, k : k + width] for k in range(0, lanes, width))
    return jnp.concatenate([total] * (lanes // width), axis=1)


def norm_pack(total, pairs, out, folds):
    out[0:2] = total
    for lo, hi, width in folds:
        groups = width / (hi - lo)
        mean = over_groups(total[0:1, lo:hi], width) * groups
        off = total[0:1, lo:hi] - mean
        out[0:1, lo:hi] = mean
        out[1:2, lo:hi] = over_groups(total[1:2, lo:hi] + off * off, width) * groups
    out[1:2] = lax.rsqrt(out[1:2] + EPSILON)
    at = 0
    for pair, lo, hi in pairs:
        out[2:4, at : at + hi - lo] = pair[:, lo:hi]
        at += hi - lo


def sum_pack(total, out, folds):
    out[...] = total
    for lo, hi, width in folds:
        for k in range(out.shape[0]):
            out[k : k + 1, lo:hi] = over_groups(total[k : k + 1, lo:hi], width)


def swap_scratch(shape, n):
    DS, depth = pltpu.SemaphoreType.DMA, n // INNER
    return [pltpu.VMEM((INNER,) + shape, f32), pltpu.VMEM((depth,) + shape, f32), pltpu.VMEM(shape, f32),
        DS((INNER,)), DS((INNER,)), DS((depth,)), DS((depth,))]


def run(body, rows, ins, outs, scratch, n=1, swap=None, call=None, same=None):
    def spec(shape, how):
        if how == "any":
            return pl.BlockSpec(memory_space=pl.ANY)
        if how == "rows":
            return pl.BlockSpec((shape[0] // STEPS,) + tuple(shape[1:]), lambda i, d=len(shape): (i,) + (0,) * (d - 1))
        return pl.BlockSpec(tuple(shape), lambda i, d=len(shape): (0,) * d, pipeline_mode=pl.Buffered(1))
    def out_spec(shape, how):
        if how in ("rows", "any"):
            return spec(shape, how)
        return pl.BlockSpec(tuple(shape), lambda i, d=len(shape): (0,) * d)
    extra = {}
    if swap is not None:
        scratch = scratch + [pltpu.VMEM(swap, f32)]
    if n > 1 and swap is not None:
        scratch = scratch + swap_scratch(swap, n)
    if n > 1 and call is not None:
        extra = dict(collective_id=call, has_side_effects=True)
    return pl.pallas_call(
        body,
        grid=(STEPS,),
        in_specs=[spec(a.shape, how) for a, how in ins],
        out_specs=[out_spec(shape, how) for shape, _, how in outs],
        out_shape=[jax.ShapeDtypeStruct(shape, kind) for shape, kind, _ in outs],
        scratch_shapes=scratch,
        input_output_aliases=same or {},
        compiler_params=pltpu.CompilerParams(dimension_semantics=("arbitrary",), vmem_limit_bytes=58 * 1024 * 1024, **extra),
    )(*[a for a, _ in ins])


def close_moments(step, acc, pairs, out, count, folds, n, ticks, own, *links):
    @pl.when(step == STEPS - 1)
    def _():
        mean = jnp.mean(acc[0], axis=0, keepdims=True)
        off = acc[0] - mean
        own[0:1] = mean
        own[1:2] = jnp.sum(acc[1], axis=0, keepdims=True) * (1.0 / count) + jnp.mean(off * off, axis=0, keepdims=True)
        if n > 1:
            ticks[3]()
            norm_pack(total_of(n, True, own, *links), pairs, out, folds)
            ticks[4]()
        else:
            norm_pack(own[...], pairs, out, folds)


def close_sums(step, acc, out, folds, n, ticks, own, *links):
    if n > 1 and not ticks:
        @pl.when(step == 0)
        def _():
            greet(n)

    @pl.when(step == STEPS - 1)
    def _():
        for k in range(acc.shape[0]):
            own[k : k + 1] = jnp.sum(acc[k], axis=0, keepdims=True)
        if n > 1:
            if ticks:
                ticks[3]()
            else:
                greeted(n)
            sum_pack(total_of(n, False, own, *links), out, folds)
            if ticks:
                ticks[4]()
        else:
            sum_pack(own[...], out, folds)


def places():
    me = lax.axis_index("fsdp")
    return lax.div(me, 8), lax.rem(lax.div(me, 4), 2), lax.rem(lax.div(me, 2), 2), lax.rem(me, 2)


def flat(z, y, x, c):
    return ((z * 2 + y) * 2 + x) * 2 + c


def six(term, n):
    return term.reshape((n // 8, 2, 2, 2, term.shape[0] // n) + term.shape[1:])


def halves(width):
    if width < 256:
        return ((0, width),)
    middle = width // 256 * 128
    return ((0, middle), (middle, width))


def scatter_scratch(parts, n):
    depth, k, DS = n // 8, len(parts), pltpu.SemaphoreType.DMA
    def buf(lead):
        return [pltpu.VMEM(lead + part, bf16) for part in parts]
    return (buf((depth, 2, 2)) + buf((depth, 2, 2)) + buf((depth, 2)) + buf((depth,)) + buf((depth,))
        + [DS((k,)), DS((k, 2)), DS((k, 2, 2)), DS((k, 2, 2)), DS((k, depth)), DS((k, depth))])


def scatter_ticks(n, ins, outs, rest):
    k, depth = len(ins), n // 8
    half, r1, r2, r3, r4 = (rest[j * k : (j + 1) * k] for j in range(5))
    own_sem, c_sem, p_sem, q_sem, z_send, z_recv = rest[5 * k :]
    z, y, x, c = places()
    core, over_x, over_y = flat(z, y, x, 1 - c), flat(z, y, 1 - x, c), flat(z, 1 - y, x, c)
    line = [flat(lax.rem(z + s, depth), y, x, c) for s in range(depth)]
    spots = [lax.rem(z + s, depth) for s in range(depth)]

    def remote(src, dst, send, recv, peer):
        return pltpu.make_async_remote_copy(
            src_ref=src, dst_ref=dst, send_sem=send, recv_sem=recv, device_id=(peer,), device_id_type=MESH)
    def sides(i):
        return tuple(enumerate(halves(half[i].shape[-1])))
    def own(i):
        return pltpu.make_async_copy(ins[i].at[:, :, :, c], half[i], own_sem.at[i])
    def to_core(i):
        return remote(ins[i].at[:, :, :, 1 - c], r1[i], c_sem.at[i, 0], c_sem.at[i, 1], core)
    def to_first(i, t, lo, hi):
        src, peer = (half[i].at[:, :, 1 - x, :, lo:hi], over_x) if t == 0 else (half[i].at[:, 1 - y, :, :, lo:hi], over_y)
        return remote(src, r2[i].at[:, :, :, lo:hi], p_sem.at[i, t, 0], p_sem.at[i, t, 1], peer)
    def to_second(i, t, lo, hi):
        src, peer = (half[i].at[:, 1 - y, x, :, lo:hi], over_y) if t == 0 else (half[i].at[:, y, 1 - x, :, lo:hi], over_x)
        return remote(src, r3[i].at[:, :, lo:hi], q_sem.at[i, t, 0], q_sem.at[i, t, 1], peer)
    def to_line(i, s):
        return remote(half[i].at[spots[s], y, x], r4[i].at[s], z_send.at[i, s], z_recv.at[i, s], line[s])
    def add(target, other):
        target[...] = (target[...].astype(f32) + other[...].astype(f32)).astype(target.dtype)

    def begin():
        for i in range(k):
            own(i).start()
            to_core(i).start()
    def first():
        for i in range(k):
            own(i).wait()
            to_core(i).wait()
            @pl.loop(0, depth)
            def _(zz, i=i):
                for a in range(2):
                    for b in range(2):
                        add(half[i].at[zz, a, b], r1[i].at[zz, a, b])
            for t, (lo, hi) in sides(i):
                to_first(i, t, lo, hi).start()
    def second():
        for i in range(k):
            for t, (lo, hi) in sides(i):
                to_first(i, t, lo, hi).wait()
                @pl.loop(0, depth)
                def _(zz, i=i, t=t, lo=lo, hi=hi):
                    for o in range(2):
                        target = half[i].at[zz, o, x] if t == 0 else half[i].at[zz, y, o]
                        add(target.at[:, lo:hi], r2[i].at[zz, o, :, lo:hi])
                to_second(i, t, lo, hi).start()
    def third():
        for i in range(k):
            for t, (lo, hi) in sides(i):
                to_second(i, t, lo, hi).wait()
            @pl.loop(0, depth)
            def _(zz, i=i):
                add(half[i].at[zz, y, x], r3[i].at[zz])
            for s in range(1, depth):
                to_line(i, s).start()
    def finish():
        for i in range(k):
            outs[i][...] = half[i][z, y, x].astype(f32)
            for s in range(1, depth):
                to_line(i, s).wait()
                outs[i][...] += r4[i][s].astype(f32)
    return begin, first, second, third, finish


GATHER_SEMS = 9


def gather_scratch(k, n):
    DS, depth = pltpu.SemaphoreType.DMA, n // 8
    return [DS((1,)), DS((depth,)), DS((depth,)), DS((2, 2)), DS((2, 2)), DS((2, 3)), DS((2, 3)), DS((8,)), DS((8,))] * k


class Moves:
    def __init__(self, n, shard, whole, sems):
        self.n, self.shard, self.whole, self.sems = n, shard, whole, sems
        self.at = places()
        self.sides = tuple(enumerate(halves(whole.shape[-1])))

    def remote(self, src, dst, send, recv, *peer):
        return pltpu.make_async_remote_copy(
            src_ref=src, dst_ref=dst, send_sem=send, recv_sem=recv, device_id=(flat(*peer),), device_id_type=MESH)

    def part(self, name, t, lo, hi):
        z, y, x, c = self.at
        index = {
            "p": (slice(None), y, x, c),
            "q": (slice(None), y, slice(None), c) if t == 0 else (slice(None), slice(None), x, c),
            "c1": (slice(None), y, 1 - x, c) if t == 0 else (slice(None), 1 - y, x, c),
            "c2": (slice(None), 1 - y, slice(None), c) if t == 0 else (slice(None), slice(None), 1 - x, c),
        }["p" if name == "c0" else name]
        return self.whole.at[index + (slice(None), slice(lo, hi))]

    def copies(self, name):
        z, y, x, c = self.at
        own, z_send, z_recv, p, q, c_send, c_recv, d_send, d_recv = self.sems
        depth = self.n // 8
        if name == "z":
            mine = self.whole.at[z, y, x, c]
            return [pltpu.make_async_copy(self.shard, mine, own.at[0])] + [
                self.remote(self.shard, mine, z_send.at[s], z_recv.at[s], lax.rem(z + s, depth), y, x, c) for s in range(1, depth)]
        if name == "d":
            mine = self.whole.at[:, y, x, c]
            found = []
            for k in range(1, 8):
                other = lax.rem((y * 2 + x) * 2 + c + k, 8)
                found.append(self.remote(mine, mine, d_send.at[k], d_recv.at[k], z, 0, 0, other))
            return found
        found = []
        for t, (lo, hi) in self.sides:
            src = self.part(name, t, lo, hi)
            if name[0] == "c":
                j = int(name[1])
                found.append(self.remote(src, src, c_send.at[t, j], c_recv.at[t, j], z, y, x, 1 - c))
                continue
            sem = p if name == "p" else q
            peer = (z, y, 1 - x, c) if (t == 0) == (name == "p") else (z, 1 - y, x, c)
            found.append(self.remote(src, src, sem.at[t, 0], sem.at[t, 1], *peer))
        return found

    def start(self, *names):
        for name in names:
            for copy in self.copies(name):
                copy.start()

    def wait(self, *names):
        for name in names:
            for copy in self.copies(name):
                copy.wait()


def moves(n, shards, wholes, rest):
    return [Moves(n, shard, whole, rest[GATHER_SEMS * i : GATHER_SEMS * (i + 1)]) for i, (shard, whole) in enumerate(zip(shards, wholes))]


def spread_shapes(shards, n):
    return [((n // 8, 2, 2, 2) + v.shape, v.dtype, "any") for v in shards]


def whole_shapes(wholes):
    return [(v.shape, v.dtype, "any") for v in wholes]


def gathered(v, n):
    return v.reshape((n * v.shape[4],) + v.shape[5:])


def at_lanes(v, offset):
    rows, width = v.shape
    wide = v if width == 128 else jnp.concatenate([v, jnp.zeros((rows, 128 - width), v.dtype)], axis=1)
    return pltpu.roll(wide, offset, 1) if offset else wide


def build_fast(first_t, middle_t, last, skip, mid_norm, out_norm, ids, band, fproj, fmid, flast, fpair, mask, lanes):
    band[...] = jnp.zeros(band.shape, bf16)
    fproj[...] = jnp.zeros(fproj.shape, bf16)
    flast[...] = jnp.zeros(flast.shape, bf16)
    none = jnp.zeros((96, 128), f32)
    for tap in range(3):
        block = jnp.concatenate([first_t[:, 128 * tap : 128 * (tap + 1)].astype(f32), none], axis=0).T
        placed = [pltpu.roll(block, 32 * j, 1) if j else block for j in range(4)]
        for part in range(3):
            for k in range(4):
                here = [j for j in range(4) if (j + tap - 1) % 4 == k and part == (1 if j + tap < 1 else 2 if j + tap > 4 else 0)]
                if here:
                    (j,) = here
                    band[128 * k : 128 * (k + 1), 128 * part : 128 * (part + 1)] += placed[j].astype(bf16)
    lanes[...] = jnp.zeros(lanes.shape, f32)
    lanes[:, :288] = middle_t[...].astype(f32)
    for group in range(3):
        block = jnp.concatenate([lanes[:, 128 * group : 128 * (group + 1)], none], axis=0).T
        for tap in range(4 * group, min(4 * group + 4, 9)):
            part = block[32 * (tap % 4) : 32 * (tap % 4 + 1)]
            for k in range(4):
                fmid[128 * tap + 32 * k : 128 * tap + 32 * (k + 1)] = (pltpu.roll(part, 32 * k, 1) if k else part).astype(bf16)
    for k in range(4):
        flast[32 * k : 32 * (k + 1), 128 * k : 128 * (k + 1)] = last[...]
    for k in range(2):
        fproj[128 * k : 128 * (k + 1), 128 * k : 128 * (k + 1)] = skip[...]
        narrow = at_lanes(mid_norm[k].astype(f32), 0)
        wide = jnp.concatenate([narrow] * 4, axis=0)
        fpair[:, 128 * k : 128 * (k + 1)] = sum(pltpu.roll(wide, 32 * j, 1) for j in range(1, 4))[:2] + narrow
        for j in range(4):
            fpair[:, 256 + 512 * k + 128 * j : 384 + 512 * k + 128 * j] = out_norm[k].astype(f32)
    frames = mask.shape[1]
    row = lax.broadcasted_iota(jnp.int32, (frames, frames), 0)
    column = lax.broadcasted_iota(jnp.int32, (frames, frames), 1)
    spread_ids = jnp.broadcast_to(ids[...].astype(f32), (frames, frames))
    def pick(by):
        return jnp.sum(jnp.where(column == row + by, spread_ids, 0.0), axis=1, keepdims=True)
    at = lax.broadcasted_iota(jnp.int32, (frames, 1), 0)
    here = pick(0)
    prev = jnp.where((here == pick(-1)) & (at > 0), 1.0, 0.0)
    after = jnp.where((here == pick(1)) & (at < frames - 1), 1.0, 0.0)
    mask[0] = jnp.broadcast_to(prev, mask.shape[1:])
    mask[1] = jnp.broadcast_to(after, mask.shape[1:])


def pack_norms(pairs, out):
    total, offset = None, 0
    for pair in pairs:
        v = at_lanes(jnp.concatenate([pair[...].astype(f32)] * 4, axis=0), offset)
        total = v if total is None else total + v
        offset += pair.shape[1]
    out[...] = total


def join_norms(gathered_of, shares, out):
    n = gathered_of.shape[0]
    offset, lo = 0, 0
    for share in shares:
        wide = share * n
        pick = lax.broadcasted_iota(jnp.int32, (128, wide), 0) == offset + lax.broadcasted_iota(jnp.int32, (128, wide), 1) % share
        pick = jnp.where(pick, 1.0, 0.0).astype(bf16)
        mine = lax.broadcasted_iota(jnp.int32, (n, wide), 0) == lax.broadcasted_iota(jnp.int32, (n, wide), 1) // share
        for row in range(2):
            each = dot(gathered_of[:, row, :].astype(bf16), pick)
            out[row : row + 1, lo : lo + wide] = jnp.sum(jnp.where(mine, each, 0.0), axis=0, keepdims=True)
        offset += share
        lo += wide


def body0(n, lat_shard, first_shard, p_lat, p_one, p_two, p_out, p_proj, first_t, middle_t, last_w, skip, mid_norm, out_norm, ids,
          lat_whole, first_whole, spair, band, fproj, fmid, flast, fpair, mask, own, norms_whole, lanes, *sems):
    lat, norms, first = moves(n, (lat_shard, own, first_shard), (lat_whole, norms_whole, first_whole), sems)
    pairs = (p_lat, p_one, p_two, p_out, p_proj)
    greet(n)
    pack_norms(pairs, own)
    greeted(n)
    for m in (lat, norms, first):
        m.start("z")
    build_fast(first_t, middle_t, last_w, skip, mid_norm, out_norm, ids, band, fproj, fmid, flast, fpair, mask, lanes)
    for m in (lat, norms):
        m.wait("z")
        m.start("d")
    first.wait("z")
    first.start("p", "c0")
    lat.wait("d")
    norms.wait("d")
    join_norms(norms_whole[...].reshape(n, 8, 128), [p.shape[1] for p in pairs], spair)
    first.wait("p", "c0")


def stage0(lat_shard, first_shard, pairs, fast, ids, n):
    VM, ANY = pl.BlockSpec(memory_space=pltpu.VMEM), pl.BlockSpec(memory_space=pl.ANY)
    shape_of = lambda shape, kind: jax.ShapeDtypeStruct(shape, kind)
    small = tuple(pairs) + tuple(fast) + (ids,)
    width = sum(p.shape[1] for p in pairs) * n
    return pl.pallas_call(
        functools.partial(body0, n),
        in_specs=[ANY, ANY] + [VM] * len(small),
        out_specs=[ANY, ANY] + [VM] * 7,
        out_shape=[shape_of(s, k) for s, k, _ in spread_shapes([lat_shard, first_shard], n)]
        + [shape_of((2, width), f32), shape_of((512, 384), bf16), shape_of((256, 256), bf16), shape_of((1152, 128), bf16),
           shape_of((128, 512), bf16), shape_of((2, 1280), f32), shape_of((2, ids.shape[1], 256), f32)],
        scratch_shapes=[pltpu.VMEM((8, 128), f32), pltpu.VMEM((n // 8, 2, 2, 2, 8, 128), f32), pltpu.VMEM((32, 384), f32)] + gather_scratch(3, n),
        compiler_params=pltpu.CompilerParams(collective_id=1, has_side_effects=True),
    )(lat_shard, first_shard, *small)


def run_ticks(step, n, ticks, at):
    @pl.when(step == 0)
    def _():
        greet(n)
    for j in range(3):
        @pl.when(step == at[j])
        def _(j=j):
            if j == 0:
                greeted(n)
            ticks[j]()


def strips(rows, width, body, init):
    return lax.fori_loop(0, rows // STRIP, lambda k, carry: body(pl.ds(pl.multiple_of(k * STRIP, STRIP), STRIP), carry), init, unroll=True)


FOLDS1 = ((256, 384, 32), (384, 896, 128))
FOLDS2 = ((256, 384, 32),)
FOLDS3 = ((256, 768, 128),)


def body1(n, raw, lat, band, fproj, mask, spair, fpair, held, *refs):
    shards, (fast4, lat_pre, fone_pre, n1), wholes, (wide, acc), rest = refs[:2], refs[2:6], refs[6:9], refs[9:11], refs[11:]
    step = pl.program_id(0)
    clear_first(step, acc)
    ticks, swap = (), rest
    if n > 1:
        first, *others = moves(n, (None,) + tuple(shards), wholes, rest)
        swap = rest[3 * GATHER_SEMS :]

        def begin():
            first.start("q", "c1")
            for m in others:
                m.start("z")
        def middle():
            first.wait("q")
            first.start("c2")
        def finish():
            first.wait("c1", "c2")
            for m in others:
                m.wait("z")
        ticks = (begin, middle, lambda: None, lambda: None, finish)
        run_ticks(step, n, ticks, (1, 4, 6))
    f = split_fours(raw, wide).astype(bf16)
    fast4[...] = f
    prev, nxt = mask[0], mask[1]
    z = dot_nt(f[:, :384], lat[:, 256:]) + shift(dot_nt(f[:, 256:], lat[:, :256]), prev, 1)
    lat_pre[...] = z
    add_moments(step, acc, 0, z)
    y = dot(f, band[...])
    z = y[:, :128] + shift(y[:, 128:256], prev, 1) + shift(y[:, 256:], nxt, -1)
    fone_pre[...] = z
    add_moments(step, acc, 256, z)
    z = jnp.concatenate([dot(f[:, :256], fproj[...]), dot(f[:, 256:], fproj[...])], axis=1)
    add_moments(step, acc, 384, z)
    close_moments(step, acc, ((spair, 0, 256), (fpair, 0, 128), (fpair, 768, 1280)), n1, f.shape[0] * STEPS, FOLDS1, n, ticks, *swap)


def stage1(raw, lat, band, fproj, mask, spair, fpair, held, shards_of, n):
    rows = raw.shape[0] * raw.shape[1] // 4
    return run(functools.partial(body1, n), rows,
        [(raw, "rows")] + [(v, "all") for v in (lat, band, fproj, mask, spair, fpair)] + [(v, "any") for v in (held,) + tuple(shards_of)],
        [((rows, 512), bf16, "rows"), ((rows, 256), f32, "rows"), ((rows, 128), f32, "rows"), ((4, 896), f32, "all")] + whole_shapes([held]) + spread_shapes(shards_of, n),
        [pltpu.VMEM((rows * 4 // STEPS, 128), f32), pltpu.VMEM((2, 8, 896), f32)] + (gather_scratch(3, n) if n > 1 else []), n, (2, 896), 2, {7: 4})


def body2(n, side, slow, lat_pre, fone_pre, n1, first, fmid, mask, spair, fpair, held_a, held_b, shard,
          lateral, one_pre, ftwo_pre, n2, whole_a, whole_b, whole_c, grid, acc, *rest):
    step = pl.program_id(0)
    rows = slow.shape[0]
    n_lat, n_fone = n1[:, :256], n1[:, 256:384]
    ticks, swap = (), rest
    if n > 1:
        middle, last, proj = moves(n, (None, None, shard), (whole_a, whole_b, whole_c), rest)
        swap = rest[3 * GATHER_SEMS :]

        def begin():
            middle.start("p", "c0")
            last.start("p", "c0")
            proj.start("z")
        def half():
            middle.wait("p")
            middle.start("q", "c1")
        def late():
            proj.wait("z")
            proj.start("p", "c0")
        def close():
            middle.wait("q")
            middle.start("c2")
        def finish():
            last.wait("p", "c0")
            proj.wait("p", "c0")
            middle.wait("c0", "c1", "c2")
        ticks = (begin, half, late, close, finish)
        run_ticks(step, n, ticks, (1, 3, 5))

    def put(block):
        part = fone_pre[pl.ds(pl.multiple_of(block * rows, 16), rows), :]
        fill(grid, side, silu(acted(part, n_fone)).astype(bf16), block)

    @pl.when(step == 0)
    def _():
        clear(grid)
        clear(acc)
        put(0)

    put(jnp.minimum(step + 1, STEPS - 1))
    lat = silu(acted(lat_pre[...], n_lat)).astype(bf16)
    lateral[...] = lat
    joined = jnp.concatenate([slow[...], lat], axis=1)
    z = dot(joined, first[1]) + shift(dot(joined, first[0]), mask[0], 1) + shift(dot(joined, first[2]), mask[1], -1)
    one_pre[...] = z
    add_moments(step, acc, 0, z)
    z = dot(tap_columns(grid, side, step, rows, False), fmid[...])
    ftwo_pre[...] = z
    add_moments(step, acc, 256, z)
    close_moments(step, acc, ((spair, 256, 512), (fpair, 128, 256)), n2, rows * STEPS, FOLDS2, n, ticks, *swap)


def stage2(slow, lat_pre, fone_pre, n1, first, fmid, mask, spair, fpair, held, shard, side, n):
    rows = slow.shape[0]
    frames = rows // side**2
    return run(functools.partial(body2, n, side), rows,
        [(slow, "rows"), (lat_pre, "rows")] + [(v, "all") for v in (fone_pre, n1, first, fmid, mask, spair, fpair)] + [(v, "any") for v in tuple(held) + (shard,)],
        [((rows, 256), bf16, "rows"), ((rows, 256), f32, "rows"), ((rows, 128), f32, "rows"), ((4, 384), f32, "all")] + whole_shapes(held) + spread_shapes([shard], n),
        [pltpu.VMEM(((side + 2) ** 2 * frames, 128), bf16), pltpu.VMEM((2, 8, 384), f32)] + (gather_scratch(3, n) if n > 1 else []), n, (2, 384), 3, {9: 4, 10: 5})


def body3(n, side, one_pre, ftwo_pre, n2, middle, flast, spair, fpair, held_a, held_b, two_pre, ftwo, n3, whole_a, whole_b, grid, acc, *rest):
    step = pl.program_id(0)
    rows = two_pre.shape[0]
    n_one, n_ftwo = n2[:, :256], n2[:, 256:]
    ticks, swap = (), rest
    if n > 1:
        both = moves(n, (None, None), (whole_a, whole_b), rest)
        swap = rest[2 * GATHER_SEMS :]

        def begin():
            for m in both:
                m.start("q", "c1")
        def half():
            for m in both:
                m.wait("q")
                m.start("c2")
        def finish():
            for m in both:
                m.wait("c1", "c2")
        ticks = (begin, half, lambda: None, lambda: None, finish)
        run_ticks(step, n, ticks, (1, 5, 6))

    def put(block):
        part = one_pre[pl.ds(pl.multiple_of(block * rows, 16), rows), :]
        fill(grid, side, silu(acted(part, n_one)).astype(bf16), block)

    @pl.when(step == 0)
    def _():
        clear(grid)
        clear(acc)
        put(0)

    put(jnp.minimum(step + 1, STEPS - 1))
    z = dot(tap_columns(grid, side, step, rows, False), middle[...])
    two_pre[...] = z
    add_moments(step, acc, 0, z)
    f = silu(acted(ftwo_pre[...], n_ftwo)).astype(bf16)
    ftwo[...] = f
    for k in range(2):
        add_moments(step, acc, 256 * (k + 1), dot(f, flast[:, 256 * k : 256 * (k + 1)]))
    close_moments(step, acc, ((spair, 512, 768), (fpair, 256, 768)), n3, rows * STEPS, FOLDS3, n, ticks, *swap)


def stage3(one_pre, ftwo_pre, n2, middle, flast, spair, fpair, held, side, n):
    rows = one_pre.shape[0]
    frames = rows // side**2
    return run(functools.partial(body3, n, side), rows,
        [(one_pre, "all"), (ftwo_pre, "rows")] + [(v, "all") for v in (n2, middle, flast, spair, fpair)] + [(v, "any") for v in held],
        [((rows, 256), f32, "rows"), ((rows, 128), bf16, "rows"), ((4, 768), f32, "all")] + whole_shapes(held),
        [pltpu.VMEM(((side + 2) ** 2 * frames, 256), bf16), pltpu.VMEM((2, 8, 768), f32)] + (gather_scratch(2, n) if n > 1 else []), n, (2, 768), 4, {7: 3, 8: 4})


def body4(n, two_pre, slow, lateral, n3, last, proj, spair, two, proj_pre, n4, acc, *swap):
    step = pl.program_id(0)
    clear_first(step, acc)
    v = silu(acted(two_pre[...], n3[:, :256])).astype(bf16)
    two[...] = v
    for k in range(4):
        add_moments(step, acc, 256 * k, dot(v, last[:, 256 * k : 256 * (k + 1)]))
    joined = jnp.concatenate([slow[...], lateral[...]], axis=1)
    for k in range(4):
        z = dot(joined, proj[:, 256 * k : 256 * (k + 1)])
        proj_pre[:, 256 * k : 256 * (k + 1)] = z.astype(proj_pre.dtype)
        add_moments(step, acc, 1024 + 256 * k, z)
    if n > 1:
        @pl.when(step == 0)
        def _():
            greet(n)
    close_moments(step, acc, ((spair, 768, 2816),), n4, v.shape[0] * STEPS, (), n,
        (None, None, None, lambda: greeted(n), lambda: None), *swap)


def stage4(two_pre, slow, lateral, n3, last, proj, spair, n):
    rows = two_pre.shape[0]
    return run(functools.partial(body4, n), rows,
        [(v, "rows") for v in (two_pre, slow, lateral)] + [(v, "all") for v in (n3, last, proj, spair)],
        [((rows, 256), bf16, "rows"), ((rows, 1024), f32, "rows"), ((4, 2048), f32, "all")], [pltpu.VMEM((2, 8, 2048), f32)], n, (2, 2048), 5)


def body5(two, proj_pre, cot, fast4, ftwo, fcot, n1, n3, n4, last, fproj, flast,
          slow_out, fast_out, delta, fdelta, sums, wide, three, fthree, fskip, fgrad, fout, acc):
    step = pl.program_id(0)
    rows = two.shape[0]
    clear_first(step, acc)
    fgrad[...] = split_fours(fcot, wide)
    three[...] = dot(two[...], last[...])
    fthree[...] = dot(ftwo[...], flast[...])
    for k in range(2):
        fskip[:, 256 * k : 256 * (k + 1)] = dot(fast4[:, 256 * k : 256 * (k + 1)], fproj[...])

    def side_of(za, zb, grad, na, nb, out, keep, lo, lanes):
        ga, gb, base = 0.5 * na[1:2] * na[2:3], 0.5 * nb[1:2] * nb[2:3], 0.5 * (na[3:4] + nb[3:4])
        ma, mb = na[0:1], nb[0:1]
        def one(at, carry):
            ha = za[at, lanes].astype(f32) - ma
            hb = zb[at, lanes].astype(f32) - mb
            h = ha * ga + hb * gb + base
            th = jnp.tanh(h)
            u = 1.0 + th
            out[at, lanes] = (h * u).astype(out.dtype)
            d = (0.5 * grad[at, lanes].astype(f32)) * (u * (1.0 + h * (1.0 - th)))
            keep[at, lanes] = d
            return carry[0] + eighth(d), carry[1] + eighth(d * ha), carry[2] + eighth(d * hb)
        zero = jnp.zeros((8, 256), f32)
        add_sums(step, acc, lo, strips(rows, 256, one, (zero, zero, zero)))

    for k in range(4):
        lanes = slice(256 * k, 256 * (k + 1))
        side_of(three, proj_pre, cot, n4[:, lanes], n4[:, 1024 + 256 * k : 1280 + 256 * k], slow_out, delta, 256 * k, lanes)
    for k in range(2):
        lanes = slice(256 * k, 256 * (k + 1))
        side_of(fthree, fskip, fgrad, n3[:, 256 + 256 * k : 512 + 256 * k], n1[:, 384 + 256 * k : 640 + 256 * k], fout, fdelta, 1024 + 256 * k, lanes)
    join_fours(fout[...], wide, fast_out)

    @pl.when(step == STEPS - 1)
    def _():
        scales = (1.0, jnp.concatenate([n4[1:2, :1024], n3[1:2, 256:]], axis=1), jnp.concatenate([n4[1:2, 1024:], n1[1:2, 384:]], axis=1))
        for k in range(3):
            sums[k : k + 1] = jnp.sum(acc[k], axis=0, keepdims=True) * scales[k]


def stage5(two, proj_pre, cot, fast4, ftwo, fcot, n1, n3, n4, last, fproj, flast):
    rows = two.shape[0]
    part = rows // STEPS
    return run(body5, rows,
        [(two, "rows"), (proj_pre, "rows"), (cot, "rows"), (fast4, "rows"), (ftwo, "rows"), (fcot, "rows"),
         (n1, "all"), (n3, "all"), (n4, "all"), (last, "all"), (fproj, "all"), (flast, "all")],
        [((rows, 1024), bf16, "rows"), (fcot.shape, bf16, "rows"), ((rows, 1024), f32, "rows"), ((rows, 512), f32, "rows"), ((3, 1536), f32, "all")],
        [pltpu.VMEM((part * 4, 128), f32), pltpu.VMEM((part, 1024), f32), pltpu.VMEM((part, 512), f32), pltpu.VMEM((part, 512), f32),
         pltpu.VMEM((part, 512), f32), pltpu.VMEM((part, 512), f32), pltpu.VMEM((3, 8, 1536), f32)])


def body5x(n, own, out, *links):
    greet(n)
    greeted(n)
    sum_pack(total_of(n, False, own, *links), out, ((1024, 1536, 128),))


def stage5x(sums, n):
    return pl.pallas_call(
        functools.partial(body5x, n),
        in_specs=[pl.BlockSpec(memory_space=pltpu.VMEM)],
        out_specs=pl.BlockSpec(memory_space=pltpu.VMEM),
        out_shape=jax.ShapeDtypeStruct(sums.shape, f32),
        scratch_shapes=swap_scratch(sums.shape, n),
        compiler_params=pltpu.CompilerParams(collective_id=6, has_side_effects=True),
    )(sums)


def body6(n, total, two, two_pre, proj_pre, slow, lateral, delta, fast4, ftwo, ftwo_pre, fdelta, n1, n2, n3, n4, s5, last, fproj, flast,
          d_proj, d_fproj, last_term, proj_term, flast_term, e_two, e_ftwo, sums,
          three, fthree, fskip, d_three, d_fthree, acc, last_acc, proj_acc, *swap):
    step = pl.program_id(0)
    rows = two.shape[0]
    clear_first(step, acc, last_acc, proj_acc, flast_term)
    three[...] = dot(two[...], last[...])
    fthree[...] = dot(ftwo[...], flast[...])
    for k in range(2):
        fskip[:, 256 * k : 256 * (k + 1)] = dot(fast4[:, 256 * k : 256 * (k + 1)], fproj[...])

    def side_of(za, zb, e, na, nb, s, da, db, lanes):
        pa, pb = na[2:3] * na[1:2], nb[2:3] * nb[1:2]
        qa, qb = pa * na[1:2] * s[1:2], pb * nb[1:2] * s[2:3]
        ma, mb, base = na[0:1], nb[0:1], s[0:1]
        def one(at, carry):
            d = e[at, lanes] - base
            da[at, lanes] = (d * pa - (za[at, lanes].astype(f32) - ma) * qa).astype(bf16)
            db[at, lanes] = (d * pb - (zb[at, lanes].astype(f32) - mb) * qb).astype(bf16)
            return carry
        strips(rows, 256, one, 0)

    for k in range(4):
        lanes = slice(256 * k, 256 * (k + 1))
        side_of(three, proj_pre, delta, n4[:, lanes], n4[:, 1024 + 256 * k : 1280 + 256 * k], s5[:, lanes] * (1.0 / total), d_three, d_proj, lanes)
    for k in range(2):
        lanes = slice(256 * k, 256 * (k + 1))
        side_of(fthree, fskip, fdelta, n3[:, 256 + 256 * k : 512 + 256 * k], n1[:, 384 + 256 * k : 640 + 256 * k],
                s5[:, 1024 + 256 * k : 1280 + 256 * k] * (0.25 / total), d_fthree, d_fproj, lanes)

    wide = slow.shape[1]
    last_acc[...] += dot_tn(two[...], d_three[...])
    proj_acc[:wide] += dot_tn(slow[...], d_proj[...])
    proj_acc[wide:] += dot_tn(lateral[...], d_proj[...])
    flast_term[...] += dot_tn(ftwo[...], d_fthree[...])
    h = normed(two_pre[...], n3[:, :256])
    e = dot_nt(d_three[...], last[...]) * slope(scaled(h, n3[:, :256]))
    e_two[...] = e
    add_sums(step, acc, 0, (eighth(e), eighth(e * h)))
    h = normed(ftwo_pre[...], n2[:, 256:])
    e = dot_nt(d_fthree[...], flast[...]) * slope(scaled(h, n2[:, 256:]))
    e_ftwo[...] = e
    add_sums(step, acc, 256, (eighth(e), eighth(e * h)))
    close_sums(step, acc, sums, ((256, 384, 32),), n, (), *swap)

    @pl.when(step == STEPS - 1)
    def _():
        last_term[...] = last_acc[...].astype(bf16)
        proj_term[...] = proj_acc[...].astype(bf16)


def stage6(total, two, two_pre, proj_pre, slow, lateral, delta, fast4, ftwo, ftwo_pre, fdelta, n1, n2, n3, n4, s5, last, fproj, flast, n):
    rows = two.shape[0]
    part = rows // STEPS
    return run(functools.partial(body6, n, total), rows,
        [(a, "rows") for a in (two, two_pre, proj_pre, slow, lateral, delta, fast4, ftwo, ftwo_pre, fdelta)]
        + [(a, "all") for a in (n1, n2, n3, n4, s5, last, fproj, flast)],
        [((rows, 1024), bf16, "rows"), ((rows, 512), bf16, "rows"), ((256, 1024), bf16, "all"), ((1280, 1024), bf16, "all"), ((128, 512), f32, "all"),
         ((rows, 256), f32, "rows"), ((rows, 128), f32, "rows"), ((2, 384), f32, "all")],
        [pltpu.VMEM((part, 1024), f32), pltpu.VMEM((part, 512), f32), pltpu.VMEM((part, 512), f32),
         pltpu.VMEM((part, 1024), bf16), pltpu.VMEM((part, 512), bf16), pltpu.VMEM((2, 8, 384), f32),
         pltpu.VMEM((256, 1024), f32), pltpu.VMEM((1280, 1024), f32)], n, (2, 384), 7)


def body7(n, side, total, one_pre, two_pre, e_two, fone_pre, ftwo_pre, e_ftwo, n1, n2, n3, s6, middle, fmid, proj_term,
          middleerm, fmid_term, e_one, e_fone, sums, proj_grad, grid, fgrid, acc, mid_acc, *rest):
    step = pl.program_id(0)
    ticks, swap = (), rest
    if n > 1:
        ticks = scatter_ticks(n, (proj_term,), (proj_grad,), rest[:11])
        swap = rest[11:]
        run_ticks(step, n, ticks, (1, 3, 5))
    rows = one_pre.shape[0]

    def put(block):
        at = pl.ds(pl.multiple_of(block * rows, 16), rows)
        p, s = n3[:, :256], s6[:, :256] * (1.0 / total)
        fill(grid, side, input_grad(e_two[at, :], normed(two_pre[at, :], p), p, s[0:1], s[1:2]), block)
        p, s = n2[:, 256:], s6[:, 256:] * (0.25 / total)
        fill(fgrid, side, input_grad(e_ftwo[at, :], normed(ftwo_pre[at, :], p), p, s[0:1], s[1:2]), block)

    @pl.when(step == 0)
    def _():
        clear(grid)
        clear(fgrid)
        clear(acc)
        put(0)
        mid_acc[...] = jnp.zeros_like(mid_acc)
        fmid_term[...] = jnp.zeros_like(fmid_term)

    put(jnp.minimum(step + 1, STEPS - 1))

    def one_side(pre, p, columns, weight, lo, term, e_out):
        h = normed(pre[...], p)
        act = scaled(h, p)
        s = sigma(act)
        mid = act * s
        term[...] += dot_tn(mid.astype(bf16), columns)
        width = weight.shape[1]
        turned = jnp.concatenate([weight[width * k : width * (k + 1)] for k in range(9)], axis=1)
        e = dot_nt(columns, turned) * (s + mid * (1.0 - s))
        e_out[...] = e
        add_sums(step, acc, lo, (eighth(e), eighth(e * h)))

    one_side(one_pre, n2[:, :256], tap_columns(grid, side, step, rows, True), middle, 0, mid_acc, e_one)
    one_side(fone_pre, n1[:, 256:384], tap_columns(fgrid, side, step, rows, True), fmid, 256, fmid_term, e_fone)
    close_sums(step, acc, sums, ((256, 384, 32),), n, ticks, *swap)

    @pl.when(step == STEPS - 1)
    def _():
        for k in range(9):
            middleerm[k] = mid_acc[:, 256 * k : 256 * (k + 1)].astype(bf16)


def stage7(total, one_pre, two_pre, e_two, fone_pre, ftwo_pre, e_ftwo, n1, n2, n3, s6, middle, fmid, proj_term, side, n):
    terms = [six(v, n) for v in (proj_term,)] if n > 1 else [proj_term]
    parts = [(v.shape[0] // n, v.shape[1]) for v in (proj_term,)]
    rows = one_pre.shape[0]
    frames = rows // side**2
    return run(functools.partial(body7, n, side, total), rows,
        [(one_pre, "rows"), (two_pre, "all"), (e_two, "all"), (fone_pre, "rows"), (ftwo_pre, "all"), (e_ftwo, "all")]
        + [(a, "all") for a in (n1, n2, n3, s6, middle, fmid)] + [(v, "any") for v in terms],
        [((9, 256, 256), bf16, "all"), ((128, 1152), f32, "all"), ((rows, 256), f32, "rows"), ((rows, 128), f32, "rows"), ((2, 384), f32, "all")] + [(part, f32, "all") for part in parts],
        [pltpu.VMEM(((side + 2) ** 2 * frames, 256), bf16), pltpu.VMEM(((side + 2) ** 2 * frames, 128), bf16),
         pltpu.VMEM((2, 8, 384), f32), pltpu.VMEM((256, 2304), f32)] + (scatter_scratch(parts, n) if n > 1 else []), n, (2, 384), 8)


def body8(n, total, slow, lateral, one_pre, e_one, n2, s7, mask, middleerm, first_term, pieces, middle_grad, first_acc, *rest):
    step = pl.program_id(0)
    if n > 1:
        ticks = scatter_ticks(n, (middleerm,), (middle_grad,), rest)
        run_ticks(step, n, ticks, (1, 2, 4))

        @pl.when(step == STEPS - 1)
        def _():
            ticks[3]()
    clear_first(step, first_acc)
    p, s = n2[:, :256], s7[:, :256] * (1.0 / total)
    d = input_grad(e_one[...], normed(one_pre[...], p), p, s[0:1], s[1:2])
    w = d.astype(f32)
    rows = w.shape[0]
    before = pltpu.roll(masked(w, mask[0]), rows - 1, 0).astype(bf16)
    after = pltpu.roll(masked(w, mask[1]), 1, 0).astype(bf16)
    columns = jnp.concatenate([before, d, after], axis=1)
    pieces[...] = columns
    wide = slow.shape[1]
    first_acc[:wide] += dot_tn(slow[...], columns)
    first_acc[wide:] += dot_tn(lateral[...], columns)

    @pl.when(step == STEPS - 1)
    def _():
        for k in range(3):
            first_term[k] = first_acc[:, 256 * k : 256 * (k + 1)].astype(bf16)
        if n > 1:
            ticks[4]()


def stage8(total, slow, lateral, one_pre, e_one, n2, s7, mask, middleerm, n):
    rows = slow.shape[0]
    part = (middleerm.shape[0] // n, middleerm.shape[1])
    return run(functools.partial(body8, n, total), rows,
        [(a, "rows") for a in (slow, lateral, one_pre, e_one)] + [(a, "all") for a in (n2, s7, mask)]
        + [(six(middleerm, n) if n > 1 else middleerm, "any")],
        [((3, 1280, 256), bf16, "all"), ((rows, 768), bf16, "rows"), (part, f32, "all")],
        [pltpu.VMEM((1280, 768), f32)] + (scatter_scratch([part], n) if n > 1 else []), n, None, 12)


def body8b(n, pieces, d_proj, lat_pre, n1, first, proj, last_term, first_term,
           slow_grad, e_lat, sums, last_grad, first_grad, acc, *rest):
    step = pl.program_id(0)
    ticks, swap = (), rest
    if n > 1:
        ticks = scatter_ticks(n, (last_term, first_term), (last_grad, first_grad), rest[:16])
        swap = rest[16:]
        run_ticks(step, n, ticks, (1, 3, 5))
    clear_first(step, acc)
    wide = proj.shape[0] - 256

    def back(lo, hi):
        part = dot_nt(d_proj[...], proj[lo:hi])
        for k in range(3):
            part += dot_nt(pieces[:, 256 * k : 256 * (k + 1)], first[k, lo:hi])
        return part

    for k in range(4):
        slow_grad[:, 256 * k : 256 * (k + 1)] = back(256 * k, 256 * (k + 1)).astype(bf16)
    h = normed(lat_pre[...], n1[:, :256])
    e = back(wide, wide + 256) * slope(scaled(h, n1[:, :256]))
    e_lat[...] = e
    add_sums(step, acc, 0, (eighth(e), eighth(e * h)))
    close_sums(step, acc, sums, (), n, ticks, *swap)


def stage8b(pieces, d_proj, lat_pre, n1, first, proj, last_term, first_term, n):
    rows = pieces.shape[0]
    terms = [six(v, n) if n > 1 else v for v in (last_term, first_term)]
    parts = [(v.shape[0] // n, v.shape[1]) for v in (last_term, first_term)]
    return run(functools.partial(body8b, n), rows,
        [(a, "rows") for a in (pieces, d_proj, lat_pre)] + [(a, "all") for a in (n1, first, proj)] + [(v, "any") for v in terms],
        [((rows, 1024), bf16, "rows"), ((rows, 256), f32, "rows"), ((2, 256), f32, "all")] + [(part, f32, "all") for part in parts],
        [pltpu.VMEM((2, 8, 256), f32)] + (scatter_scratch(parts, n) if n > 1 else []), n, (2, 256), 9)


def lanes_at(v, source, target):
    moved = pltpu.roll(v, (target - source) % 128, 1) if target != source else v
    lane = lax.broadcasted_iota(jnp.int32, v.shape, 1)
    return jnp.where((lane >= target) & (lane < target + 32), moved, 0.0)


def pack_fast(out, band, fproj, flast, fmid):
    places_of = (
        ((0, 0, 1), (0, 1, 2), (0, 2, 3), (1, 3, 0)),
        ((0, 0, 0), (0, 1, 1), (0, 2, 2), (0, 3, 3)),
        ((0, 1, 0), (0, 2, 1), (0, 3, 2), (2, 0, 3)),
    )
    for tap in range(3):
        out[32 * tap : 32 * (tap + 1)] = sum(
            band[128 * part + 32 * j : 128 * part + 32 * (j + 1), 128 * k : 128 * (k + 1)] for part, k, j in places_of[tap])
    out[96:224] = fproj[...]
    out[224:256] = sum(flast[32 * k : 32 * (k + 1), 128 * k : 128 * (k + 1)] for k in range(4))
    for group in range(3):
        total = None
        for tap in range(4 * group, min(4 * group + 4, 9)):
            for k in range(4):
                turned = fmid[:, 128 * tap : 128 * (tap + 1)].T
                v = lanes_at(turned[32 * k : 32 * (k + 1)], 32 * k, 32 * (tap % 4))
                total = v if total is None else total + v
        out[256 + 32 * group : 288 + 32 * group] = total
    out[352:384] = jnp.zeros((32, 128), f32)


def own_pair(out, sums, lo, hi, row):
    share = out.shape[1]
    back = lax.rem(hi - lo - lax.axis_index("fsdp") * share, hi - lo)
    for at, k in enumerate((row, 0)):
        wide = jnp.broadcast_to(sums[k : k + 1, lo:hi], (8, hi - lo))
        out[at : at + 1] = pltpu.roll(wide, back, 1)[0:1, :share]


def body9(n, total, fast4, lat_pre, e_lat, fone_pre, e_fone, d_fproj, ready, n1, s5, s6, s7, s8, lat, band, fproj, mask, flast_term, fmid_term,
          ready_first, ready_middle, ready_last, ready_proj, lat_term, packed, raw, slow_grad, lat_n, one_n, two_n, out_n, proj_n, mid_n, fout_n,
          first_grad, middle_grad, last_grad, proj_grad, wide, lat_acc, whole, band_term, fproj_term):
    step = pl.program_id(0)
    clear_first(step, lat_acc, band_term, fproj_term)
    slow_grad[...] = ready[...]
    rows = fast4.shape[0]
    def backward(e, pre, p, s):
        d = input_grad(e[...], normed(pre[...], p), p, s[0:1], s[1:2])
        w = d.astype(f32)
        return d, pltpu.roll(masked(w, mask[0]), rows - 1, 0).astype(bf16), pltpu.roll(masked(w, mask[1]), 1, 0).astype(bf16)
    d, before, _ = backward(e_lat, lat_pre, n1[:, :256], s8[...] * (1.0 / total))
    f, fbefore, fafter = backward(e_fone, fone_pre, n1[:, 256:384], s7[:, 256:] * (0.25 / total))
    narrow = jnp.concatenate([f, fbefore, fafter], axis=1)
    lat_acc[:, :256] += dot_tn(before, fast4[:, 256:])
    lat_acc[:, 256:] += dot_tn(d, fast4[:, :384])
    band_term[...] += dot_tn(narrow, fast4[...])
    for k in range(4):
        fproj_term[...] += dot_tn(fast4[:, 128 * k : 128 * (k + 1)], d_fproj[:, 128 * k : 128 * (k + 1)])
    base = dot_nt(narrow, band[...])
    skip = jnp.concatenate([dot_nt(d_fproj[:, 256 * k : 256 * (k + 1)], fproj[...]) for k in range(2)], axis=1)
    whole[...] = base + skip
    whole[:, :384] += dot(d, lat[:, 256:])
    whole[:, 256:] += dot(before, lat[:, :256])
    join_fours(whole[...], wide, raw)

    @pl.when(step == STEPS - 1)
    def _():
        lat_term[...] = lat_acc[...].astype(bf16)
        for grad, found in ((first_grad, ready_first), (middle_grad, ready_middle), (last_grad, ready_last), (proj_grad, ready_proj)):
            grad[...] = found[...]
        pack_fast(packed, band_term, fproj_term, flast_term, fmid_term)
        if n > 1:
            own_pair(lat_n, s8, 0, 256, 1)
            own_pair(one_n, s7, 0, 256, 1)
            own_pair(two_n, s6, 0, 256, 1)
            own_pair(out_n, s5, 0, 1024, 1)
            own_pair(proj_n, s5, 0, 1024, 2)
        for j, (sums, lo, row) in enumerate(((s7, 256, 1), (s6, 256, 1))):
            mid_n[j, 0:1] = sums[row : row + 1, lo : lo + 32]
            mid_n[j, 1:2] = sums[0:1, lo : lo + 32]
        for j in range(2):
            fout_n[j, 0:1] = s5[j + 1 : j + 2, 1024:1152]
            fout_n[j, 1:2] = s5[0:1, 1024:1152]


def stage9(total, fast4, lat_pre, e_lat, fone_pre, e_fone, d_fproj, ready, n1, s5, s6, s7, s8, lat, band, fproj, mask, flast_term, fmid_term, grads, n):
    rows = fast4.shape[0]
    part = rows // STEPS
    return run(functools.partial(body9, n, total), rows,
        [(a, "rows") for a in (fast4, lat_pre, e_lat, fone_pre, e_fone, d_fproj, ready)]
        + [(a, "all") for a in (n1, s5, s6, s7, s8, lat, band, fproj, mask, flast_term, fmid_term) + tuple(grads)],
        [((256, 640), bf16, "all"), ((384, 128), f32, "all"), ((rows // 16, 64, 128), bf16, "rows"), (ready.shape, bf16, "rows")]
        + [((2, 256 // n), f32, "all")] * 3 + [((2, 1024 // n), f32, "all")] * 2 + [((2, 2, 32), f32, "all"), ((2, 2, 128), f32, "all")] + [(v.shape, f32, "all") for v in grads],
        [pltpu.VMEM((part * 4, 128), f32), pltpu.VMEM((256, 640), f32), pltpu.VMEM((part, 512), f32),
         pltpu.VMEM((384, 512), f32), pltpu.VMEM((128, 128), f32)])


def body10(n, lat_term, packed, lat_grad, first_t, middle_t, last, proj, sums, slots, line, mine, lat_slots, lat_line, lat_mine,
           a_send, a_recv, b_send, b_recv, g_send, g_recv, l_send, l_recv, m_send, m_recv):
    me = lax.axis_index("fsdp")
    mi, mo, depth = lax.rem(me, INNER), lax.div(me, INNER), n // INNER
    peers = [mo * INNER + lax.rem(mi + k, INNER) for k in range(INNER)]
    spots = [lax.rem(mi + k, INNER) for k in range(INNER)]
    beyond = [lax.rem(mo + k, depth) for k in range(depth)]

    def remote(src, dst, send, recv, peer):
        copy = pltpu.make_async_remote_copy(
            src_ref=src, dst_ref=dst, send_sem=send, recv_sem=recv, device_id=(peer,), device_id_type=MESH)
        copy.start()
        return copy

    greet(n)
    greeted(n)
    fast = [remote(packed.at[spots[k]], slots.at[mi], a_send.at[k], a_recv.at[k], peers[k]) for k in range(1, INNER)]
    slow = [remote(lat_term.at[:, spots[k]], lat_slots.at[mi], l_send.at[k], l_recv.at[k], peers[k]) for k in range(1, INNER)]
    slots[mi] = packed[mi]
    lat_slots[mi] = lat_term[:, mi]
    for copy in fast:
        copy.wait()
    mine[...] = sum(slots[k] for k in range(1, INNER)) + slots[0]
    fast = [remote(mine, line.at[mo], b_send.at[k], b_recv.at[k], beyond[k] * INNER + mi) for k in range(1, depth)]
    line[mo] = mine[...]
    for copy in slow:
        copy.wait()
    lat_mine[...] = sum(lat_slots[k].astype(f32) for k in range(INNER)).astype(bf16)
    slow = [remote(lat_mine.at[beyond[k]], lat_line.at[mo], m_send.at[k], m_recv.at[k], beyond[k] * INNER + mi) for k in range(1, depth)]
    lat_line[mo] = lat_mine[mo]
    for copy in fast:
        copy.wait()
    sums[mi] = sum((line[k] for k in range(1, depth)), line[0])
    fast = [remote(sums.at[mi], sums.at[mi], g_send.at[k], g_recv.at[k], peers[k]) for k in range(1, INNER)]
    for copy in slow:
        copy.wait()
    lat_grad[...] = sum(lat_line[k].astype(f32) for k in range(depth))
    for copy in fast:
        copy.wait()

    high = sums.shape[1]
    def rows_of(lo, hi):
        found = []
        while lo < hi:
            top = min(hi, (lo // high + 1) * high)
            found.append(sums[lo // high, lo % high : lo % high + top - lo])
            lo = top
        return jnp.concatenate(found, axis=0) if len(found) > 1 else found[0]

    for k in range(3):
        first_t[:, 128 * k : 128 * (k + 1)] = rows_of(32 * k, 32 * (k + 1))
        wide = min(128, 288 - 128 * k)
        middle_t[:, 128 * k : 128 * k + wide] = rows_of(256 + 32 * k, 288 + 32 * k)[:, :wide]
    proj[...] = rows_of(96, 224)
    last[...] = rows_of(224, 256)


def stage10(lat_term, packed, n):
    depth, DS = n // INNER, pltpu.SemaphoreType.DMA
    packed = packed.reshape(INNER, -1, 128)
    chunk = packed.shape[1:]
    share = (lat_term.shape[0] // n, lat_term.shape[1])
    lat_grad, first_t, middle_t, last, proj = pl.pallas_call(
        functools.partial(body10, n),
        in_specs=[pl.BlockSpec(memory_space=pltpu.VMEM)] * 2,
        out_specs=[pl.BlockSpec(memory_space=pltpu.VMEM)] * 5,
        out_shape=[jax.ShapeDtypeStruct(shape, f32) for shape in (share, (32, 384), (32, 288), (32, 128), (128, 128))],
        scratch_shapes=[pltpu.VMEM((INNER,) + chunk, f32), pltpu.VMEM((INNER,) + chunk, f32), pltpu.VMEM((depth,) + chunk, f32), pltpu.VMEM(chunk, f32),
            pltpu.VMEM((INNER, depth) + share, bf16), pltpu.VMEM((depth,) + share, bf16), pltpu.VMEM((depth,) + share, bf16)]
        + [DS((INNER,)), DS((INNER,)), DS((depth,)), DS((depth,)), DS((INNER,)), DS((INNER,)), DS((INNER,)), DS((INNER,)), DS((depth,)), DS((depth,))],
        compiler_params=pltpu.CompilerParams(collective_id=10, has_side_effects=True),
    )(lat_term.reshape((depth, INNER) + share), packed)
    lat_grad, first_t, middle_t, last, proj = stage11((lat_grad, first_t, middle_t, last, proj))
    return lat_grad, (first_t.T, middle_t.T, last, proj)


def body11(*refs):
    half = len(refs) // 2
    for source, target in zip(refs[:half], refs[half:]):
        target[...] = source[...]


def stage11(arrays):
    VM = pl.BlockSpec(memory_space=pltpu.VMEM)
    return pl.pallas_call(
        body11,
        in_specs=[VM] * len(arrays),
        out_specs=[VM] * len(arrays),
        out_shape=[jax.ShapeDtypeStruct(v.shape, v.dtype) for v in arrays],
    )(*arrays)


def shards(slow_in, fast_in, clip_ids, lateral_weight, first_weight, middle_weight, last_weight, proj_weight,
           lat_norm, one_norm, two_norm, out_norm, proj_norm, fast_first, fast_middle, fast_last, fast_proj,
           fast_mid_norm, fast_out_norm, slow_cot, fast_cot):
    n = lax.axis_size("fsdp")
    side = slow_in.shape[1]
    count = slow_in.shape[0] * side * side * n
    lat, first, spair, band, fproj, fmid, flast, fpair, mask = stage0(
        lateral_weight.T, first_weight, (lat_norm, one_norm, two_norm, out_norm, proj_norm),
        (fast_first.T, fast_middle.T, fast_last, fast_proj, fast_mid_norm, fast_out_norm), clip_ids, n)
    lat = gathered(lat, n)

    def rows(v):
        return v.transpose(1, 2, 0, 3).reshape(-1, v.shape[3])
    def unrows(v):
        return v.reshape(side, side, -1, v.shape[1]).transpose(2, 0, 1, 3)
    def raw(v):
        return v.transpose(1, 2, 0, 3).reshape(side * side, -1, v.shape[3])
    def unraw(v):
        return v.reshape((side, side) + v.shape[1:]).transpose(2, 0, 1, 3)

    slow = rows(slow_in)
    fast4, lat_pre, fone_pre, n1, first, *held = stage1(
        raw(fast_in), lat, band, fproj, mask, spair, fpair, first, (middle_weight, last_weight), n)
    first = gathered(first, n).reshape(3, -1, first_weight.shape[1])
    lateral, one_pre, ftwo_pre, n2, middle, last, proj = stage2(
        slow, lat_pre, fone_pre, n1, first, fmid, mask, spair, fpair, held, proj_weight, side, n)
    middle = gathered(middle, n)
    two_pre, ftwo, n3, last, proj = stage3(one_pre, ftwo_pre, n2, middle, flast, spair, fpair, (last, proj), side, n)
    last, proj = gathered(last, n), gathered(proj, n)
    two, proj_pre, n4 = stage4(two_pre, slow, lateral, n3, last, proj, spair, n)
    slow_out, fast_out, delta, fdelta, local = stage5(
        two, proj_pre, rows(slow_cot), fast4, ftwo, raw(fast_cot), n1, n3, n4, last, fproj, flast)
    s5 = stage5x(local, n)
    d_proj, d_fproj, last_term, proj_term, flast_term, e_two, e_ftwo, s6 = stage6(
        count, two, two_pre, proj_pre, slow, lateral, delta, fast4, ftwo, ftwo_pre, fdelta, n1, n2, n3, n4, s5, last, fproj, flast, n)
    middle_term, fmid_term, e_one, e_fone, s7, proj_grad = stage7(
        count, one_pre, two_pre, e_two, fone_pre, ftwo_pre, e_ftwo, n1, n2, n3, s6, middle, fmid, proj_term, side, n)
    first_term, pieces, middle_grad = stage8(count, slow, lateral, one_pre, e_one, n2, s7, mask, middle_term.reshape(-1, 256), n)
    slow_grad, e_lat, s8, last_grad, first_grad = stage8b(
        pieces, d_proj, lat_pre, n1, first, proj, last_term, first_term.reshape(-1, 256), n)
    lat_term, packed, fast_grad, slow_grad, *small = stage9(
        count, fast4, lat_pre, e_lat, fone_pre, e_fone, d_fproj, slow_grad, n1, s5, s6, s7, s8, lat, band, fproj, mask, flast_term, fmid_term,
        (first_grad, middle_grad, last_grad, proj_grad), n)
    lateral_grad, fast_grads = stage10(lat_term, packed, n)
    return (unrows(slow_out), unraw(fast_out), unrows(slow_grad), unraw(fast_grad),
            lateral_grad.T, *small[7:],
            *small[:5], *fast_grads, *small[5:7])


def solution(mesh):
    in_specs = (
        P("fsdp", None, None, None),
        P("fsdp", None, None, None),
        P("fsdp", None),
        P(None, "fsdp"),
        P("fsdp", None),
        P("fsdp", None),
        P("fsdp", None),
        P("fsdp", None),
        P(None, "fsdp"),
        P(None, "fsdp"),
        P(None, "fsdp"),
        P(None, "fsdp"),
        P(None, "fsdp"),
        P(),
        P(),
        P(),
        P(),
        P(),
        P(),
        P("fsdp", None, None, None),
        P("fsdp", None, None, None),
    )
    out_specs = (
        P("fsdp", None, None, None),
        P("fsdp", None, None, None),
        P("fsdp", None, None, None),
        P("fsdp", None, None, None),
        P(None, "fsdp"),
        P("fsdp", None),
        P("fsdp", None),
        P("fsdp", None),
        P("fsdp", None),
        P(None, "fsdp"),
        P(None, "fsdp"),
        P(None, "fsdp"),
        P(None, "fsdp"),
        P(None, "fsdp"),
        P(),
        P(),
        P(),
        P(),
        P(),
        P(),
    )
    return jax.shard_map(shards, mesh=mesh, in_specs=in_specs, out_specs=out_specs, check_vma=False)
```

```python
import functools

import jax
import jax.numpy as jnp
import numpy as np
from jax import lax
from jax.experimental import pallas as pl
from jax.experimental.pallas import tpu as pltpu
from jax.sharding import PartitionSpec as P

EPSILON = 1e-05


MESH = pl.DeviceIdType.MESH


f32 = jnp.float32
bf16 = jnp.bfloat16
STEPS = 7
STRIP = 32


def dot(a, b):
    return lax.dot_general(a, b, (((1,), (0,)), ((), ())), preferred_element_type=f32)


def dot_nt(a, b):
    return lax.dot_general(a, b, (((1,), (1,)), ((), ())), preferred_element_type=f32)


def dot_tn(a, b):
    return lax.dot_general(a, b, (((0,), (0,)), ((), ())), preferred_element_type=f32)


def shift(v, mask, by):
    rows = v.shape[0]
    moved = pltpu.roll(v, by % rows, 0)
    return masked(moved, mask)


def masked(v, mask):
    return (v.reshape(-1, mask.shape[0], v.shape[1]) * mask[None, :, : v.shape[1]]).reshape(v.shape)


def sigma(x):
    return 0.5 + 0.5 * jnp.tanh(0.5 * x)


def silu(x):
    return x * sigma(x)


def slope(x):
    s = sigma(x)
    return s * (1.0 + x * (1.0 - s))


def normed(z, n):
    return (z - n[0:1]) * n[1:2]


def scaled(hat, n):
    return hat * n[2:3] + n[3:4]


def acted(z, n):
    return scaled(normed(z, n), n)


def input_grad(e, hat, n, s_mean, s_cross):
    return ((n[2:3] * n[1:2]) * (e - s_mean - hat * s_cross)).astype(bf16)


def eighth(v):
    return jnp.sum(v.reshape(-1, 8, v.shape[1]), axis=0)


def clear_first(step, *refs):
    @pl.when(step == 0)
    def _():
        for ref in refs:
            ref[...] = jnp.zeros(ref.shape, ref.dtype)


def add_moments(step, acc, lo, z):
    hi = lo + z.shape[1]
    high = z.shape[0] // 8
    deep = z.reshape(high, 8, hi - lo)
    own = jnp.sum(deep, axis=0) * (1.0 / high)
    off = deep - own[None]
    spread_of = jnp.sum(off * off, axis=0)
    past = step.astype(f32)
    share = 1.0 / (past + 1.0)
    gap = own - acc[0, :, lo:hi]
    acc[0, :, lo:hi] += gap * share
    acc[1, :, lo:hi] += spread_of + gap * gap * (past * share * high)


def add_sums(step, acc, lo, parts):
    hi = lo + parts[0].shape[1]
    for k, part in enumerate(parts):
        acc[k, :, lo:hi] += part


def split_fours(raw, wide):
    rows = wide.shape[0]
    wide[...] = raw[...].astype(f32).reshape(rows, 128)
    return jnp.concatenate([wide[pl.ds(k, rows // 4, stride=4), :] for k in range(4)], axis=1)


def join_fours(value, wide, raw):
    rows = wide.shape[0]
    for k in range(4):
        wide[pl.ds(k, rows // 4, stride=4), :] = value[:, 128 * k : 128 * (k + 1)]
    raw[...] = wide[...].astype(bf16).reshape(raw.shape)


def clear(grid):
    grid[...] = jnp.zeros(grid.shape, grid.dtype)


def fill(grid, side, value, block):
    per = side // STEPS
    line = value.shape[0] // per
    frames = line // side
    for r in range(per):
        at = ((block * per + r + 1) * (side + 2) + 1) * frames
        grid[pl.ds(pl.multiple_of(at, 16), line), :] = value[r * line : (r + 1) * line]


def tap_columns(grid, side, step, rows, flip):
    per = side // STEPS
    line = rows // per
    frames = line // side
    lines = []
    for r in range(per):
        pieces = []
        for a in range(3):
            for b in range(3):
                ra, rb = (2 - a, 2 - b) if flip else (a, b)
                at = ((step * per + r + ra) * (side + 2) + rb) * frames
                pieces.append(grid[pl.ds(pl.multiple_of(at, 16), line), :])
        lines.append(jnp.concatenate(pieces, axis=1))
    return jnp.concatenate(lines, axis=0)


INNER = 8


def greet(n):
    me = lax.axis_index("fsdp")
    mi, mo, depth = lax.rem(me, INNER), lax.div(me, INNER), n // INNER
    barrier = pltpu.get_barrier_semaphore()
    for k in range(1, INNER):
        pl.semaphore_signal(barrier, inc=1, device_id=(mo * INNER + lax.rem(mi + k, INNER),), device_id_type=MESH)
    for k in range(1, depth):
        pl.semaphore_signal(barrier, inc=1, device_id=(lax.rem(mo + k, depth) * INNER + mi,), device_id_type=MESH)


def greeted(n):
    pl.semaphore_wait(pltpu.get_barrier_semaphore(), INNER - 1 + n // INNER - 1)


def total_of(n, centred, own, near, far, mid, near_send, near_recv, far_send, far_recv):
    me = lax.axis_index("fsdp")
    mi, mo, depth = lax.rem(me, INNER), lax.div(me, INNER), n // INNER

    def swap(src, slots, sends, recvs, mine, size, peer):
        copies = []
        for k in range(1, size):
            copy = pltpu.make_async_remote_copy(
                src_ref=src, dst_ref=slots.at[mine], send_sem=sends.at[k], recv_sem=recvs.at[k],
                device_id=(peer(k),), device_id_type=MESH)
            copy.start()
            copies.append(copy)
        slots[mine] = src[...]
        for copy in copies:
            copy.wait()

    def merge(slots, size):
        if not centred:
            return sum(slots[k] for k in range(1, size)) + slots[0]
        mean = sum(slots[k, 0:1] for k in range(size)) * (1.0 / size)
        off = [slots[k, 0:1] - mean for k in range(size)]
        return jnp.concatenate([mean, sum(slots[k, 1:2] + off[k] * off[k] for k in range(size)) * (1.0 / size)], axis=0)

    swap(own, near, near_send, near_recv, mi, INNER, lambda k: mo * INNER + lax.rem(mi + k, INNER))
    mid[...] = merge(near, INNER)
    if depth == 1:
        return mid[...]
    swap(mid, far, far_send, far_recv, mo, depth, lambda k: lax.rem(mo + k, depth) * INNER + mi)
    return merge(far, depth)


def over_groups(part, width):
    lanes = part.shape[1]
    if width < 128:
        wide = jnp.broadcast_to(part, (8, lanes))
        total = wide
        for k in range(1, lanes // width):
            total = total + pltpu.roll(wide, k * width, 1)
        return total[0:1]
    total = sum(part[:, k : k + width] for k in range(0, lanes, width))
    return jnp.concatenate([total] * (lanes // width), axis=1)


def norm_pack(total, pairs, out, folds):
    out[0:2] = total
    for lo, hi, width in folds:
        groups = width / (hi - lo)
        mean = over_groups(total[0:1, lo:hi], width) * groups
        off = total[0:1, lo:hi] - mean
        out[0:1, lo:hi] = mean
        out[1:2, lo:hi] = over_groups(total[1:2, lo:hi] + off * off, width) * groups
    out[1:2] = lax.rsqrt(out[1:2] + EPSILON)
    at = 0
    for pair, lo, hi in pairs:
        out[2:4, at : at + hi - lo] = pair[:, lo:hi]
        at += hi - lo


def sum_pack(total, out, folds):
    out[...] = total
    for lo, hi, width in folds:
        for k in range(out.shape[0]):
            out[k : k + 1, lo:hi] = over_groups(total[k : k + 1, lo:hi], width)


def swap_scratch(shape, n):
    DS, depth = pltpu.SemaphoreType.DMA, n // INNER
    return [pltpu.VMEM((INNER,) + shape, f32), pltpu.VMEM((depth,) + shape, f32), pltpu.VMEM(shape, f32),
        DS((INNER,)), DS((INNER,)), DS((depth,)), DS((depth,))]


def run(body, rows, ins, outs, scratch, n=1, swap=None, call=None, same=None):
    def spec(shape, how):
        if how == "any":
            return pl.BlockSpec(memory_space=pl.ANY)
        if how == "rows":
            return pl.BlockSpec((shape[0] // STEPS,) + tuple(shape[1:]), lambda i, d=len(shape): (i,) + (0,) * (d - 1))
        return pl.BlockSpec(tuple(shape), lambda i, d=len(shape): (0,) * d, pipeline_mode=pl.Buffered(1))
    def out_spec(shape, how):
        if how in ("rows", "any"):
            return spec(shape, how)
        return pl.BlockSpec(tuple(shape), lambda i, d=len(shape): (0,) * d)
    extra = {}
    if swap is not None:
        scratch = scratch + [pltpu.VMEM(swap, f32)]
    if n > 1 and swap is not None:
        scratch = scratch + swap_scratch(swap, n)
    if n > 1 and call is not None:
        extra = dict(collective_id=call, has_side_effects=True)
    return pl.pallas_call(
        body,
        grid=(STEPS,),
        in_specs=[spec(a.shape, how) for a, how in ins],
        out_specs=[out_spec(shape, how) for shape, _, how in outs],
        out_shape=[jax.ShapeDtypeStruct(shape, kind) for shape, kind, _ in outs],
        scratch_shapes=scratch,
        input_output_aliases=same or {},
        compiler_params=pltpu.CompilerParams(dimension_semantics=("arbitrary",), vmem_limit_bytes=58 * 1024 * 1024, **extra),
    )(*[a for a, _ in ins])


def close_moments(step, acc, pairs, out, count, folds, n, ticks, own, *links):
    @pl.when(step == STEPS - 1)
    def _():
        mean = jnp.mean(acc[0], axis=0, keepdims=True)
        off = acc[0] - mean
        own[0:1] = mean
        own[1:2] = jnp.sum(acc[1], axis=0, keepdims=True) * (1.0 / count) + jnp.mean(off * off, axis=0, keepdims=True)
        if n > 1:
            ticks[3]()
            norm_pack(total_of(n, True, own, *links), pairs, out, folds)
            ticks[4]()
        else:
            norm_pack(own[...], pairs, out, folds)


def close_sums(step, acc, out, folds, n, ticks, own, *links):
    if n > 1 and not ticks:
        @pl.when(step == 0)
        def _():
            greet(n)

    @pl.when(step == STEPS - 1)
    def _():
        for k in range(acc.shape[0]):
            own[k : k + 1] = jnp.sum(acc[k], axis=0, keepdims=True)
        if n > 1:
            if ticks:
                ticks[3]()
            else:
                greeted(n)
            sum_pack(total_of(n, False, own, *links), out, folds)
            if ticks:
                ticks[4]()
        else:
            sum_pack(own[...], out, folds)


def places():
    me = lax.axis_index("fsdp")
    return lax.div(me, 8), lax.rem(lax.div(me, 4), 2), lax.rem(lax.div(me, 2), 2), lax.rem(me, 2)


def flat(z, y, x, c):
    return ((z * 2 + y) * 2 + x) * 2 + c


def six(term, n):
    return term.reshape((n // 8, 2, 2, 2, term.shape[0] // n) + term.shape[1:])


def halves(width):
    if width < 256:
        return ((0, width),)
    middle = width // 256 * 128
    return ((0, middle), (middle, width))


def scatter_scratch(parts, n):
    depth, k, DS = n // 8, len(parts), pltpu.SemaphoreType.DMA
    def buf(lead):
        return [pltpu.VMEM(lead + part, bf16) for part in parts]
    return (buf((depth, 2, 2)) + buf((depth, 2, 2)) + buf((depth, 2)) + buf((depth,)) + buf((depth,))
        + [DS((k,)), DS((k, 2)), DS((k, 2, 2)), DS((k, 2, 2)), DS((k, depth)), DS((k, depth))])


def scatter_ticks(n, ins, outs, rest):
    k, depth = len(ins), n // 8
    half, r1, r2, r3, r4 = (rest[j * k : (j + 1) * k] for j in range(5))
    own_sem, c_sem, p_sem, q_sem, z_send, z_recv = rest[5 * k :]
    z, y, x, c = places()
    core, over_x, over_y = flat(z, y, x, 1 - c), flat(z, y, 1 - x, c), flat(z, 1 - y, x, c)
    line = [flat(lax.rem(z + s, depth), y, x, c) for s in range(depth)]
    spots = [lax.rem(z + s, depth) for s in range(depth)]

    def remote(src, dst, send, recv, peer):
        return pltpu.make_async_remote_copy(
            src_ref=src, dst_ref=dst, send_sem=send, recv_sem=recv, device_id=(peer,), device_id_type=MESH)
    def sides(i):
        return tuple(enumerate(halves(half[i].shape[-1])))
    def own(i):
        return pltpu.make_async_copy(ins[i].at[:, :, :, c], half[i], own_sem.at[i])
    def to_core(i):
        return remote(ins[i].at[:, :, :, 1 - c], r1[i], c_sem.at[i, 0], c_sem.at[i, 1], core)
    def to_first(i, t, lo, hi):
        src, peer = (half[i].at[:, :, 1 - x, :, lo:hi], over_x) if t == 0 else (half[i].at[:, 1 - y, :, :, lo:hi], over_y)
        return remote(src, r2[i].at[:, :, :, lo:hi], p_sem.at[i, t, 0], p_sem.at[i, t, 1], peer)
    def to_second(i, t, lo, hi):
        src, peer = (half[i].at[:, 1 - y, x, :, lo:hi], over_y) if t == 0 else (half[i].at[:, y, 1 - x, :, lo:hi], over_x)
        return remote(src, r3[i].at[:, :, lo:hi], q_sem.at[i, t, 0], q_sem.at[i, t, 1], peer)
    def to_line(i, s):
        return remote(half[i].at[spots[s], y, x], r4[i].at[s], z_send.at[i, s], z_recv.at[i, s], line[s])
    def add(target, other):
        target[...] = (target[...].astype(f32) + other[...].astype(f32)).astype(target.dtype)

    def begin():
        for i in range(k):
            own(i).start()
            to_core(i).start()
    def first():
        for i in range(k):
            own(i).wait()
            to_core(i).wait()
            @pl.loop(0, depth)
            def _(zz, i=i):
                for a in range(2):
                    for b in range(2):
                        add(half[i].at[zz, a, b], r1[i].at[zz, a, b])
            for t, (lo, hi) in sides(i):
                to_first(i, t, lo, hi).start()
    def second():
        for i in range(k):
            for t, (lo, hi) in sides(i):
                to_first(i, t, lo, hi).wait()
                @pl.loop(0, depth)
                def _(zz, i=i, t=t, lo=lo, hi=hi):
                    for o in range(2):
                        target = half[i].at[zz, o, x] if t == 0 else half[i].at[zz, y, o]
                        add(target.at[:, lo:hi], r2[i].at[zz, o, :, lo:hi])
                to_second(i, t, lo, hi).start()
    def third():
        for i in range(k):
            for t, (lo, hi) in sides(i):
                to_second(i, t, lo, hi).wait()
            @pl.loop(0, depth)
            def _(zz, i=i):
                add(half[i].at[zz, y, x], r3[i].at[zz])
            for s in range(1, depth):
                to_line(i, s).start()
    def finish():
        for i in range(k):
            outs[i][...] = half[i][z, y, x].astype(f32)
            for s in range(1, depth):
                to_line(i, s).wait()
                outs[i][...] += r4[i][s].astype(f32)
    return begin, first, second, third, finish


GATHER_SEMS = 9


def gather_scratch(k, n):
    DS, depth = pltpu.SemaphoreType.DMA, n // 8
    return [DS((1,)), DS((depth,)), DS((depth,)), DS((2, 2)), DS((2, 2)), DS((2, 3)), DS((2, 3)), DS((8,)), DS((8,))] * k


class Moves:
    def __init__(self, n, shard, whole, sems):
        self.n, self.shard, self.whole, self.sems = n, shard, whole, sems
        self.at = places()
        self.sides = tuple(enumerate(halves(whole.shape[-1])))

    def remote(self, src, dst, send, recv, *peer):
        return pltpu.make_async_remote_copy(
            src_ref=src, dst_ref=dst, send_sem=send, recv_sem=recv, device_id=(flat(*peer),), device_id_type=MESH)

    def part(self, name, t, lo, hi):
        z, y, x, c = self.at
        index = {
            "p": (slice(None), y, x, c),
            "q": (slice(None), y, slice(None), c) if t == 0 else (slice(None), slice(None), x, c),
            "c1": (slice(None), y, 1 - x, c) if t == 0 else (slice(None), 1 - y, x, c),
            "c2": (slice(None), 1 - y, slice(None), c) if t == 0 else (slice(None), slice(None), 1 - x, c),
        }["p" if name == "c0" else name]
        return self.whole.at[index + (slice(None), slice(lo, hi))]

    def copies(self, name):
        z, y, x, c = self.at
        own, z_send, z_recv, p, q, c_send, c_recv, d_send, d_recv = self.sems
        depth = self.n // 8
        if name == "z":
            mine = self.whole.at[z, y, x, c]
            return [pltpu.make_async_copy(self.shard, mine, own.at[0])] + [
                self.remote(self.shard, mine, z_send.at[s], z_recv.at[s], lax.rem(z + s, depth), y, x, c) for s in range(1, depth)]
        if name == "d":
            mine = self.whole.at[:, y, x, c]
            found = []
            for k in range(1, 8):
                other = lax.rem((y * 2 + x) * 2 + c + k, 8)
                found.append(self.remote(mine, mine, d_send.at[k], d_recv.at[k], z, 0, 0, other))
            return found
        found = []
        for t, (lo, hi) in self.sides:
            src = self.part(name, t, lo, hi)
            if name[0] == "c":
                j = int(name[1])
                found.append(self.remote(src, src, c_send.at[t, j], c_recv.at[t, j], z, y, x, 1 - c))
                continue
            sem = p if name == "p" else q
            peer = (z, y, 1 - x, c) if (t == 0) == (name == "p") else (z, 1 - y, x, c)
            found.append(self.remote(src, src, sem.at[t, 0], sem.at[t, 1], *peer))
        return found

    def start(self, *names):
        for name in names:
            for copy in self.copies(name):
                copy.start()

    def wait(self, *names):
        for name in names:
            for copy in self.copies(name):
                copy.wait()


def moves(n, shards, wholes, rest):
    return [Moves(n, shard, whole, rest[GATHER_SEMS * i : GATHER_SEMS * (i + 1)]) for i, (shard, whole) in enumerate(zip(shards, wholes))]


def spread_shapes(shards, n):
    return [((n // 8, 2, 2, 2) + v.shape, v.dtype, "any") for v in shards]


def whole_shapes(wholes):
    return [(v.shape, v.dtype, "any") for v in wholes]


def gathered(v, n):
    return v.reshape((n * v.shape[4],) + v.shape[5:])


def at_lanes(v, offset):
    rows, width = v.shape
    wide = v if width == 128 else jnp.concatenate([v, jnp.zeros((rows, 128 - width), v.dtype)], axis=1)
    return pltpu.roll(wide, offset, 1) if offset else wide


def build_fast(first_t, middle_t, last, skip, mid_norm, out_norm, ids, band, fproj, fmid, flast, fpair, mask, lanes):
    band[...] = jnp.zeros(band.shape, bf16)
    fproj[...] = jnp.zeros(fproj.shape, bf16)
    flast[...] = jnp.zeros(flast.shape, bf16)
    none = jnp.zeros((96, 128), f32)
    for tap in range(3):
        block = jnp.concatenate([first_t[:, 128 * tap : 128 * (tap + 1)].astype(f32), none], axis=0).T
        placed = [pltpu.roll(block, 32 * j, 1) if j else block for j in range(4)]
        for part in range(3):
            for k in range(4):
                here = [j for j in range(4) if (j + tap - 1) % 4 == k and part == (1 if j + tap < 1 else 2 if j + tap > 4 else 0)]
                if here:
                    (j,) = here
                    band[128 * k : 128 * (k + 1), 128 * part : 128 * (part + 1)] += placed[j].astype(bf16)
    lanes[...] = jnp.zeros(lanes.shape, f32)
    lanes[:, :288] = middle_t[...].astype(f32)
    for group in range(3):
        block = jnp.concatenate([lanes[:, 128 * group : 128 * (group + 1)], none], axis=0).T
        for tap in range(4 * group, min(4 * group + 4, 9)):
            part = block[32 * (tap % 4) : 32 * (tap % 4 + 1)]
            for k in range(4):
                fmid[128 * tap + 32 * k : 128 * tap + 32 * (k + 1)] = (pltpu.roll(part, 32 * k, 1) if k else part).astype(bf16)
    for k in range(4):
        flast[32 * k : 32 * (k + 1), 128 * k : 128 * (k + 1)] = last[...]
    for k in range(2):
        fproj[128 * k : 128 * (k + 1), 128 * k : 128 * (k + 1)] = skip[...]
        narrow = at_lanes(mid_norm[k].astype(f32), 0)
        wide = jnp.concatenate([narrow] * 4, axis=0)
        fpair[:, 128 * k : 128 * (k + 1)] = sum(pltpu.roll(wide, 32 * j, 1) for j in range(1, 4))[:2] + narrow
        for j in range(4):
            fpair[:, 256 + 512 * k + 128 * j : 384 + 512 * k + 128 * j] = out_norm[k].astype(f32)
    frames = mask.shape[1]
    row = lax.broadcasted_iota(jnp.int32, (frames, frames), 0)
    column = lax.broadcasted_iota(jnp.int32, (frames, frames), 1)
    spread_ids = jnp.broadcast_to(ids[...].astype(f32), (frames, frames))
    def pick(by):
        return jnp.sum(jnp.where(column == row + by, spread_ids, 0.0), axis=1, keepdims=True)
    at = lax.broadcasted_iota(jnp.int32, (frames, 1), 0)
    here = pick(0)
    prev = jnp.where((here == pick(-1)) & (at > 0), 1.0, 0.0)
    after = jnp.where((here == pick(1)) & (at < frames - 1), 1.0, 0.0)
    mask[0] = jnp.broadcast_to(prev, mask.shape[1:])
    mask[1] = jnp.broadcast_to(after, mask.shape[1:])


def pack_norms(pairs, out):
    total, offset = None, 0
    for pair in pairs:
        v = at_lanes(jnp.concatenate([pair[...].astype(f32)] * 4, axis=0), offset)
        total = v if total is None else total + v
        offset += pair.shape[1]
    out[...] = total


def join_norms(gathered_of, shares, out):
    n = gathered_of.shape[0]
    offset, lo = 0, 0
    for share in shares:
        wide = share * n
        pick = lax.broadcasted_iota(jnp.int32, (128, wide), 0) == offset + lax.broadcasted_iota(jnp.int32, (128, wide), 1) % share
        pick = jnp.where(pick, 1.0, 0.0).astype(bf16)
        mine = lax.broadcasted_iota(jnp.int32, (n, wide), 0) == lax.broadcasted_iota(jnp.int32, (n, wide), 1) // share
        for row in range(2):
            each = dot(gathered_of[:, row, :].astype(bf16), pick)
            out[row : row + 1, lo : lo + wide] = jnp.sum(jnp.where(mine, each, 0.0), axis=0, keepdims=True)
        offset += share
        lo += wide


def body0(n, lat_shard, first_shard, p_lat, p_one, p_two, p_out, p_proj, first_t, middle_t, last_w, skip, mid_norm, out_norm, ids,
          lat_whole, first_whole, spair, band, fproj, fmid, flast, fpair, mask, own, norms_whole, lanes, *sems):
    lat, norms, first = moves(n, (lat_shard, own, first_shard), (lat_whole, norms_whole, first_whole), sems)
    pairs = (p_lat, p_one, p_two, p_out, p_proj)
    greet(n)
    pack_norms(pairs, own)
    greeted(n)
    for m in (lat, norms, first):
        m.start("z")
    build_fast(first_t, middle_t, last_w, skip, mid_norm, out_norm, ids, band, fproj, fmid, flast, fpair, mask, lanes)
    for m in (lat, norms):
        m.wait("z")
        m.start("d")
    first.wait("z")
    first.start("p", "c0")
    lat.wait("d")
    norms.wait("d")
    join_norms(norms_whole[...].reshape(n, 8, 128), [p.shape[1] for p in pairs], spair)
    first.wait("p", "c0")


def stage0(lat_shard, first_shard, pairs, fast, ids, n):
    VM, ANY = pl.BlockSpec(memory_space=pltpu.VMEM), pl.BlockSpec(memory_space=pl.ANY)
    shape_of = lambda shape, kind: jax.ShapeDtypeStruct(shape, kind)
    small = tuple(pairs) + tuple(fast) + (ids,)
    width = sum(p.shape[1] for p in pairs) * n
    return pl.pallas_call(
        functools.partial(body0, n),
        in_specs=[ANY, ANY] + [VM] * len(small),
        out_specs=[ANY, ANY] + [VM] * 7,
        out_shape=[shape_of(s, k) for s, k, _ in spread_shapes([lat_shard, first_shard], n)]
        + [shape_of((2, width), f32), shape_of((512, 384), bf16), shape_of((256, 256), bf16), shape_of((1152, 128), bf16),
           shape_of((128, 512), bf16), shape_of((2, 1280), f32), shape_of((2, ids.shape[1], 256), f32)],
        scratch_shapes=[pltpu.VMEM((8, 128), f32), pltpu.VMEM((n // 8, 2, 2, 2, 8, 128), f32), pltpu.VMEM((32, 384), f32)] + gather_scratch(3, n),
        compiler_params=pltpu.CompilerParams(collective_id=1, has_side_effects=True),
    )(lat_shard, first_shard, *small)


def run_ticks(step, n, ticks, at):
    @pl.when(step == 0)
    def _():
        greet(n)
    for j in range(len(at)):
        @pl.when(step == at[j])
        def _(j=j):
            if j == 0:
                greeted(n)
            ticks[j]()
    return tuple(ticks) if len(at) == 3 else tuple(ticks[:3]) + (lambda: None, ticks[4])


def strips(rows, width, body, init):
    return lax.fori_loop(0, rows // STRIP, lambda k, carry: body(pl.ds(pl.multiple_of(k * STRIP, STRIP), STRIP), carry), init, unroll=True)


FOLDS1 = ((256, 384, 32), (384, 896, 128))
FOLDS2 = ((256, 384, 32),)
FOLDS3 = ((256, 768, 128),)


def body1(n, raw, lat, band, fproj, mask, spair, fpair, held, *refs):
    shards, (fast4, lat_pre, fone_pre, n1), wholes, (wide, acc), rest = refs[:2], refs[2:6], refs[6:9], refs[9:11], refs[11:]
    step = pl.program_id(0)
    clear_first(step, acc)
    ticks, swap = (), rest
    if n > 1:
        first, *others = moves(n, (None,) + tuple(shards), wholes, rest)
        swap = rest[3 * GATHER_SEMS :]

        def begin():
            first.start("q", "c1")
            for m in others:
                m.start("z")
        def middle():
            first.wait("q")
            first.start("c2")
        def finish():
            first.wait("c1", "c2")
            for m in others:
                m.wait("z")
        ticks = (begin, middle, lambda: None, lambda: None, finish)
        ticks = run_ticks(step, n, ticks, (0, 4, 6))
    f = split_fours(raw, wide).astype(bf16)
    fast4[...] = f
    prev, nxt = mask[0], mask[1]
    z = dot_nt(f[:, :384], lat[:, 256:]) + shift(dot_nt(f[:, 256:], lat[:, :256]), prev, 1)
    lat_pre[...] = z
    add_moments(step, acc, 0, z)
    y = dot(f, band[...])
    z = y[:, :128] + shift(y[:, 128:256], prev, 1) + shift(y[:, 256:], nxt, -1)
    fone_pre[...] = z
    add_moments(step, acc, 256, z)
    z = jnp.concatenate([dot(f[:, :256], fproj[...]), dot(f[:, 256:], fproj[...])], axis=1)
    add_moments(step, acc, 384, z)
    close_moments(step, acc, ((spair, 0, 256), (fpair, 0, 128), (fpair, 768, 1280)), n1, f.shape[0] * STEPS, FOLDS1, n, ticks, *swap)


def stage1(raw, lat, band, fproj, mask, spair, fpair, held, shards_of, n):
    rows = raw.shape[0] * raw.shape[1] // 4
    return run(functools.partial(body1, n), rows,
        [(raw, "rows")] + [(v, "all") for v in (lat, band, fproj, mask, spair, fpair)] + [(v, "any") for v in (held,) + tuple(shards_of)],
        [((rows, 512), bf16, "rows"), ((rows, 256), f32, "rows"), ((rows, 128), f32, "rows"), ((4, 896), f32, "all")] + whole_shapes([held]) + spread_shapes(shards_of, n),
        [pltpu.VMEM((rows * 4 // STEPS, 128), f32), pltpu.VMEM((2, 8, 896), f32)] + (gather_scratch(3, n) if n > 1 else []), n, (2, 896), 2, {7: 4})


def body2(n, side, slow, lat_pre, fone_pre, n1, first, fmid, mask, spair, fpair, held_a, held_b, shard,
          lateral, one_pre, ftwo_pre, n2, whole_a, whole_b, whole_c, grid, acc, *rest):
    step = pl.program_id(0)
    rows = slow.shape[0]
    n_lat, n_fone = n1[:, :256], n1[:, 256:384]
    ticks, swap = (), rest
    if n > 1:
        middle, last, proj = moves(n, (None, None, shard), (whole_a, whole_b, whole_c), rest)
        swap = rest[3 * GATHER_SEMS :]

        def begin():
            middle.start("p", "c0")
            last.start("p", "c0")
            proj.start("z")
        def half():
            middle.wait("p")
            middle.start("q", "c1")
        def late():
            proj.wait("z")
            proj.start("p", "c0")
        def close():
            middle.wait("q")
            middle.start("c2")
        def finish():
            last.wait("p", "c0")
            proj.wait("p", "c0")
            middle.wait("c0", "c1", "c2")
        ticks = (begin, half, late, close, finish)
        ticks = run_ticks(step, n, ticks, (0, 2, 4, 6))

    def put(block):
        part = fone_pre[pl.ds(pl.multiple_of(block * rows, 16), rows), :]
        fill(grid, side, silu(acted(part, n_fone)).astype(bf16), block)

    @pl.when(step == 0)
    def _():
        clear(grid)
        clear(acc)
        put(0)

    put(jnp.minimum(step + 1, STEPS - 1))
    lat = silu(acted(lat_pre[...], n_lat)).astype(bf16)
    lateral[...] = lat
    joined = jnp.concatenate([slow[...], lat], axis=1)
    z = dot(joined, first[1]) + shift(dot(joined, first[0]), mask[0], 1) + shift(dot(joined, first[2]), mask[1], -1)
    one_pre[...] = z
    add_moments(step, acc, 0, z)
    z = dot(tap_columns(grid, side, step, rows, False), fmid[...])
    ftwo_pre[...] = z
    add_moments(step, acc, 256, z)
    close_moments(step, acc, ((spair, 256, 512), (fpair, 128, 256)), n2, rows * STEPS, FOLDS2, n, ticks, *swap)


def stage2(slow, lat_pre, fone_pre, n1, first, fmid, mask, spair, fpair, held, shard, side, n):
    rows = slow.shape[0]
    frames = rows // side**2
    return run(functools.partial(body2, n, side), rows,
        [(slow, "rows"), (lat_pre, "rows")] + [(v, "all") for v in (fone_pre, n1, first, fmid, mask, spair, fpair)] + [(v, "any") for v in tuple(held) + (shard,)],
        [((rows, 256), bf16, "rows"), ((rows, 256), f32, "rows"), ((rows, 128), f32, "rows"), ((4, 384), f32, "all")] + whole_shapes(held) + spread_shapes([shard], n),
        [pltpu.VMEM(((side + 2) ** 2 * frames, 128), bf16), pltpu.VMEM((2, 8, 384), f32)] + (gather_scratch(3, n) if n > 1 else []), n, (2, 384), 3, {9: 4, 10: 5})


def body3(n, side, one_pre, ftwo_pre, n2, middle, flast, spair, fpair, held_a, held_b, two_pre, ftwo, n3, whole_a, whole_b, grid, acc, *rest):
    step = pl.program_id(0)
    rows = two_pre.shape[0]
    n_one, n_ftwo = n2[:, :256], n2[:, 256:]
    ticks, swap = (), rest
    if n > 1:
        both = moves(n, (None, None), (whole_a, whole_b), rest)
        swap = rest[2 * GATHER_SEMS :]

        def begin():
            for m in both:
                m.start("q", "c1")
        def half():
            for m in both:
                m.wait("q")
                m.start("c2")
        def finish():
            for m in both:
                m.wait("c1", "c2")
        ticks = (begin, half, lambda: None, lambda: None, finish)
        ticks = run_ticks(step, n, ticks, (0, 5, 6))

    def put(block):
        part = one_pre[pl.ds(pl.multiple_of(block * rows, 16), rows), :]
        fill(grid, side, silu(acted(part, n_one)).astype(bf16), block)

    @pl.when(step == 0)
    def _():
        clear(grid)
        clear(acc)
        put(0)

    put(jnp.minimum(step + 1, STEPS - 1))
    z = dot(tap_columns(grid, side, step, rows, False), middle[...])
    two_pre[...] = z
    add_moments(step, acc, 0, z)
    f = silu(acted(ftwo_pre[...], n_ftwo)).astype(bf16)
    ftwo[...] = f
    for k in range(2):
        add_moments(step, acc, 256 * (k + 1), dot(f, flast[:, 256 * k : 256 * (k + 1)]))
    close_moments(step, acc, ((spair, 512, 768), (fpair, 256, 768)), n3, rows * STEPS, FOLDS3, n, ticks, *swap)


def stage3(one_pre, ftwo_pre, n2, middle, flast, spair, fpair, held, side, n):
    rows = one_pre.shape[0]
    frames = rows // side**2
    return run(functools.partial(body3, n, side), rows,
        [(one_pre, "all"), (ftwo_pre, "rows")] + [(v, "all") for v in (n2, middle, flast, spair, fpair)] + [(v, "any") for v in held],
        [((rows, 256), f32, "rows"), ((rows, 128), bf16, "rows"), ((4, 768), f32, "all")] + whole_shapes(held),
        [pltpu.VMEM(((side + 2) ** 2 * frames, 256), bf16), pltpu.VMEM((2, 8, 768), f32)] + (gather_scratch(2, n) if n > 1 else []), n, (2, 768), 4, {7: 3, 8: 4})


def body4(n, two_pre, slow, lateral, n3, last, proj, spair, two, proj_pre, n4, acc, *swap):
    step = pl.program_id(0)
    clear_first(step, acc)
    v = silu(acted(two_pre[...], n3[:, :256])).astype(bf16)
    two[...] = v
    for k in range(4):
        add_moments(step, acc, 256 * k, dot(v, last[:, 256 * k : 256 * (k + 1)]))
    joined = jnp.concatenate([slow[...], lateral[...]], axis=1)
    for k in range(4):
        z = dot(joined, proj[:, 256 * k : 256 * (k + 1)])
        proj_pre[:, 256 * k : 256 * (k + 1)] = z.astype(proj_pre.dtype)
        add_moments(step, acc, 1024 + 256 * k, z)
    if n > 1:
        @pl.when(step == 0)
        def _():
            greet(n)
    close_moments(step, acc, ((spair, 768, 2816),), n4, v.shape[0] * STEPS, (), n,
        (None, None, None, lambda: greeted(n), lambda: None), *swap)


def stage4(two_pre, slow, lateral, n3, last, proj, spair, n):
    rows = two_pre.shape[0]
    return run(functools.partial(body4, n), rows,
        [(v, "rows") for v in (two_pre, slow, lateral)] + [(v, "all") for v in (n3, last, proj, spair)],
        [((rows, 256), bf16, "rows"), ((rows, 1024), f32, "rows"), ((4, 2048), f32, "all")], [pltpu.VMEM((2, 8, 2048), f32)], n, (2, 2048), 5)


def body5(two, proj_pre, cot, fast4, ftwo, fcot, n1, n3, n4, last, fproj, flast,
          slow_out, fast_out, delta, fdelta, sums, wide, three, fthree, fskip, fgrad, fout, acc):
    step = pl.program_id(0)
    rows = two.shape[0]
    clear_first(step, acc)
    fgrad[...] = split_fours(fcot, wide)
    three[...] = dot(two[...], last[...])
    fthree[...] = dot(ftwo[...], flast[...])
    for k in range(2):
        fskip[:, 256 * k : 256 * (k + 1)] = dot(fast4[:, 256 * k : 256 * (k + 1)], fproj[...])

    def side_of(za, zb, grad, na, nb, out, keep, lo, lanes):
        ga, gb, base = 0.5 * na[1:2] * na[2:3], 0.5 * nb[1:2] * nb[2:3], 0.5 * (na[3:4] + nb[3:4])
        ma, mb = na[0:1], nb[0:1]
        def one(at, carry):
            ha = za[at, lanes].astype(f32) - ma
            hb = zb[at, lanes].astype(f32) - mb
            h = ha * ga + hb * gb + base
            th = jnp.tanh(h)
            u = 1.0 + th
            out[at, lanes] = (h * u).astype(out.dtype)
            d = (0.5 * grad[at, lanes].astype(f32)) * (u * (1.0 + h * (1.0 - th)))
            keep[at, lanes] = d
            return carry[0] + eighth(d), carry[1] + eighth(d * ha), carry[2] + eighth(d * hb)
        zero = jnp.zeros((8, 256), f32)
        add_sums(step, acc, lo, strips(rows, 256, one, (zero, zero, zero)))

    for k in range(4):
        lanes = slice(256 * k, 256 * (k + 1))
        side_of(three, proj_pre, cot, n4[:, lanes], n4[:, 1024 + 256 * k : 1280 + 256 * k], slow_out, delta, 256 * k, lanes)
    for k in range(2):
        lanes = slice(256 * k, 256 * (k + 1))
        side_of(fthree, fskip, fgrad, n3[:, 256 + 256 * k : 512 + 256 * k], n1[:, 384 + 256 * k : 640 + 256 * k], fout, fdelta, 1024 + 256 * k, lanes)
    join_fours(fout[...], wide, fast_out)

    @pl.when(step == STEPS - 1)
    def _():
        scales = (1.0, jnp.concatenate([n4[1:2, :1024], n3[1:2, 256:]], axis=1), jnp.concatenate([n4[1:2, 1024:], n1[1:2, 384:]], axis=1))
        for k in range(3):
            sums[k : k + 1] = jnp.sum(acc[k], axis=0, keepdims=True) * scales[k]


def stage5(two, proj_pre, cot, fast4, ftwo, fcot, n1, n3, n4, last, fproj, flast):
    rows = two.shape[0]
    part = rows // STEPS
    return run(body5, rows,
        [(two, "rows"), (proj_pre, "rows"), (cot, "rows"), (fast4, "rows"), (ftwo, "rows"), (fcot, "rows"),
         (n1, "all"), (n3, "all"), (n4, "all"), (last, "all"), (fproj, "all"), (flast, "all")],
        [((rows, 1024), bf16, "rows"), (fcot.shape, bf16, "rows"), ((rows, 1024), f32, "rows"), ((rows, 512), f32, "rows"), ((3, 1536), f32, "all")],
        [pltpu.VMEM((part * 4, 128), f32), pltpu.VMEM((part, 1024), f32), pltpu.VMEM((part, 512), f32), pltpu.VMEM((part, 512), f32),
         pltpu.VMEM((part, 512), f32), pltpu.VMEM((part, 512), f32), pltpu.VMEM((3, 8, 1536), f32)])


def body5x(n, own, out, *links):
    greet(n)
    greeted(n)
    sum_pack(total_of(n, False, own, *links), out, ((1024, 1536, 128),))


def stage5x(sums, n):
    return pl.pallas_call(
        functools.partial(body5x, n),
        in_specs=[pl.BlockSpec(memory_space=pltpu.VMEM)],
        out_specs=pl.BlockSpec(memory_space=pltpu.VMEM),
        out_shape=jax.ShapeDtypeStruct(sums.shape, f32),
        scratch_shapes=swap_scratch(sums.shape, n),
        compiler_params=pltpu.CompilerParams(collective_id=6, has_side_effects=True),
    )(sums)


def body6(n, total, two, two_pre, proj_pre, slow, lateral, delta, fast4, ftwo, ftwo_pre, fdelta, n1, n2, n3, n4, s5, last, fproj, flast,
          d_proj, d_fproj, last_term, proj_term, flast_term, e_two, e_ftwo, sums,
          three, fthree, fskip, d_three, d_fthree, acc, last_acc, proj_acc, *swap):
    step = pl.program_id(0)
    rows = two.shape[0]
    clear_first(step, acc, last_acc, proj_acc, flast_term)
    three[...] = dot(two[...], last[...])
    fthree[...] = dot(ftwo[...], flast[...])
    for k in range(2):
        fskip[:, 256 * k : 256 * (k + 1)] = dot(fast4[:, 256 * k : 256 * (k + 1)], fproj[...])

    def side_of(za, zb, e, na, nb, s, da, db, lanes):
        pa, pb = na[2:3] * na[1:2], nb[2:3] * nb[1:2]
        qa, qb = pa * na[1:2] * s[1:2], pb * nb[1:2] * s[2:3]
        ma, mb, base = na[0:1], nb[0:1], s[0:1]
        def one(at, carry):
            d = e[at, lanes] - base
            da[at, lanes] = (d * pa - (za[at, lanes].astype(f32) - ma) * qa).astype(bf16)
            db[at, lanes] = (d * pb - (zb[at, lanes].astype(f32) - mb) * qb).astype(bf16)
            return carry
        strips(rows, 256, one, 0)

    for k in range(4):
        lanes = slice(256 * k, 256 * (k + 1))
        side_of(three, proj_pre, delta, n4[:, lanes], n4[:, 1024 + 256 * k : 1280 + 256 * k], s5[:, lanes] * (1.0 / total), d_three, d_proj, lanes)
    for k in range(2):
        lanes = slice(256 * k, 256 * (k + 1))
        side_of(fthree, fskip, fdelta, n3[:, 256 + 256 * k : 512 + 256 * k], n1[:, 384 + 256 * k : 640 + 256 * k],
                s5[:, 1024 + 256 * k : 1280 + 256 * k] * (0.25 / total), d_fthree, d_fproj, lanes)

    wide = slow.shape[1]
    last_acc[...] += dot_tn(two[...], d_three[...])
    proj_acc[:wide] += dot_tn(slow[...], d_proj[...])
    proj_acc[wide:] += dot_tn(lateral[...], d_proj[...])
    flast_term[...] += dot_tn(ftwo[...], d_fthree[...])
    h = normed(two_pre[...], n3[:, :256])
    e = dot_nt(d_three[...], last[...]) * slope(scaled(h, n3[:, :256]))
    e_two[...] = e
    add_sums(step, acc, 0, (eighth(e), eighth(e * h)))
    h = normed(ftwo_pre[...], n2[:, 256:])
    e = dot_nt(d_fthree[...], flast[...]) * slope(scaled(h, n2[:, 256:]))
    e_ftwo[...] = e
    add_sums(step, acc, 256, (eighth(e), eighth(e * h)))
    close_sums(step, acc, sums, ((256, 384, 32),), n, (), *swap)

    @pl.when(step == STEPS - 1)
    def _():
        last_term[...] = last_acc[...].astype(bf16)
        proj_term[...] = proj_acc[...].astype(bf16)


def stage6(total, two, two_pre, proj_pre, slow, lateral, delta, fast4, ftwo, ftwo_pre, fdelta, n1, n2, n3, n4, s5, last, fproj, flast, n):
    rows = two.shape[0]
    part = rows // STEPS
    return run(functools.partial(body6, n, total), rows,
        [(a, "rows") for a in (two, two_pre, proj_pre, slow, lateral, delta, fast4, ftwo, ftwo_pre, fdelta)]
        + [(a, "all") for a in (n1, n2, n3, n4, s5, last, fproj, flast)],
        [((rows, 1024), bf16, "rows"), ((rows, 512), bf16, "rows"), ((256, 1024), bf16, "all"), ((1280, 1024), bf16, "all"), ((128, 512), f32, "all"),
         ((rows, 256), f32, "rows"), ((rows, 128), f32, "rows"), ((2, 384), f32, "all")],
        [pltpu.VMEM((part, 1024), f32), pltpu.VMEM((part, 512), f32), pltpu.VMEM((part, 512), f32),
         pltpu.VMEM((part, 1024), bf16), pltpu.VMEM((part, 512), bf16), pltpu.VMEM((2, 8, 384), f32),
         pltpu.VMEM((256, 1024), f32), pltpu.VMEM((1280, 1024), f32)], n, (2, 384), 7)


def body7(n, side, total, one_pre, two_pre, e_two, fone_pre, ftwo_pre, e_ftwo, n1, n2, n3, s6, middle, fmid, proj_term,
          middleerm, fmid_term, e_one, e_fone, sums, proj_grad, grid, fgrid, acc, mid_acc, *rest):
    step = pl.program_id(0)
    ticks, swap = (), rest
    if n > 1:
        ticks = scatter_ticks(n, (proj_term,), (proj_grad,), rest[:11])
        swap = rest[11:]
        ticks = run_ticks(step, n, ticks, (0, 2, 4, 6))
    rows = one_pre.shape[0]

    def put(block):
        at = pl.ds(pl.multiple_of(block * rows, 16), rows)
        p, s = n3[:, :256], s6[:, :256] * (1.0 / total)
        fill(grid, side, input_grad(e_two[at, :], normed(two_pre[at, :], p), p, s[0:1], s[1:2]), block)
        p, s = n2[:, 256:], s6[:, 256:] * (0.25 / total)
        fill(fgrid, side, input_grad(e_ftwo[at, :], normed(ftwo_pre[at, :], p), p, s[0:1], s[1:2]), block)

    @pl.when(step == 0)
    def _():
        clear(grid)
        clear(fgrid)
        clear(acc)
        put(0)
        mid_acc[...] = jnp.zeros_like(mid_acc)
        fmid_term[...] = jnp.zeros_like(fmid_term)

    put(jnp.minimum(step + 1, STEPS - 1))

    def one_side(pre, p, columns, weight, lo, term, e_out):
        h = normed(pre[...], p)
        act = scaled(h, p)
        s = sigma(act)
        mid = act * s
        term[...] += dot_tn(mid.astype(bf16), columns)
        width = weight.shape[1]
        turned = jnp.concatenate([weight[width * k : width * (k + 1)] for k in range(9)], axis=1)
        e = dot_nt(columns, turned) * (s + mid * (1.0 - s))
        e_out[...] = e
        add_sums(step, acc, lo, (eighth(e), eighth(e * h)))

    one_side(one_pre, n2[:, :256], tap_columns(grid, side, step, rows, True), middle, 0, mid_acc, e_one)
    one_side(fone_pre, n1[:, 256:384], tap_columns(fgrid, side, step, rows, True), fmid, 256, fmid_term, e_fone)
    close_sums(step, acc, sums, ((256, 384, 32),), n, ticks, *swap)

    @pl.when(step == STEPS - 1)
    def _():
        for k in range(9):
            middleerm[k] = mid_acc[:, 256 * k : 256 * (k + 1)].astype(bf16)


def stage7(total, one_pre, two_pre, e_two, fone_pre, ftwo_pre, e_ftwo, n1, n2, n3, s6, middle, fmid, proj_term, side, n):
    terms = [six(v, n) for v in (proj_term,)] if n > 1 else [proj_term]
    parts = [(v.shape[0] // n, v.shape[1]) for v in (proj_term,)]
    rows = one_pre.shape[0]
    frames = rows // side**2
    return run(functools.partial(body7, n, side, total), rows,
        [(one_pre, "rows"), (two_pre, "all"), (e_two, "all"), (fone_pre, "rows"), (ftwo_pre, "all"), (e_ftwo, "all")]
        + [(a, "all") for a in (n1, n2, n3, s6, middle, fmid)] + [(v, "any") for v in terms],
        [((9, 256, 256), bf16, "all"), ((128, 1152), f32, "all"), ((rows, 256), f32, "rows"), ((rows, 128), f32, "rows"), ((2, 384), f32, "all")] + [(part, f32, "all") for part in parts],
        [pltpu.VMEM(((side + 2) ** 2 * frames, 256), bf16), pltpu.VMEM(((side + 2) ** 2 * frames, 128), bf16),
         pltpu.VMEM((2, 8, 384), f32), pltpu.VMEM((256, 2304), f32)] + (scatter_scratch(parts, n) if n > 1 else []), n, (2, 384), 8)


def body8(n, total, slow, lateral, one_pre, e_one, n2, s7, mask, middleerm, first_term, pieces, middle_grad, first_acc, *rest):
    step = pl.program_id(0)
    if n > 1:
        ticks = scatter_ticks(n, (middleerm,), (middle_grad,), rest)
        run_ticks(step, n, ticks, (0, 2, 4))

        @pl.when(step == STEPS - 1)
        def _():
            ticks[3]()
    clear_first(step, first_acc)
    p, s = n2[:, :256], s7[:, :256] * (1.0 / total)
    d = input_grad(e_one[...], normed(one_pre[...], p), p, s[0:1], s[1:2])
    w = d.astype(f32)
    rows = w.shape[0]
    before = pltpu.roll(masked(w, mask[0]), rows - 1, 0).astype(bf16)
    after = pltpu.roll(masked(w, mask[1]), 1, 0).astype(bf16)
    columns = jnp.concatenate([before, d, after], axis=1)
    pieces[...] = columns
    wide = slow.shape[1]
    first_acc[:wide] += dot_tn(slow[...], columns)
    first_acc[wide:] += dot_tn(lateral[...], columns)

    @pl.when(step == STEPS - 1)
    def _():
        for k in range(3):
            first_term[k] = first_acc[:, 256 * k : 256 * (k + 1)].astype(bf16)
        if n > 1:
            ticks[4]()


def stage8(total, slow, lateral, one_pre, e_one, n2, s7, mask, middleerm, n):
    rows = slow.shape[0]
    part = (middleerm.shape[0] // n, middleerm.shape[1])
    return run(functools.partial(body8, n, total), rows,
        [(a, "rows") for a in (slow, lateral, one_pre, e_one)] + [(a, "all") for a in (n2, s7, mask)]
        + [(six(middleerm, n) if n > 1 else middleerm, "any")],
        [((3, 1280, 256), bf16, "all"), ((rows, 768), bf16, "rows"), (part, f32, "all")],
        [pltpu.VMEM((1280, 768), f32)] + (scatter_scratch([part], n) if n > 1 else []), n, None, 12)


def body8b(n, pieces, d_proj, lat_pre, n1, first, proj, last_term, first_term,
           slow_grad, e_lat, sums, last_grad, first_grad, acc, *rest):
    step = pl.program_id(0)
    ticks, swap = (), rest
    if n > 1:
        ticks = scatter_ticks(n, (last_term, first_term), (last_grad, first_grad), rest[:16])
        swap = rest[16:]
        ticks = run_ticks(step, n, ticks, (0, 2, 4, 6))
    clear_first(step, acc)
    wide = proj.shape[0] - 256

    def back(lo, hi):
        part = dot_nt(d_proj[...], proj[lo:hi])
        for k in range(3):
            part += dot_nt(pieces[:, 256 * k : 256 * (k + 1)], first[k, lo:hi])
        return part

    for k in range(4):
        slow_grad[:, 256 * k : 256 * (k + 1)] = back(256 * k, 256 * (k + 1)).astype(bf16)
    h = normed(lat_pre[...], n1[:, :256])
    e = back(wide, wide + 256) * slope(scaled(h, n1[:, :256]))
    e_lat[...] = e
    add_sums(step, acc, 0, (eighth(e), eighth(e * h)))
    close_sums(step, acc, sums, (), n, ticks, *swap)


def stage8b(pieces, d_proj, lat_pre, n1, first, proj, last_term, first_term, n):
    rows = pieces.shape[0]
    terms = [six(v, n) if n > 1 else v for v in (last_term, first_term)]
    parts = [(v.shape[0] // n, v.shape[1]) for v in (last_term, first_term)]
    return run(functools.partial(body8b, n), rows,
        [(a, "rows") for a in (pieces, d_proj, lat_pre)] + [(a, "all") for a in (n1, first, proj)] + [(v, "any") for v in terms],
        [((rows, 1024), bf16, "rows"), ((rows, 256), f32, "rows"), ((2, 256), f32, "all")] + [(part, f32, "all") for part in parts],
        [pltpu.VMEM((2, 8, 256), f32)] + (scatter_scratch(parts, n) if n > 1 else []), n, (2, 256), 9)


def lanes_at(v, source, target):
    moved = pltpu.roll(v, (target - source) % 128, 1) if target != source else v
    lane = lax.broadcasted_iota(jnp.int32, v.shape, 1)
    return jnp.where((lane >= target) & (lane < target + 32), moved, 0.0)


def pack_fast(out, band, fproj, flast, fmid):
    places_of = (
        ((0, 0, 1), (0, 1, 2), (0, 2, 3), (1, 3, 0)),
        ((0, 0, 0), (0, 1, 1), (0, 2, 2), (0, 3, 3)),
        ((0, 1, 0), (0, 2, 1), (0, 3, 2), (2, 0, 3)),
    )
    for tap in range(3):
        out[32 * tap : 32 * (tap + 1)] = sum(
            band[128 * part + 32 * j : 128 * part + 32 * (j + 1), 128 * k : 128 * (k + 1)] for part, k, j in places_of[tap])
    out[96:224] = fproj[...]
    out[224:256] = sum(flast[32 * k : 32 * (k + 1), 128 * k : 128 * (k + 1)] for k in range(4))
    for group in range(3):
        total = None
        for tap in range(4 * group, min(4 * group + 4, 9)):
            for k in range(4):
                turned = fmid[:, 128 * tap : 128 * (tap + 1)].T
                v = lanes_at(turned[32 * k : 32 * (k + 1)], 32 * k, 32 * (tap % 4))
                total = v if total is None else total + v
        out[256 + 32 * group : 288 + 32 * group] = total
    out[352:384] = jnp.zeros((32, 128), f32)


def own_pair(out, sums, lo, hi, row):
    share = out.shape[1]
    back = lax.rem(hi - lo - lax.axis_index("fsdp") * share, hi - lo)
    for at, k in enumerate((row, 0)):
        wide = jnp.broadcast_to(sums[k : k + 1, lo:hi], (8, hi - lo))
        out[at : at + 1] = pltpu.roll(wide, back, 1)[0:1, :share]


def body9(n, total, fast4, lat_pre, e_lat, fone_pre, e_fone, d_fproj, ready, n1, s5, s6, s7, s8, lat, band, fproj, mask, flast_term, fmid_term,
          ready_first, ready_middle, ready_last, ready_proj, lat_term, packed, raw, slow_grad, lat_n, one_n, two_n, out_n, proj_n, mid_n, fout_n,
          first_grad, middle_grad, last_grad, proj_grad, wide, lat_acc, whole, band_term, fproj_term):
    step = pl.program_id(0)
    clear_first(step, lat_acc, band_term, fproj_term)
    slow_grad[...] = ready[...]
    rows = fast4.shape[0]
    def backward(e, pre, p, s):
        d = input_grad(e[...], normed(pre[...], p), p, s[0:1], s[1:2])
        w = d.astype(f32)
        return d, pltpu.roll(masked(w, mask[0]), rows - 1, 0).astype(bf16), pltpu.roll(masked(w, mask[1]), 1, 0).astype(bf16)
    d, before, _ = backward(e_lat, lat_pre, n1[:, :256], s8[...] * (1.0 / total))
    f, fbefore, fafter = backward(e_fone, fone_pre, n1[:, 256:384], s7[:, 256:] * (0.25 / total))
    narrow = jnp.concatenate([f, fbefore, fafter], axis=1)
    lat_acc[:, :256] += dot_tn(before, fast4[:, 256:])
    lat_acc[:, 256:] += dot_tn(d, fast4[:, :384])
    band_term[...] += dot_tn(narrow, fast4[...])
    for k in range(4):
        fproj_term[...] += dot_tn(fast4[:, 128 * k : 128 * (k + 1)], d_fproj[:, 128 * k : 128 * (k + 1)])
    base = dot_nt(narrow, band[...])
    skip = jnp.concatenate([dot_nt(d_fproj[:, 256 * k : 256 * (k + 1)], fproj[...]) for k in range(2)], axis=1)
    whole[...] = base + skip
    whole[:, :384] += dot(d, lat[:, 256:])
    whole[:, 256:] += dot(before, lat[:, :256])
    join_fours(whole[...], wide, raw)

    @pl.when(step == STEPS - 1)
    def _():
        lat_term[...] = lat_acc[...].astype(bf16)
        for grad, found in ((first_grad, ready_first), (middle_grad, ready_middle), (last_grad, ready_last), (proj_grad, ready_proj)):
            grad[...] = found[...]
        pack_fast(packed, band_term, fproj_term, flast_term, fmid_term)
        if n > 1:
            own_pair(lat_n, s8, 0, 256, 1)
            own_pair(one_n, s7, 0, 256, 1)
            own_pair(two_n, s6, 0, 256, 1)
            own_pair(out_n, s5, 0, 1024, 1)
            own_pair(proj_n, s5, 0, 1024, 2)
        for j, (sums, lo, row) in enumerate(((s7, 256, 1), (s6, 256, 1))):
            mid_n[j, 0:1] = sums[row : row + 1, lo : lo + 32]
            mid_n[j, 1:2] = sums[0:1, lo : lo + 32]
        for j in range(2):
            fout_n[j, 0:1] = s5[j + 1 : j + 2, 1024:1152]
            fout_n[j, 1:2] = s5[0:1, 1024:1152]


def stage9(total, fast4, lat_pre, e_lat, fone_pre, e_fone, d_fproj, ready, n1, s5, s6, s7, s8, lat, band, fproj, mask, flast_term, fmid_term, grads, n):
    rows = fast4.shape[0]
    part = rows // STEPS
    return run(functools.partial(body9, n, total), rows,
        [(a, "rows") for a in (fast4, lat_pre, e_lat, fone_pre, e_fone, d_fproj, ready)]
        + [(a, "all") for a in (n1, s5, s6, s7, s8, lat, band, fproj, mask, flast_term, fmid_term) + tuple(grads)],
        [((256, 640), bf16, "all"), ((384, 128), f32, "all"), ((rows // 16, 64, 128), bf16, "rows"), (ready.shape, bf16, "rows")]
        + [((2, 256 // n), f32, "all")] * 3 + [((2, 1024 // n), f32, "all")] * 2 + [((2, 2, 32), f32, "all"), ((2, 2, 128), f32, "all")] + [(v.shape, f32, "all") for v in grads],
        [pltpu.VMEM((part * 4, 128), f32), pltpu.VMEM((256, 640), f32), pltpu.VMEM((part, 512), f32),
         pltpu.VMEM((384, 512), f32), pltpu.VMEM((128, 128), f32)])


def body10(n, lat_term, packed, lat_grad, first_t, middle_t, last, proj, sums, slots, line, mine, lat_slots, lat_line, lat_mine,
           a_send, a_recv, b_send, b_recv, g_send, g_recv, l_send, l_recv, m_send, m_recv):
    me = lax.axis_index("fsdp")
    mi, mo, depth = lax.rem(me, INNER), lax.div(me, INNER), n // INNER
    peers = [mo * INNER + lax.rem(mi + k, INNER) for k in range(INNER)]
    spots = [lax.rem(mi + k, INNER) for k in range(INNER)]
    beyond = [lax.rem(mo + k, depth) for k in range(depth)]

    def remote(src, dst, send, recv, peer):
        copy = pltpu.make_async_remote_copy(
            src_ref=src, dst_ref=dst, send_sem=send, recv_sem=recv, device_id=(peer,), device_id_type=MESH)
        copy.start()
        return copy

    greet(n)
    greeted(n)
    fast = [remote(packed.at[spots[k]], slots.at[mi], a_send.at[k], a_recv.at[k], peers[k]) for k in range(1, INNER)]
    slow = [remote(lat_term.at[:, spots[k]], lat_slots.at[mi], l_send.at[k], l_recv.at[k], peers[k]) for k in range(1, INNER)]
    slots[mi] = packed[mi]
    lat_slots[mi] = lat_term[:, mi]
    for copy in fast:
        copy.wait()
    mine[...] = sum(slots[k] for k in range(1, INNER)) + slots[0]
    fast = [remote(mine, line.at[mo], b_send.at[k], b_recv.at[k], beyond[k] * INNER + mi) for k in range(1, depth)]
    line[mo] = mine[...]
    for copy in slow:
        copy.wait()
    lat_mine[...] = sum(lat_slots[k].astype(f32) for k in range(INNER)).astype(bf16)
    slow = [remote(lat_mine.at[beyond[k]], lat_line.at[mo], m_send.at[k], m_recv.at[k], beyond[k] * INNER + mi) for k in range(1, depth)]
    lat_line[mo] = lat_mine[mo]
    for copy in fast:
        copy.wait()
    sums[mi] = sum((line[k] for k in range(1, depth)), line[0])
    fast = [remote(sums.at[mi], sums.at[mi], g_send.at[k], g_recv.at[k], peers[k]) for k in range(1, INNER)]
    for copy in slow:
        copy.wait()
    lat_grad[...] = sum(lat_line[k].astype(f32) for k in range(depth))
    for copy in fast:
        copy.wait()

    high = sums.shape[1]
    def rows_of(lo, hi):
        found = []
        while lo < hi:
            top = min(hi, (lo // high + 1) * high)
            found.append(sums[lo // high, lo % high : lo % high + top - lo])
            lo = top
        return jnp.concatenate(found, axis=0) if len(found) > 1 else found[0]

    for k in range(3):
        first_t[:, 128 * k : 128 * (k + 1)] = rows_of(32 * k, 32 * (k + 1))
        wide = min(128, 288 - 128 * k)
        middle_t[:, 128 * k : 128 * k + wide] = rows_of(256 + 32 * k, 288 + 32 * k)[:, :wide]
    proj[...] = rows_of(96, 224)
    last[...] = rows_of(224, 256)


def stage10(lat_term, packed, n):
    depth, DS = n // INNER, pltpu.SemaphoreType.DMA
    packed = packed.reshape(INNER, -1, 128)
    chunk = packed.shape[1:]
    share = (lat_term.shape[0] // n, lat_term.shape[1])
    lat_grad, first_t, middle_t, last, proj = pl.pallas_call(
        functools.partial(body10, n),
        in_specs=[pl.BlockSpec(memory_space=pltpu.VMEM)] * 2,
        out_specs=[pl.BlockSpec(memory_space=pltpu.VMEM)] * 5,
        out_shape=[jax.ShapeDtypeStruct(shape, f32) for shape in (share, (32, 384), (32, 288), (32, 128), (128, 128))],
        scratch_shapes=[pltpu.VMEM((INNER,) + chunk, f32), pltpu.VMEM((INNER,) + chunk, f32), pltpu.VMEM((depth,) + chunk, f32), pltpu.VMEM(chunk, f32),
            pltpu.VMEM((INNER, depth) + share, bf16), pltpu.VMEM((depth,) + share, bf16), pltpu.VMEM((depth,) + share, bf16)]
        + [DS((INNER,)), DS((INNER,)), DS((depth,)), DS((depth,)), DS((INNER,)), DS((INNER,)), DS((INNER,)), DS((INNER,)), DS((depth,)), DS((depth,))],
        compiler_params=pltpu.CompilerParams(collective_id=10, has_side_effects=True),
    )(lat_term.reshape((depth, INNER) + share), packed)
    lat_grad, first_t, middle_t, last, proj = stage11((lat_grad, first_t, middle_t, last, proj))
    return lat_grad, (first_t.T, middle_t.T, last, proj)


def body11(*refs):
    half = len(refs) // 2
    for source, target in zip(refs[:half], refs[half:]):
        target[...] = source[...]


def stage11(arrays):
    VM = pl.BlockSpec(memory_space=pltpu.VMEM)
    return pl.pallas_call(
        body11,
        in_specs=[VM] * len(arrays),
        out_specs=[VM] * len(arrays),
        out_shape=[jax.ShapeDtypeStruct(v.shape, v.dtype) for v in arrays],
    )(*arrays)


def shards(slow_in, fast_in, clip_ids, lateral_weight, first_weight, middle_weight, last_weight, proj_weight,
           lat_norm, one_norm, two_norm, out_norm, proj_norm, fast_first, fast_middle, fast_last, fast_proj,
           fast_mid_norm, fast_out_norm, slow_cot, fast_cot):
    n = lax.axis_size("fsdp")
    side = slow_in.shape[1]
    count = slow_in.shape[0] * side * side * n
    lat, first, spair, band, fproj, fmid, flast, fpair, mask = stage0(
        lateral_weight.T, first_weight, (lat_norm, one_norm, two_norm, out_norm, proj_norm),
        (fast_first.T, fast_middle.T, fast_last, fast_proj, fast_mid_norm, fast_out_norm), clip_ids, n)
    lat = gathered(lat, n)

    def rows(v):
        return v.transpose(1, 2, 0, 3).reshape(-1, v.shape[3])
    def unrows(v):
        return v.reshape(side, side, -1, v.shape[1]).transpose(2, 0, 1, 3)
    def raw(v):
        return v.transpose(1, 2, 0, 3).reshape(side * side, -1, v.shape[3])
    def unraw(v):
        return v.reshape((side, side) + v.shape[1:]).transpose(2, 0, 1, 3)

    slow = rows(slow_in)
    fast4, lat_pre, fone_pre, n1, first, *held = stage1(
        raw(fast_in), lat, band, fproj, mask, spair, fpair, first, (middle_weight, last_weight), n)
    first = gathered(first, n).reshape(3, -1, first_weight.shape[1])
    lateral, one_pre, ftwo_pre, n2, middle, last, proj = stage2(
        slow, lat_pre, fone_pre, n1, first, fmid, mask, spair, fpair, held, proj_weight, side, n)
    middle = gathered(middle, n)
    two_pre, ftwo, n3, last, proj = stage3(one_pre, ftwo_pre, n2, middle, flast, spair, fpair, (last, proj), side, n)
    last, proj = gathered(last, n), gathered(proj, n)
    two, proj_pre, n4 = stage4(two_pre, slow, lateral, n3, last, proj, spair, n)
    slow_out, fast_out, delta, fdelta, local = stage5(
        two, proj_pre, rows(slow_cot), fast4, ftwo, raw(fast_cot), n1, n3, n4, last, fproj, flast)
    s5 = stage5x(local, n)
    d_proj, d_fproj, last_term, proj_term, flast_term, e_two, e_ftwo, s6 = stage6(
        count, two, two_pre, proj_pre, slow, lateral, delta, fast4, ftwo, ftwo_pre, fdelta, n1, n2, n3, n4, s5, last, fproj, flast, n)
    middle_term, fmid_term, e_one, e_fone, s7, proj_grad = stage7(
        count, one_pre, two_pre, e_two, fone_pre, ftwo_pre, e_ftwo, n1, n2, n3, s6, middle, fmid, proj_term, side, n)
    first_term, pieces, middle_grad = stage8(count, slow, lateral, one_pre, e_one, n2, s7, mask, middle_term.reshape(-1, 256), n)
    slow_grad, e_lat, s8, last_grad, first_grad = stage8b(
        pieces, d_proj, lat_pre, n1, first, proj, last_term, first_term.reshape(-1, 256), n)
    lat_term, packed, fast_grad, slow_grad, *small = stage9(
        count, fast4, lat_pre, e_lat, fone_pre, e_fone, d_fproj, slow_grad, n1, s5, s6, s7, s8, lat, band, fproj, mask, flast_term, fmid_term,
        (first_grad, middle_grad, last_grad, proj_grad), n)
    lateral_grad, fast_grads = stage10(lat_term, packed, n)
    return (unrows(slow_out), unraw(fast_out), unrows(slow_grad), unraw(fast_grad),
            lateral_grad.T, *small[7:],
            *small[:5], *fast_grads, *small[5:7])


def solution(mesh):
    in_specs = (
        P("fsdp", None, None, None),
        P("fsdp", None, None, None),
        P("fsdp", None),
        P(None, "fsdp"),
        P("fsdp", None),
        P("fsdp", None),
        P("fsdp", None),
        P("fsdp", None),
        P(None, "fsdp"),
        P(None, "fsdp"),
        P(None, "fsdp"),
        P(None, "fsdp"),
        P(None, "fsdp"),
        P(),
        P(),
        P(),
        P(),
        P(),
        P(),
        P("fsdp", None, None, None),
        P("fsdp", None, None, None),
    )
    out_specs = (
        P("fsdp", None, None, None),
        P("fsdp", None, None, None),
        P("fsdp", None, None, None),
        P("fsdp", None, None, None),
        P(None, "fsdp"),
        P("fsdp", None),
        P("fsdp", None),
        P("fsdp", None),
        P("fsdp", None),
        P(None, "fsdp"),
        P(None, "fsdp"),
        P(None, "fsdp"),
        P(None, "fsdp"),
        P(None, "fsdp"),
        P(),
        P(),
        P(),
        P(),
        P(),
        P(),
    )
    return jax.shard_map(shards, mesh=mesh, in_specs=in_specs, out_specs=out_specs, check_vma=False)
```

```python
import functools

import jax
import jax.numpy as jnp
import numpy as np
from jax import lax
from jax.experimental import pallas as pl
from jax.experimental.pallas import tpu as pltpu
from jax.sharding import PartitionSpec as P

EPSILON = 1e-05


MESH = pl.DeviceIdType.MESH


f32 = jnp.float32
bf16 = jnp.bfloat16
STEPS = 7
STRIP = 32


def dot(a, b):
    return lax.dot_general(a, b, (((1,), (0,)), ((), ())), preferred_element_type=f32)


def dot_nt(a, b):
    return lax.dot_general(a, b, (((1,), (1,)), ((), ())), preferred_element_type=f32)


def dot_tn(a, b):
    return lax.dot_general(a, b, (((0,), (0,)), ((), ())), preferred_element_type=f32)


def shift(v, mask, by):
    rows = v.shape[0]
    moved = pltpu.roll(v, by % rows, 0)
    return masked(moved, mask)


def masked(v, mask):
    return (v.reshape(-1, mask.shape[0], v.shape[1]) * mask[None, :, : v.shape[1]]).reshape(v.shape)


def sigma(x):
    return 0.5 + 0.5 * jnp.tanh(0.5 * x)


def silu(x):
    return x * sigma(x)


def slope(x):
    s = sigma(x)
    return s * (1.0 + x * (1.0 - s))


def normed(z, n):
    return (z - n[0:1]) * n[1:2]


def scaled(hat, n):
    return hat * n[2:3] + n[3:4]


def acted(z, n):
    return scaled(normed(z, n), n)


def input_grad(e, hat, n, s_mean, s_cross):
    return ((n[2:3] * n[1:2]) * (e - s_mean - hat * s_cross)).astype(bf16)


def eighth(v):
    return jnp.sum(v.reshape(-1, 8, v.shape[1]), axis=0)


def clear_first(step, *refs):
    @pl.when(step == 0)
    def _():
        for ref in refs:
            ref[...] = jnp.zeros(ref.shape, ref.dtype)


def add_moments(step, acc, lo, z):
    hi = lo + z.shape[1]
    high = z.shape[0] // 8
    deep = z.reshape(high, 8, hi - lo)
    own = jnp.sum(deep, axis=0) * (1.0 / high)
    off = deep - own[None]
    spread_of = jnp.sum(off * off, axis=0)
    past = step.astype(f32)
    share = 1.0 / (past + 1.0)
    gap = own - acc[0, :, lo:hi]
    acc[0, :, lo:hi] += gap * share
    acc[1, :, lo:hi] += spread_of + gap * gap * (past * share * high)


def add_sums(step, acc, lo, parts):
    hi = lo + parts[0].shape[1]
    for k, part in enumerate(parts):
        acc[k, :, lo:hi] += part


def split_fours(raw, wide):
    rows = wide.shape[0]
    wide[...] = raw[...].astype(f32).reshape(rows, 128)
    return jnp.concatenate([wide[pl.ds(k, rows // 4, stride=4), :] for k in range(4)], axis=1)


def join_fours(value, wide, raw):
    rows = wide.shape[0]
    for k in range(4):
        wide[pl.ds(k, rows // 4, stride=4), :] = value[:, 128 * k : 128 * (k + 1)]
    raw[...] = wide[...].astype(bf16).reshape(raw.shape)


def clear(grid):
    grid[...] = jnp.zeros(grid.shape, grid.dtype)


def fill(grid, side, value, block):
    per = side // STEPS
    line = value.shape[0] // per
    frames = line // side
    for r in range(per):
        at = ((block * per + r + 1) * (side + 2) + 1) * frames
        grid[pl.ds(pl.multiple_of(at, 16), line), :] = value[r * line : (r + 1) * line]


def tap_columns(grid, side, step, rows, flip):
    per = side // STEPS
    line = rows // per
    frames = line // side
    lines = []
    for r in range(per):
        pieces = []
        for a in range(3):
            for b in range(3):
                ra, rb = (2 - a, 2 - b) if flip else (a, b)
                at = ((step * per + r + ra) * (side + 2) + rb) * frames
                pieces.append(grid[pl.ds(pl.multiple_of(at, 16), line), :])
        lines.append(jnp.concatenate(pieces, axis=1))
    return jnp.concatenate(lines, axis=0)


INNER = 8


def greet(n):
    me = lax.axis_index("fsdp")
    mi, mo, depth = lax.rem(me, INNER), lax.div(me, INNER), n // INNER
    barrier = pltpu.get_barrier_semaphore()
    for k in range(1, INNER):
        pl.semaphore_signal(barrier, inc=1, device_id=(mo * INNER + lax.rem(mi + k, INNER),), device_id_type=MESH)
    for k in range(1, depth):
        pl.semaphore_signal(barrier, inc=1, device_id=(lax.rem(mo + k, depth) * INNER + mi,), device_id_type=MESH)


def greeted(n):
    pl.semaphore_wait(pltpu.get_barrier_semaphore(), INNER - 1 + n // INNER - 1)


def total_of(n, centred, own, near, far, mid, near_send, near_recv, far_send, far_recv):
    me = lax.axis_index("fsdp")
    mi, mo, depth = lax.rem(me, INNER), lax.div(me, INNER), n // INNER

    def swap(src, slots, sends, recvs, mine, size, peer):
        copies = []
        for k in range(1, size):
            copy = pltpu.make_async_remote_copy(
                src_ref=src, dst_ref=slots.at[mine], send_sem=sends.at[k], recv_sem=recvs.at[k],
                device_id=(peer(k),), device_id_type=MESH)
            copy.start()
            copies.append(copy)
        slots[mine] = src[...]
        for copy in copies:
            copy.wait()

    def merge(slots, size):
        if not centred:
            return sum(slots[k] for k in range(1, size)) + slots[0]
        mean = sum(slots[k, 0:1] for k in range(size)) * (1.0 / size)
        off = [slots[k, 0:1] - mean for k in range(size)]
        return jnp.concatenate([mean, sum(slots[k, 1:2] + off[k] * off[k] for k in range(size)) * (1.0 / size)], axis=0)

    swap(own, near, near_send, near_recv, mi, INNER, lambda k: mo * INNER + lax.rem(mi + k, INNER))
    mid[...] = merge(near, INNER)
    if depth == 1:
        return mid[...]
    swap(mid, far, far_send, far_recv, mo, depth, lambda k: lax.rem(mo + k, depth) * INNER + mi)
    return merge(far, depth)


def over_groups(part, width):
    lanes = part.shape[1]
    if width < 128:
        wide = jnp.broadcast_to(part, (8, lanes))
        total = wide
        for k in range(1, lanes // width):
            total = total + pltpu.roll(wide, k * width, 1)
        return total[0:1]
    total = sum(part[:, k : k + width] for k in range(0, lanes, width))
    return jnp.concatenate([total] * (lanes // width), axis=1)


def norm_pack(total, pairs, out, folds):
    out[0:2] = total
    for lo, hi, width in folds:
        groups = width / (hi - lo)
        mean = over_groups(total[0:1, lo:hi], width) * groups
        off = total[0:1, lo:hi] - mean
        out[0:1, lo:hi] = mean
        out[1:2, lo:hi] = over_groups(total[1:2, lo:hi] + off * off, width) * groups
    out[1:2] = lax.rsqrt(out[1:2] + EPSILON)
    at = 0
    for pair, lo, hi in pairs:
        out[2:4, at : at + hi - lo] = pair[:, lo:hi]
        at += hi - lo


def sum_pack(total, out, folds):
    out[...] = total
    for lo, hi, width in folds:
        for k in range(out.shape[0]):
            out[k : k + 1, lo:hi] = over_groups(total[k : k + 1, lo:hi], width)


def swap_scratch(shape, n):
    DS, depth = pltpu.SemaphoreType.DMA, n // INNER
    return [pltpu.VMEM((INNER,) + shape, f32), pltpu.VMEM((depth,) + shape, f32), pltpu.VMEM(shape, f32),
        DS((INNER,)), DS((INNER,)), DS((depth,)), DS((depth,))]


def run(body, rows, ins, outs, scratch, n=1, swap=None, call=None, same=None):
    def spec(shape, how):
        if how == "any":
            return pl.BlockSpec(memory_space=pl.ANY)
        if how == "rows":
            return pl.BlockSpec((shape[0] // STEPS,) + tuple(shape[1:]), lambda i, d=len(shape): (i,) + (0,) * (d - 1))
        return pl.BlockSpec(tuple(shape), lambda i, d=len(shape): (0,) * d, pipeline_mode=pl.Buffered(1))
    def out_spec(shape, how):
        if how in ("rows", "any"):
            return spec(shape, how)
        return pl.BlockSpec(tuple(shape), lambda i, d=len(shape): (0,) * d)
    extra = {}
    if swap is not None:
        scratch = scratch + [pltpu.VMEM(swap, f32)]
    if n > 1 and swap is not None:
        scratch = scratch + swap_scratch(swap, n)
    if n > 1 and call is not None:
        extra = dict(collective_id=call, has_side_effects=True)
    return pl.pallas_call(
        body,
        grid=(STEPS,),
        in_specs=[spec(a.shape, how) for a, how in ins],
        out_specs=[out_spec(shape, how) for shape, _, how in outs],
        out_shape=[jax.ShapeDtypeStruct(shape, kind) for shape, kind, _ in outs],
        scratch_shapes=scratch,
        input_output_aliases=same or {},
        compiler_params=pltpu.CompilerParams(dimension_semantics=("arbitrary",), vmem_limit_bytes=58 * 1024 * 1024, **extra),
    )(*[a for a, _ in ins])


def close_moments(step, acc, pairs, out, count, folds, n, ticks, own, *links):
    @pl.when(step == STEPS - 1)
    def _():
        mean = jnp.mean(acc[0], axis=0, keepdims=True)
        off = acc[0] - mean
        own[0:1] = mean
        own[1:2] = jnp.sum(acc[1], axis=0, keepdims=True) * (1.0 / count) + jnp.mean(off * off, axis=0, keepdims=True)
        if n > 1:
            ticks[3]()
            norm_pack(total_of(n, True, own, *links), pairs, out, folds)
            ticks[4]()
        else:
            norm_pack(own[...], pairs, out, folds)


def close_sums(step, acc, out, folds, n, ticks, own, *links):
    if n > 1 and not ticks:
        @pl.when(step == 0)
        def _():
            greet(n)

    @pl.when(step == STEPS - 1)
    def _():
        for k in range(acc.shape[0]):
            own[k : k + 1] = jnp.sum(acc[k], axis=0, keepdims=True)
        if n > 1:
            if ticks:
                ticks[3]()
            else:
                greeted(n)
            sum_pack(total_of(n, False, own, *links), out, folds)
            if ticks:
                ticks[4]()
        else:
            sum_pack(own[...], out, folds)


def places():
    me = lax.axis_index("fsdp")
    return lax.div(me, 8), lax.rem(lax.div(me, 4), 2), lax.rem(lax.div(me, 2), 2), lax.rem(me, 2)


def flat(z, y, x, c):
    return ((z * 2 + y) * 2 + x) * 2 + c


def six(term, n):
    return term.reshape((n // 8, 2, 2, 2, term.shape[0] // n) + term.shape[1:])


def halves(width):
    if width < 256:
        return ((0, width),)
    middle = width // 256 * 128
    return ((0, middle), (middle, width))


def scatter_scratch(parts, n):
    depth, k, DS = n // 8, len(parts), pltpu.SemaphoreType.DMA
    def buf(lead):
        return [pltpu.VMEM(lead + part, bf16) for part in parts]
    return (buf((depth, 2, 2)) + buf((depth, 2, 2)) + buf((depth, 2)) + buf((depth,)) + buf((depth,))
        + [DS((k,)), DS((k, 2)), DS((k, 2, 2)), DS((k, 2, 2)), DS((k, depth)), DS((k, depth))])


def scatter_ticks(n, ins, outs, rest):
    k, depth = len(ins), n // 8
    half, r1, r2, r3, r4 = (rest[j * k : (j + 1) * k] for j in range(5))
    own_sem, c_sem, p_sem, q_sem, z_send, z_recv = rest[5 * k :]
    z, y, x, c = places()
    core, over_x, over_y = flat(z, y, x, 1 - c), flat(z, y, 1 - x, c), flat(z, 1 - y, x, c)
    line = [flat(lax.rem(z + s, depth), y, x, c) for s in range(depth)]
    spots = [lax.rem(z + s, depth) for s in range(depth)]

    def remote(src, dst, send, recv, peer):
        return pltpu.make_async_remote_copy(
            src_ref=src, dst_ref=dst, send_sem=send, recv_sem=recv, device_id=(peer,), device_id_type=MESH)
    def sides(i):
        return tuple(enumerate(halves(half[i].shape[-1])))
    def own(i):
        return pltpu.make_async_copy(ins[i].at[:, :, :, c], half[i], own_sem.at[i])
    def to_core(i):
        return remote(ins[i].at[:, :, :, 1 - c], r1[i], c_sem.at[i, 0], c_sem.at[i, 1], core)
    def to_first(i, t, lo, hi):
        src, peer = (half[i].at[:, :, 1 - x, :, lo:hi], over_x) if t == 0 else (half[i].at[:, 1 - y, :, :, lo:hi], over_y)
        return remote(src, r2[i].at[:, :, :, lo:hi], p_sem.at[i, t, 0], p_sem.at[i, t, 1], peer)
    def to_second(i, t, lo, hi):
        src, peer = (half[i].at[:, 1 - y, x, :, lo:hi], over_y) if t == 0 else (half[i].at[:, y, 1 - x, :, lo:hi], over_x)
        return remote(src, r3[i].at[:, :, lo:hi], q_sem.at[i, t, 0], q_sem.at[i, t, 1], peer)
    def to_line(i, s):
        return remote(half[i].at[spots[s], y, x], r4[i].at[s], z_send.at[i, s], z_recv.at[i, s], line[s])
    def add(target, other):
        target[...] = (target[...].astype(f32) + other[...].astype(f32)).astype(target.dtype)

    def begin():
        for i in range(k):
            own(i).start()
            to_core(i).start()
    def first():
        for i in range(k):
            own(i).wait()
            to_core(i).wait()
            @pl.loop(0, depth)
            def _(zz, i=i):
                for a in range(2):
                    for b in range(2):
                        add(half[i].at[zz, a, b], r1[i].at[zz, a, b])
            for t, (lo, hi) in sides(i):
                to_first(i, t, lo, hi).start()
    def second():
        for i in range(k):
            for t, (lo, hi) in sides(i):
                to_first(i, t, lo, hi).wait()
                @pl.loop(0, depth)
                def _(zz, i=i, t=t, lo=lo, hi=hi):
                    for o in range(2):
                        target = half[i].at[zz, o, x] if t == 0 else half[i].at[zz, y, o]
                        add(target.at[:, lo:hi], r2[i].at[zz, o, :, lo:hi])
                to_second(i, t, lo, hi).start()
    def third():
        for i in range(k):
            for t, (lo, hi) in sides(i):
                to_second(i, t, lo, hi).wait()
            @pl.loop(0, depth)
            def _(zz, i=i):
                add(half[i].at[zz, y, x], r3[i].at[zz])
            for s in range(1, depth):
                to_line(i, s).start()
    def finish():
        for i in range(k):
            outs[i][...] = half[i][z, y, x].astype(f32)
            for s in range(1, depth):
                to_line(i, s).wait()
                outs[i][...] += r4[i][s].astype(f32)
    return begin, first, second, third, finish


GATHER_SEMS = 9


def gather_scratch(k, n):
    DS, depth = pltpu.SemaphoreType.DMA, n // 8
    return [DS((1,)), DS((depth,)), DS((depth,)), DS((2, 2)), DS((2, 2)), DS((2, 3)), DS((2, 3)), DS((8,)), DS((8,))] * k


class Moves:
    def __init__(self, n, shard, whole, sems):
        self.n, self.shard, self.whole, self.sems = n, shard, whole, sems
        self.at = places()
        self.sides = tuple(enumerate(halves(whole.shape[-1])))

    def remote(self, src, dst, send, recv, *peer):
        return pltpu.make_async_remote_copy(
            src_ref=src, dst_ref=dst, send_sem=send, recv_sem=recv, device_id=(flat(*peer),), device_id_type=MESH)

    def part(self, name, t, lo, hi):
        z, y, x, c = self.at
        index = {
            "p": (slice(None), y, x, c),
            "q": (slice(None), y, slice(None), c) if t == 0 else (slice(None), slice(None), x, c),
            "c1": (slice(None), y, 1 - x, c) if t == 0 else (slice(None), 1 - y, x, c),
            "c2": (slice(None), 1 - y, slice(None), c) if t == 0 else (slice(None), slice(None), 1 - x, c),
        }["p" if name == "c0" else name]
        return self.whole.at[index + (slice(None), slice(lo, hi))]

    def copies(self, name):
        z, y, x, c = self.at
        own, z_send, z_recv, p, q, c_send, c_recv, d_send, d_recv = self.sems
        depth = self.n // 8
        if name == "z":
            mine = self.whole.at[z, y, x, c]
            return [pltpu.make_async_copy(self.shard, mine, own.at[0])] + [
                self.remote(self.shard, mine, z_send.at[s], z_recv.at[s], lax.rem(z + s, depth), y, x, c) for s in range(1, depth)]
        if name == "d":
            mine = self.whole.at[:, y, x, c]
            found = []
            for k in range(1, 8):
                other = lax.rem((y * 2 + x) * 2 + c + k, 8)
                found.append(self.remote(mine, mine, d_send.at[k], d_recv.at[k], z, 0, 0, other))
            return found
        found = []
        for t, (lo, hi) in self.sides:
            src = self.part(name, t, lo, hi)
            if name[0] == "c":
                j = int(name[1])
                found.append(self.remote(src, src, c_send.at[t, j], c_recv.at[t, j], z, y, x, 1 - c))
                continue
            sem = p if name == "p" else q
            peer = (z, y, 1 - x, c) if (t == 0) == (name == "p") else (z, 1 - y, x, c)
            found.append(self.remote(src, src, sem.at[t, 0], sem.at[t, 1], *peer))
        return found

    def start(self, *names):
        for name in names:
            for copy in self.copies(name):
                copy.start()

    def wait(self, *names):
        for name in names:
            for copy in self.copies(name):
                copy.wait()


def moves(n, shards, wholes, rest):
    return [Moves(n, shard, whole, rest[GATHER_SEMS * i : GATHER_SEMS * (i + 1)]) for i, (shard, whole) in enumerate(zip(shards, wholes))]


def spread_shapes(shards, n):
    return [((n // 8, 2, 2, 2) + v.shape, v.dtype, "any") for v in shards]


def whole_shapes(wholes):
    return [(v.shape, v.dtype, "any") for v in wholes]


def gathered(v, n):
    return v.reshape((n * v.shape[4],) + v.shape[5:])


def at_lanes(v, offset):
    rows, width = v.shape
    wide = v if width == 128 else jnp.concatenate([v, jnp.zeros((rows, 128 - width), v.dtype)], axis=1)
    return pltpu.roll(wide, offset, 1) if offset else wide


def build_fast(first_t, middle_t, last, skip, mid_norm, out_norm, ids, band, fproj, fmid, flast, fpair, mask, lanes):
    band[...] = jnp.zeros(band.shape, bf16)
    fproj[...] = jnp.zeros(fproj.shape, bf16)
    flast[...] = jnp.zeros(flast.shape, bf16)
    none = jnp.zeros((96, 128), f32)
    for tap in range(3):
        block = jnp.concatenate([first_t[:, 128 * tap : 128 * (tap + 1)].astype(f32), none], axis=0).T
        placed = [pltpu.roll(block, 32 * j, 1) if j else block for j in range(4)]
        for part in range(3):
            for k in range(4):
                here = [j for j in range(4) if (j + tap - 1) % 4 == k and part == (1 if j + tap < 1 else 2 if j + tap > 4 else 0)]
                if here:
                    (j,) = here
                    band[128 * k : 128 * (k + 1), 128 * part : 128 * (part + 1)] += placed[j].astype(bf16)
    lanes[...] = jnp.zeros(lanes.shape, f32)
    lanes[:, :288] = middle_t[...].astype(f32)
    for group in range(3):
        block = jnp.concatenate([lanes[:, 128 * group : 128 * (group + 1)], none], axis=0).T
        for tap in range(4 * group, min(4 * group + 4, 9)):
            part = block[32 * (tap % 4) : 32 * (tap % 4 + 1)]
            for k in range(4):
                fmid[128 * tap + 32 * k : 128 * tap + 32 * (k + 1)] = (pltpu.roll(part, 32 * k, 1) if k else part).astype(bf16)
    for k in range(4):
        flast[32 * k : 32 * (k + 1), 128 * k : 128 * (k + 1)] = last[...]
    for k in range(2):
        fproj[128 * k : 128 * (k + 1), 128 * k : 128 * (k + 1)] = skip[...]
        narrow = at_lanes(mid_norm[k].astype(f32), 0)
        wide = jnp.concatenate([narrow] * 4, axis=0)
        fpair[:, 128 * k : 128 * (k + 1)] = sum(pltpu.roll(wide, 32 * j, 1) for j in range(1, 4))[:2] + narrow
        for j in range(4):
            fpair[:, 256 + 512 * k + 128 * j : 384 + 512 * k + 128 * j] = out_norm[k].astype(f32)
    frames = mask.shape[1]
    row = lax.broadcasted_iota(jnp.int32, (frames, frames), 0)
    column = lax.broadcasted_iota(jnp.int32, (frames, frames), 1)
    spread_ids = jnp.broadcast_to(ids[...].astype(f32), (frames, frames))
    def pick(by):
        return jnp.sum(jnp.where(column == row + by, spread_ids, 0.0), axis=1, keepdims=True)
    at = lax.broadcasted_iota(jnp.int32, (frames, 1), 0)
    here = pick(0)
    prev = jnp.where((here == pick(-1)) & (at > 0), 1.0, 0.0)
    after = jnp.where((here == pick(1)) & (at < frames - 1), 1.0, 0.0)
    mask[0] = jnp.broadcast_to(prev, mask.shape[1:])
    mask[1] = jnp.broadcast_to(after, mask.shape[1:])


def pack_norms(pairs, out):
    total, offset = None, 0
    for pair in pairs:
        v = at_lanes(jnp.concatenate([pair[...].astype(f32)] * 4, axis=0), offset)
        total = v if total is None else total + v
        offset += pair.shape[1]
    out[...] = total


def join_norms(gathered_of, shares, out):
    n = gathered_of.shape[0]
    offset, lo = 0, 0
    for share in shares:
        wide = share * n
        pick = lax.broadcasted_iota(jnp.int32, (128, wide), 0) == offset + lax.broadcasted_iota(jnp.int32, (128, wide), 1) % share
        pick = jnp.where(pick, 1.0, 0.0).astype(bf16)
        mine = lax.broadcasted_iota(jnp.int32, (n, wide), 0) == lax.broadcasted_iota(jnp.int32, (n, wide), 1) // share
        for row in range(2):
            each = dot(gathered_of[:, row, :].astype(bf16), pick)
            out[row : row + 1, lo : lo + wide] = jnp.sum(jnp.where(mine, each, 0.0), axis=0, keepdims=True)
        offset += share
        lo += wide


def body0(n, lat_shard, first_shard, p_lat, p_one, p_two, p_out, p_proj, first_t, middle_t, last_w, skip, mid_norm, out_norm, ids,
          lat_whole, first_whole, spair, band, fproj, fmid, flast, fpair, mask, own, norms_whole, lanes, *sems):
    lat, norms, first = moves(n, (lat_shard, own, first_shard), (lat_whole, norms_whole, first_whole), sems)
    pairs = (p_lat, p_one, p_two, p_out, p_proj)
    greet(n)
    pack_norms(pairs, own)
    greeted(n)
    for m in (lat, norms, first):
        m.start("z")
    build_fast(first_t, middle_t, last_w, skip, mid_norm, out_norm, ids, band, fproj, fmid, flast, fpair, mask, lanes)
    for m in (lat, norms):
        m.wait("z")
        m.start("d")
    first.wait("z")
    first.start("p", "c0")
    lat.wait("d")
    norms.wait("d")
    join_norms(norms_whole[...].reshape(n, 8, 128), [p.shape[1] for p in pairs], spair)
    first.wait("p", "c0")


def stage0(lat_shard, first_shard, pairs, fast, ids, n):
    VM, ANY = pl.BlockSpec(memory_space=pltpu.VMEM), pl.BlockSpec(memory_space=pl.ANY)
    shape_of = lambda shape, kind: jax.ShapeDtypeStruct(shape, kind)
    small = tuple(pairs) + tuple(fast) + (ids,)
    width = sum(p.shape[1] for p in pairs) * n
    return pl.pallas_call(
        functools.partial(body0, n),
        in_specs=[ANY, ANY] + [VM] * len(small),
        out_specs=[ANY, ANY] + [VM] * 7,
        out_shape=[shape_of(s, k) for s, k, _ in spread_shapes([lat_shard, first_shard], n)]
        + [shape_of((2, width), f32), shape_of((512, 384), bf16), shape_of((256, 256), bf16), shape_of((1152, 128), bf16),
           shape_of((128, 512), bf16), shape_of((2, 1280), f32), shape_of((2, ids.shape[1], 256), f32)],
        scratch_shapes=[pltpu.VMEM((8, 128), f32), pltpu.VMEM((n // 8, 2, 2, 2, 8, 128), f32), pltpu.VMEM((32, 384), f32)] + gather_scratch(3, n),
        compiler_params=pltpu.CompilerParams(collective_id=1, has_side_effects=True),
    )(lat_shard, first_shard, *small)


def run_ticks(step, n, ticks, at):
    @pl.when(step == 0)
    def _():
        greet(n)
    for j in range(3):
        @pl.when(step == at[j])
        def _(j=j):
            if j == 0:
                greeted(n)
            ticks[j]()


def strips(rows, width, body, init):
    return lax.fori_loop(0, rows // STRIP, lambda k, carry: body(pl.ds(pl.multiple_of(k * STRIP, STRIP), STRIP), carry), init, unroll=True)


FOLDS1 = ((256, 384, 32), (384, 896, 128))
FOLDS2 = ((256, 384, 32),)
FOLDS3 = ((256, 768, 128),)


def body1(n, raw, lat, band, fproj, mask, spair, fpair, held, *refs):
    shards, (fast4, lat_pre, fone_pre, n1), wholes, (wide, acc), rest = refs[:2], refs[2:6], refs[6:9], refs[9:11], refs[11:]
    step = pl.program_id(0)
    clear_first(step, acc)
    ticks, swap = (), rest
    if n > 1:
        first, *others = moves(n, (None,) + tuple(shards), wholes, rest)
        swap = rest[3 * GATHER_SEMS :]

        def begin():
            first.start("q", "c1")
            for m in others:
                m.start("z")
        def middle():
            first.wait("q")
            first.start("c2")
        def finish():
            first.wait("c1", "c2")
            for m in others:
                m.wait("z")
        ticks = (begin, middle, lambda: None, lambda: None, finish)
        run_ticks(step, n, ticks, (1, 4, 6))
    f = split_fours(raw, wide).astype(bf16)
    fast4[...] = f
    prev, nxt = mask[0], mask[1]
    z = dot_nt(f[:, :384], lat[:, 256:]) + shift(dot_nt(f[:, 256:], lat[:, :256]), prev, 1)
    lat_pre[...] = z
    add_moments(step, acc, 0, z)
    y = dot(f, band[...])
    z = y[:, :128] + shift(y[:, 128:256], prev, 1) + shift(y[:, 256:], nxt, -1)
    fone_pre[...] = z
    add_moments(step, acc, 256, z)
    z = jnp.concatenate([dot(f[:, :256], fproj[...]), dot(f[:, 256:], fproj[...])], axis=1)
    add_moments(step, acc, 384, z)
    close_moments(step, acc, ((spair, 0, 256), (fpair, 0, 128), (fpair, 768, 1280)), n1, f.shape[0] * STEPS, FOLDS1, n, ticks, *swap)


def stage1(raw, lat, band, fproj, mask, spair, fpair, held, shards_of, n):
    rows = raw.shape[0] * raw.shape[1] // 4
    return run(functools.partial(body1, n), rows,
        [(raw, "rows")] + [(v, "all") for v in (lat, band, fproj, mask, spair, fpair)] + [(v, "any") for v in (held,) + tuple(shards_of)],
        [((rows, 512), bf16, "rows"), ((rows, 256), f32, "rows"), ((rows, 128), f32, "rows"), ((4, 896), f32, "all")] + whole_shapes([held]) + spread_shapes(shards_of, n),
        [pltpu.VMEM((rows * 4 // STEPS, 128), f32), pltpu.VMEM((2, 8, 896), f32)] + (gather_scratch(3, n) if n > 1 else []), n, (2, 896), 2, {7: 4})


def body2(n, side, slow, lat_pre, fone_pre, n1, first, fmid, mask, spair, fpair, held_a, held_b, shard,
          lateral, one_pre, ftwo_pre, n2, whole_a, whole_b, whole_c, grid, acc, *rest):
    step = pl.program_id(0)
    rows = slow.shape[0]
    n_lat, n_fone = n1[:, :256], n1[:, 256:384]
    ticks, swap = (), rest
    if n > 1:
        middle, last, proj = moves(n, (None, None, shard), (whole_a, whole_b, whole_c), rest)
        swap = rest[3 * GATHER_SEMS :]

        def begin():
            middle.start("p", "c0")
            last.start("p", "c0")
            proj.start("z")
        def half():
            middle.wait("p")
            middle.start("q", "c1")
        def late():
            proj.wait("z")
            proj.start("p", "c0")
        def close():
            middle.wait("q")
            middle.start("c2")
        def finish():
            last.wait("p", "c0")
            proj.wait("p", "c0")
            middle.wait("c0", "c1", "c2")
        ticks = (begin, half, late, close, finish)
        run_ticks(step, n, ticks, (1, 3, 5))

    def put(block):
        part = fone_pre[pl.ds(pl.multiple_of(block * rows, 16), rows), :]
        fill(grid, side, silu(acted(part, n_fone)).astype(bf16), block)

    @pl.when(step == 0)
    def _():
        clear(grid)
        clear(acc)
        put(0)

    put(jnp.minimum(step + 1, STEPS - 1))
    lat = silu(acted(lat_pre[...], n_lat)).astype(bf16)
    lateral[...] = lat
    joined = jnp.concatenate([slow[...], lat], axis=1)
    z = dot(joined, first[1]) + shift(dot(joined, first[0]), mask[0], 1) + shift(dot(joined, first[2]), mask[1], -1)
    one_pre[...] = z
    add_moments(step, acc, 0, z)
    z = dot(tap_columns(grid, side, step, rows, False), fmid[...])
    ftwo_pre[...] = z
    add_moments(step, acc, 256, z)
    close_moments(step, acc, ((spair, 256, 512), (fpair, 128, 256)), n2, rows * STEPS, FOLDS2, n, ticks, *swap)


def stage2(slow, lat_pre, fone_pre, n1, first, fmid, mask, spair, fpair, held, shard, side, n):
    rows = slow.shape[0]
    frames = rows // side**2
    return run(functools.partial(body2, n, side), rows,
        [(slow, "rows"), (lat_pre, "rows")] + [(v, "all") for v in (fone_pre, n1, first, fmid, mask, spair, fpair)] + [(v, "any") for v in tuple(held) + (shard,)],
        [((rows, 256), bf16, "rows"), ((rows, 256), f32, "rows"), ((rows, 128), f32, "rows"), ((4, 384), f32, "all")] + whole_shapes(held) + spread_shapes([shard], n),
        [pltpu.VMEM(((side + 2) ** 2 * frames, 128), bf16), pltpu.VMEM((2, 8, 384), f32)] + (gather_scratch(3, n) if n > 1 else []), n, (2, 384), 3, {9: 4, 10: 5})


def body3(n, side, one_pre, ftwo_pre, n2, middle, flast, spair, fpair, held_a, held_b, two_pre, ftwo, n3, whole_a, whole_b, grid, acc, *rest):
    step = pl.program_id(0)
    rows = two_pre.shape[0]
    n_one, n_ftwo = n2[:, :256], n2[:, 256:]
    ticks, swap = (), rest
    if n > 1:
        both = moves(n, (None, None), (whole_a, whole_b), rest)
        swap = rest[2 * GATHER_SEMS :]

        def begin():
            for m in both:
                m.start("q", "c1")
        def half():
            for m in both:
                m.wait("q")
                m.start("c2")
        def finish():
            for m in both:
                m.wait("c1", "c2")
        ticks = (begin, half, lambda: None, lambda: None, finish)
        run_ticks(step, n, ticks, (1, 5, 6))

    def put(block):
        part = one_pre[pl.ds(pl.multiple_of(block * rows, 16), rows), :]
        fill(grid, side, silu(acted(part, n_one)).astype(bf16), block)

    @pl.when(step == 0)
    def _():
        clear(grid)
        clear(acc)
        put(0)

    put(jnp.minimum(step + 1, STEPS - 1))
    z = dot(tap_columns(grid, side, step, rows, False), middle[...])
    two_pre[...] = z
    add_moments(step, acc, 0, z)
    f = silu(acted(ftwo_pre[...], n_ftwo)).astype(bf16)
    ftwo[...] = f
    for k in range(2):
        add_moments(step, acc, 256 * (k + 1), dot(f, flast[:, 256 * k : 256 * (k + 1)]))
    close_moments(step, acc, ((spair, 512, 768), (fpair, 256, 768)), n3, rows * STEPS, FOLDS3, n, ticks, *swap)


def stage3(one_pre, ftwo_pre, n2, middle, flast, spair, fpair, held, side, n):
    rows = one_pre.shape[0]
    frames = rows // side**2
    return run(functools.partial(body3, n, side), rows,
        [(one_pre, "all"), (ftwo_pre, "rows")] + [(v, "all") for v in (n2, middle, flast, spair, fpair)] + [(v, "any") for v in held],
        [((rows, 256), f32, "rows"), ((rows, 128), bf16, "rows"), ((4, 768), f32, "all")] + whole_shapes(held),
        [pltpu.VMEM(((side + 2) ** 2 * frames, 256), bf16), pltpu.VMEM((2, 8, 768), f32)] + (gather_scratch(2, n) if n > 1 else []), n, (2, 768), 4, {7: 3, 8: 4})


def body4(n, two_pre, slow, lateral, n3, last, proj, spair, two, proj_pre, n4, acc, *swap):
    step = pl.program_id(0)
    clear_first(step, acc)
    v = silu(acted(two_pre[...], n3[:, :256])).astype(bf16)
    two[...] = v
    for k in range(4):
        add_moments(step, acc, 256 * k, dot(v, last[:, 256 * k : 256 * (k + 1)]))
    joined = jnp.concatenate([slow[...], lateral[...]], axis=1)
    for k in range(4):
        z = dot(joined, proj[:, 256 * k : 256 * (k + 1)])
        proj_pre[:, 256 * k : 256 * (k + 1)] = z.astype(proj_pre.dtype)
        add_moments(step, acc, 1024 + 256 * k, z)
    if n > 1:
        @pl.when(step == 0)
        def _():
            greet(n)
    close_moments(step, acc, ((spair, 768, 2816),), n4, v.shape[0] * STEPS, (), n,
        (None, None, None, lambda: greeted(n), lambda: None), *swap)


def stage4(two_pre, slow, lateral, n3, last, proj, spair, n):
    rows = two_pre.shape[0]
    return run(functools.partial(body4, n), rows,
        [(v, "rows") for v in (two_pre, slow, lateral)] + [(v, "all") for v in (n3, last, proj, spair)],
        [((rows, 256), bf16, "rows"), ((rows, 1024), f32, "rows"), ((4, 2048), f32, "all")], [pltpu.VMEM((2, 8, 2048), f32)], n, (2, 2048), 5)


def body5(two, proj_pre, cot, fast4, ftwo, fcot, n1, n3, n4, last, fproj, flast,
          slow_out, fast_out, delta, fdelta, sums, wide, three, fthree, fskip, fgrad, fout, acc):
    step = pl.program_id(0)
    rows = two.shape[0]
    clear_first(step, acc)
    fgrad[...] = split_fours(fcot, wide)
    three[...] = dot(two[...], last[...])
    fthree[...] = dot(ftwo[...], flast[...])
    for k in range(2):
        fskip[:, 256 * k : 256 * (k + 1)] = dot(fast4[:, 256 * k : 256 * (k + 1)], fproj[...])

    def side_of(za, zb, grad, na, nb, out, keep, lo, lanes):
        ga, gb, base = 0.5 * na[1:2] * na[2:3], 0.5 * nb[1:2] * nb[2:3], 0.5 * (na[3:4] + nb[3:4])
        ma, mb = na[0:1], nb[0:1]
        def one(at, carry):
            ha = za[at, lanes].astype(f32) - ma
            hb = zb[at, lanes].astype(f32) - mb
            h = ha * ga + hb * gb + base
            th = jnp.tanh(h)
            u = 1.0 + th
            out[at, lanes] = (h * u).astype(out.dtype)
            d = (0.5 * grad[at, lanes].astype(f32)) * (u * (1.0 + h * (1.0 - th)))
            keep[at, lanes] = d
            return carry[0] + eighth(d), carry[1] + eighth(d * ha), carry[2] + eighth(d * hb)
        zero = jnp.zeros((8, 256), f32)
        add_sums(step, acc, lo, strips(rows, 256, one, (zero, zero, zero)))

    for k in range(4):
        lanes = slice(256 * k, 256 * (k + 1))
        side_of(three, proj_pre, cot, n4[:, lanes], n4[:, 1024 + 256 * k : 1280 + 256 * k], slow_out, delta, 256 * k, lanes)
    for k in range(2):
        lanes = slice(256 * k, 256 * (k + 1))
        side_of(fthree, fskip, fgrad, n3[:, 256 + 256 * k : 512 + 256 * k], n1[:, 384 + 256 * k : 640 + 256 * k], fout, fdelta, 1024 + 256 * k, lanes)
    join_fours(fout[...], wide, fast_out)

    @pl.when(step == STEPS - 1)
    def _():
        scales = (1.0, jnp.concatenate([n4[1:2, :1024], n3[1:2, 256:]], axis=1), jnp.concatenate([n4[1:2, 1024:], n1[1:2, 384:]], axis=1))
        for k in range(3):
            sums[k : k + 1] = jnp.sum(acc[k], axis=0, keepdims=True) * scales[k]


def stage5(two, proj_pre, cot, fast4, ftwo, fcot, n1, n3, n4, last, fproj, flast):
    rows = two.shape[0]
    part = rows // STEPS
    return run(body5, rows,
        [(two, "rows"), (proj_pre, "rows"), (cot, "rows"), (fast4, "rows"), (ftwo, "rows"), (fcot, "rows"),
         (n1, "all"), (n3, "all"), (n4, "all"), (last, "all"), (fproj, "all"), (flast, "all")],
        [((rows, 1024), bf16, "rows"), (fcot.shape, bf16, "rows"), ((rows, 1024), f32, "rows"), ((rows, 512), f32, "rows"), ((3, 1536), f32, "all")],
        [pltpu.VMEM((part * 4, 128), f32), pltpu.VMEM((part, 1024), f32), pltpu.VMEM((part, 512), f32), pltpu.VMEM((part, 512), f32),
         pltpu.VMEM((part, 512), f32), pltpu.VMEM((part, 512), f32), pltpu.VMEM((3, 8, 1536), f32)])


def body6(n, total, two, two_pre, proj_pre, slow, lateral, delta, fast4, ftwo, ftwo_pre, fdelta, n1, n2, n3, n4, sums5, last, fproj, flast,
          d_proj, d_fproj, last_term, proj_term, flast_term, e_two, e_ftwo, sums, s5,
          three, fthree, fskip, d_three, d_fthree, acc, last_acc, proj_acc, *swap):
    step = pl.program_id(0)
    ticks = ()
    if n > 1:
        early, swap = swap[:7], swap[7:]
        ticks = (None, None, None, lambda: None, lambda: None)

    @pl.when(step == 0)
    def _():
        if n > 1:
            greet(n)
            greeted(n)
            sum_pack(total_of(n, False, sums5, *early), s5, ((1024, 1536, 128),))
        else:
            sum_pack(sums5[...], s5, ((1024, 1536, 128),))

    rows = two.shape[0]
    clear_first(step, acc, last_acc, proj_acc, flast_term)
    three[...] = dot(two[...], last[...])
    fthree[...] = dot(ftwo[...], flast[...])
    for k in range(2):
        fskip[:, 256 * k : 256 * (k + 1)] = dot(fast4[:, 256 * k : 256 * (k + 1)], fproj[...])

    def side_of(za, zb, e, na, nb, s, da, db, lanes):
        pa, pb = na[2:3] * na[1:2], nb[2:3] * nb[1:2]
        qa, qb = pa * na[1:2] * s[1:2], pb * nb[1:2] * s[2:3]
        ma, mb, base = na[0:1], nb[0:1], s[0:1]
        def one(at, carry):
            d = e[at, lanes] - base
            da[at, lanes] = (d * pa - (za[at, lanes].astype(f32) - ma) * qa).astype(bf16)
            db[at, lanes] = (d * pb - (zb[at, lanes].astype(f32) - mb) * qb).astype(bf16)
            return carry
        strips(rows, 256, one, 0)

    for k in range(4):
        lanes = slice(256 * k, 256 * (k + 1))
        side_of(three, proj_pre, delta, n4[:, lanes], n4[:, 1024 + 256 * k : 1280 + 256 * k], s5[:, lanes] * (1.0 / total), d_three, d_proj, lanes)
    for k in range(2):
        lanes = slice(256 * k, 256 * (k + 1))
        side_of(fthree, fskip, fdelta, n3[:, 256 + 256 * k : 512 + 256 * k], n1[:, 384 + 256 * k : 640 + 256 * k],
                s5[:, 1024 + 256 * k : 1280 + 256 * k] * (0.25 / total), d_fthree, d_fproj, lanes)

    wide = slow.shape[1]
    last_acc[...] += dot_tn(two[...], d_three[...])
    proj_acc[:wide] += dot_tn(slow[...], d_proj[...])
    proj_acc[wide:] += dot_tn(lateral[...], d_proj[...])
    flast_term[...] += dot_tn(ftwo[...], d_fthree[...])
    h = normed(two_pre[...], n3[:, :256])
    e = dot_nt(d_three[...], last[...]) * slope(scaled(h, n3[:, :256]))
    e_two[...] = e
    add_sums(step, acc, 0, (eighth(e), eighth(e * h)))
    h = normed(ftwo_pre[...], n2[:, 256:])
    e = dot_nt(d_fthree[...], flast[...]) * slope(scaled(h, n2[:, 256:]))
    e_ftwo[...] = e
    add_sums(step, acc, 256, (eighth(e), eighth(e * h)))
    close_sums(step, acc, sums, ((256, 384, 32),), n, ticks, *swap)

    @pl.when(step == STEPS - 1)
    def _():
        last_term[...] = last_acc[...].astype(bf16)
        proj_term[...] = proj_acc[...].astype(bf16)


def stage6(total, two, two_pre, proj_pre, slow, lateral, delta, fast4, ftwo, ftwo_pre, fdelta, n1, n2, n3, n4, sums5, last, fproj, flast, n):
    rows = two.shape[0]
    part = rows // STEPS
    return run(functools.partial(body6, n, total), rows,
        [(a, "rows") for a in (two, two_pre, proj_pre, slow, lateral, delta, fast4, ftwo, ftwo_pre, fdelta)]
        + [(a, "all") for a in (n1, n2, n3, n4, sums5, last, fproj, flast)],
        [((rows, 1024), bf16, "rows"), ((rows, 512), bf16, "rows"), ((256, 1024), bf16, "all"), ((1280, 1024), bf16, "all"), ((128, 512), f32, "all"),
         ((rows, 256), f32, "rows"), ((rows, 128), f32, "rows"), ((2, 384), f32, "all"), (sums5.shape, f32, "all")],
        [pltpu.VMEM((part, 1024), f32), pltpu.VMEM((part, 512), f32), pltpu.VMEM((part, 512), f32),
         pltpu.VMEM((part, 1024), bf16), pltpu.VMEM((part, 512), bf16), pltpu.VMEM((2, 8, 384), f32),
         pltpu.VMEM((256, 1024), f32), pltpu.VMEM((1280, 1024), f32)] + (swap_scratch(sums5.shape, n) if n > 1 else []), n, (2, 384), 7)


def body7(n, side, total, one_pre, two_pre, e_two, fone_pre, ftwo_pre, e_ftwo, n1, n2, n3, s6, middle, fmid, proj_term,
          middleerm, fmid_term, e_one, e_fone, sums, proj_grad, grid, fgrid, acc, mid_acc, *rest):
    step = pl.program_id(0)
    ticks, swap = (), rest
    if n > 1:
        ticks = scatter_ticks(n, (proj_term,), (proj_grad,), rest[:11])
        swap = rest[11:]
        run_ticks(step, n, ticks, (1, 4, 6))
    rows = one_pre.shape[0]

    def put(block):
        at = pl.ds(pl.multiple_of(block * rows, 16), rows)
        p, s = n3[:, :256], s6[:, :256] * (1.0 / total)
        fill(grid, side, input_grad(e_two[at, :], normed(two_pre[at, :], p), p, s[0:1], s[1:2]), block)
        p, s = n2[:, 256:], s6[:, 256:] * (0.25 / total)
        fill(fgrid, side, input_grad(e_ftwo[at, :], normed(ftwo_pre[at, :], p), p, s[0:1], s[1:2]), block)

    @pl.when(step == 0)
    def _():
        clear(grid)
        clear(fgrid)
        clear(acc)
        put(0)
        mid_acc[...] = jnp.zeros_like(mid_acc)
        fmid_term[...] = jnp.zeros_like(fmid_term)

    put(jnp.minimum(step + 1, STEPS - 1))

    def one_side(pre, p, columns, weight, lo, term, e_out):
        h = normed(pre[...], p)
        act = scaled(h, p)
        s = sigma(act)
        mid = act * s
        term[...] += dot_tn(mid.astype(bf16), columns)
        width = weight.shape[1]
        turned = jnp.concatenate([weight[width * k : width * (k + 1)] for k in range(9)], axis=1)
        e = dot_nt(columns, turned) * (s + mid * (1.0 - s))
        e_out[...] = e
        add_sums(step, acc, lo, (eighth(e), eighth(e * h)))

    one_side(one_pre, n2[:, :256], tap_columns(grid, side, step, rows, True), middle, 0, mid_acc, e_one)
    one_side(fone_pre, n1[:, 256:384], tap_columns(fgrid, side, step, rows, True), fmid, 256, fmid_term, e_fone)
    close_sums(step, acc, sums, ((256, 384, 32),), n, ticks, *swap)

    @pl.when(step == STEPS - 1)
    def _():
        for k in range(9):
            middleerm[k] = mid_acc[:, 256 * k : 256 * (k + 1)].astype(bf16)


def stage7(total, one_pre, two_pre, e_two, fone_pre, ftwo_pre, e_ftwo, n1, n2, n3, s6, middle, fmid, proj_term, side, n):
    terms = [six(v, n) for v in (proj_term,)] if n > 1 else [proj_term]
    parts = [(v.shape[0] // n, v.shape[1]) for v in (proj_term,)]
    rows = one_pre.shape[0]
    frames = rows // side**2
    return run(functools.partial(body7, n, side, total), rows,
        [(one_pre, "rows"), (two_pre, "all"), (e_two, "all"), (fone_pre, "rows"), (ftwo_pre, "all"), (e_ftwo, "all")]
        + [(a, "all") for a in (n1, n2, n3, s6, middle, fmid)] + [(v, "any") for v in terms],
        [((9, 256, 256), bf16, "all"), ((128, 1152), f32, "all"), ((rows, 256), f32, "rows"), ((rows, 128), f32, "rows"), ((2, 384), f32, "all")] + [(part, f32, "all") for part in parts],
        [pltpu.VMEM(((side + 2) ** 2 * frames, 256), bf16), pltpu.VMEM(((side + 2) ** 2 * frames, 128), bf16),
         pltpu.VMEM((2, 8, 384), f32), pltpu.VMEM((256, 2304), f32)] + (scatter_scratch(parts, n) if n > 1 else []), n, (2, 384), 8)


def body8(n, total, slow, lateral, one_pre, e_one, n2, s7, mask, middleerm, first_term, pieces, middle_grad, first_acc, *rest):
    step = pl.program_id(0)
    if n > 1:
        ticks = scatter_ticks(n, (middleerm,), (middle_grad,), rest)
        run_ticks(step, n, ticks, (1, 3, 5))

        @pl.when(step == STEPS - 1)
        def _():
            ticks[3]()
    clear_first(step, first_acc)
    p, s = n2[:, :256], s7[:, :256] * (1.0 / total)
    d = input_grad(e_one[...], normed(one_pre[...], p), p, s[0:1], s[1:2])
    w = d.astype(f32)
    rows = w.shape[0]
    before = pltpu.roll(masked(w, mask[0]), rows - 1, 0).astype(bf16)
    after = pltpu.roll(masked(w, mask[1]), 1, 0).astype(bf16)
    columns = jnp.concatenate([before, d, after], axis=1)
    pieces[...] = columns
    wide = slow.shape[1]
    first_acc[:wide] += dot_tn(slow[...], columns)
    first_acc[wide:] += dot_tn(lateral[...], columns)

    @pl.when(step == STEPS - 1)
    def _():
        for k in range(3):
            first_term[k] = first_acc[:, 256 * k : 256 * (k + 1)].astype(bf16)
        if n > 1:
            ticks[4]()


def stage8(total, slow, lateral, one_pre, e_one, n2, s7, mask, middleerm, n):
    rows = slow.shape[0]
    part = (middleerm.shape[0] // n, middleerm.shape[1])
    return run(functools.partial(body8, n, total), rows,
        [(a, "rows") for a in (slow, lateral, one_pre, e_one)] + [(a, "all") for a in (n2, s7, mask)]
        + [(six(middleerm, n) if n > 1 else middleerm, "any")],
        [((3, 1280, 256), bf16, "all"), ((rows, 768), bf16, "rows"), (part, f32, "all")],
        [pltpu.VMEM((1280, 768), f32)] + (scatter_scratch([part], n) if n > 1 else []), n, None, 12)


def body8b(n, pieces, d_proj, lat_pre, n1, first, proj, last_term, first_term,
           slow_grad, e_lat, sums, last_grad, first_grad, acc, *rest):
    step = pl.program_id(0)
    ticks, swap = (), rest
    if n > 1:
        ticks = scatter_ticks(n, (last_term, first_term), (last_grad, first_grad), rest[:16])
        swap = rest[16:]
        run_ticks(step, n, ticks, (1, 4, 6))
    clear_first(step, acc)
    wide = proj.shape[0] - 256

    def back(lo, hi):
        part = dot_nt(d_proj[...], proj[lo:hi])
        for k in range(3):
            part += dot_nt(pieces[:, 256 * k : 256 * (k + 1)], first[k, lo:hi])
        return part

    for k in range(4):
        slow_grad[:, 256 * k : 256 * (k + 1)] = back(256 * k, 256 * (k + 1)).astype(bf16)
    h = normed(lat_pre[...], n1[:, :256])
    e = back(wide, wide + 256) * slope(scaled(h, n1[:, :256]))
    e_lat[...] = e
    add_sums(step, acc, 0, (eighth(e), eighth(e * h)))
    close_sums(step, acc, sums, (), n, ticks, *swap)


def stage8b(pieces, d_proj, lat_pre, n1, first, proj, last_term, first_term, n):
    rows = pieces.shape[0]
    terms = [six(v, n) if n > 1 else v for v in (last_term, first_term)]
    parts = [(v.shape[0] // n, v.shape[1]) for v in (last_term, first_term)]
    return run(functools.partial(body8b, n), rows,
        [(a, "rows") for a in (pieces, d_proj, lat_pre)] + [(a, "all") for a in (n1, first, proj)] + [(v, "any") for v in terms],
        [((rows, 1024), bf16, "rows"), ((rows, 256), f32, "rows"), ((2, 256), f32, "all")] + [(part, f32, "all") for part in parts],
        [pltpu.VMEM((2, 8, 256), f32)] + (scatter_scratch(parts, n) if n > 1 else []), n, (2, 256), 9)


def lanes_at(v, source, target):
    moved = pltpu.roll(v, (target - source) % 128, 1) if target != source else v
    lane = lax.broadcasted_iota(jnp.int32, v.shape, 1)
    return jnp.where((lane >= target) & (lane < target + 32), moved, 0.0)


def pack_fast(out, band, fproj, flast, fmid):
    places_of = (
        ((0, 0, 1), (0, 1, 2), (0, 2, 3), (1, 3, 0)),
        ((0, 0, 0), (0, 1, 1), (0, 2, 2), (0, 3, 3)),
        ((0, 1, 0), (0, 2, 1), (0, 3, 2), (2, 0, 3)),
    )
    for tap in range(3):
        out[32 * tap : 32 * (tap + 1)] = sum(
            band[128 * part + 32 * j : 128 * part + 32 * (j + 1), 128 * k : 128 * (k + 1)] for part, k, j in places_of[tap])
    out[96:224] = fproj[...]
    out[224:256] = sum(flast[32 * k : 32 * (k + 1), 128 * k : 128 * (k + 1)] for k in range(4))
    for group in range(3):
        total = None
        for tap in range(4 * group, min(4 * group + 4, 9)):
            for k in range(4):
                turned = fmid[:, 128 * tap : 128 * (tap + 1)].T
                v = lanes_at(turned[32 * k : 32 * (k + 1)], 32 * k, 32 * (tap % 4))
                total = v if total is None else total + v
        out[256 + 32 * group : 288 + 32 * group] = total
    out[352:384] = jnp.zeros((32, 128), f32)


def own_pair(out, sums, lo, hi, row):
    share = out.shape[1]
    back = lax.rem(hi - lo - lax.axis_index("fsdp") * share, hi - lo)
    for at, k in enumerate((row, 0)):
        wide = jnp.broadcast_to(sums[k : k + 1, lo:hi], (8, hi - lo))
        out[at : at + 1] = pltpu.roll(wide, back, 1)[0:1, :share]


def body9(n, total, fast4, lat_pre, e_lat, fone_pre, e_fone, d_fproj, ready, n1, s5, s6, s7, s8, lat, band, fproj, mask, flast_term, fmid_term,
          ready_first, ready_middle, ready_last, ready_proj, lat_term, packed, raw, slow_grad, lat_n, one_n, two_n, out_n, proj_n, mid_n, fout_n,
          first_grad, middle_grad, last_grad, proj_grad, wide, lat_acc, whole, band_term, fproj_term):
    step = pl.program_id(0)
    clear_first(step, lat_acc, band_term, fproj_term)
    slow_grad[...] = ready[...]
    rows = fast4.shape[0]
    def backward(e, pre, p, s):
        d = input_grad(e[...], normed(pre[...], p), p, s[0:1], s[1:2])
        w = d.astype(f32)
        return d, pltpu.roll(masked(w, mask[0]), rows - 1, 0).astype(bf16), pltpu.roll(masked(w, mask[1]), 1, 0).astype(bf16)
    d, before, _ = backward(e_lat, lat_pre, n1[:, :256], s8[...] * (1.0 / total))
    f, fbefore, fafter = backward(e_fone, fone_pre, n1[:, 256:384], s7[:, 256:] * (0.25 / total))
    narrow = jnp.concatenate([f, fbefore, fafter], axis=1)
    lat_acc[:, :256] += dot_tn(before, fast4[:, 256:])
    lat_acc[:, 256:] += dot_tn(d, fast4[:, :384])
    band_term[...] += dot_tn(narrow, fast4[...])
    for k in range(4):
        fproj_term[...] += dot_tn(fast4[:, 128 * k : 128 * (k + 1)], d_fproj[:, 128 * k : 128 * (k + 1)])
    base = dot_nt(narrow, band[...])
    skip = jnp.concatenate([dot_nt(d_fproj[:, 256 * k : 256 * (k + 1)], fproj[...]) for k in range(2)], axis=1)
    whole[...] = base + skip
    whole[:, :384] += dot(d, lat[:, 256:])
    whole[:, 256:] += dot(before, lat[:, :256])
    join_fours(whole[...], wide, raw)

    @pl.when(step == STEPS - 1)
    def _():
        lat_term[...] = lat_acc[...].astype(bf16)
        for grad, found in ((first_grad, ready_first), (middle_grad, ready_middle), (last_grad, ready_last), (proj_grad, ready_proj)):
            grad[...] = found[...]
        pack_fast(packed, band_term, fproj_term, flast_term, fmid_term)
        if n > 1:
            own_pair(lat_n, s8, 0, 256, 1)
            own_pair(one_n, s7, 0, 256, 1)
            own_pair(two_n, s6, 0, 256, 1)
            own_pair(out_n, s5, 0, 1024, 1)
            own_pair(proj_n, s5, 0, 1024, 2)
        for j, (sums, lo, row) in enumerate(((s7, 256, 1), (s6, 256, 1))):
            mid_n[j, 0:1] = sums[row : row + 1, lo : lo + 32]
            mid_n[j, 1:2] = sums[0:1, lo : lo + 32]
        for j in range(2):
            fout_n[j, 0:1] = s5[j + 1 : j + 2, 1024:1152]
            fout_n[j, 1:2] = s5[0:1, 1024:1152]


def stage9(total, fast4, lat_pre, e_lat, fone_pre, e_fone, d_fproj, ready, n1, s5, s6, s7, s8, lat, band, fproj, mask, flast_term, fmid_term, grads, n):
    rows = fast4.shape[0]
    part = rows // STEPS
    return run(functools.partial(body9, n, total), rows,
        [(a, "rows") for a in (fast4, lat_pre, e_lat, fone_pre, e_fone, d_fproj, ready)]
        + [(a, "all") for a in (n1, s5, s6, s7, s8, lat, band, fproj, mask, flast_term, fmid_term) + tuple(grads)],
        [((256, 640), bf16, "all"), ((384, 128), f32, "all"), ((rows // 16, 64, 128), bf16, "rows"), (ready.shape, bf16, "rows")]
        + [((2, 256 // n), f32, "all")] * 3 + [((2, 1024 // n), f32, "all")] * 2 + [((2, 2, 32), f32, "all"), ((2, 2, 128), f32, "all")] + [(v.shape, f32, "all") for v in grads],
        [pltpu.VMEM((part * 4, 128), f32), pltpu.VMEM((256, 640), f32), pltpu.VMEM((part, 512), f32),
         pltpu.VMEM((384, 512), f32), pltpu.VMEM((128, 128), f32)])


def body10(n, lat_term, packed, lat_grad, first_t, middle_t, last, proj, sums, slots, line, mine, lat_slots, lat_line, lat_mine,
           a_send, a_recv, b_send, b_recv, g_send, g_recv, l_send, l_recv, m_send, m_recv):
    me = lax.axis_index("fsdp")
    mi, mo, depth = lax.rem(me, INNER), lax.div(me, INNER), n // INNER
    peers = [mo * INNER + lax.rem(mi + k, INNER) for k in range(INNER)]
    spots = [lax.rem(mi + k, INNER) for k in range(INNER)]
    beyond = [lax.rem(mo + k, depth) for k in range(depth)]

    def remote(src, dst, send, recv, peer):
        copy = pltpu.make_async_remote_copy(
            src_ref=src, dst_ref=dst, send_sem=send, recv_sem=recv, device_id=(peer,), device_id_type=MESH)
        copy.start()
        return copy

    greet(n)
    greeted(n)
    fast = [remote(packed.at[spots[k]], slots.at[mi], a_send.at[k], a_recv.at[k], peers[k]) for k in range(1, INNER)]
    slow = [remote(lat_term.at[:, spots[k]], lat_slots.at[mi], l_send.at[k], l_recv.at[k], peers[k]) for k in range(1, INNER)]
    slots[mi] = packed[mi]
    lat_slots[mi] = lat_term[:, mi]
    for copy in fast:
        copy.wait()
    mine[...] = sum(slots[k] for k in range(1, INNER)) + slots[0]
    fast = [remote(mine, line.at[mo], b_send.at[k], b_recv.at[k], beyond[k] * INNER + mi) for k in range(1, depth)]
    line[mo] = mine[...]
    for copy in slow:
        copy.wait()
    lat_mine[...] = sum(lat_slots[k].astype(f32) for k in range(INNER)).astype(bf16)
    slow = [remote(lat_mine.at[beyond[k]], lat_line.at[mo], m_send.at[k], m_recv.at[k], beyond[k] * INNER + mi) for k in range(1, depth)]
    lat_line[mo] = lat_mine[mo]
    for copy in fast:
        copy.wait()
    sums[mi] = sum((line[k] for k in range(1, depth)), line[0])
    fast = [remote(sums.at[mi], sums.at[mi], g_send.at[k], g_recv.at[k], peers[k]) for k in range(1, INNER)]
    for copy in slow:
        copy.wait()
    lat_grad[...] = sum(lat_line[k].astype(f32) for k in range(depth))
    for copy in fast:
        copy.wait()

    high = sums.shape[1]
    def rows_of(lo, hi):
        found = []
        while lo < hi:
            top = min(hi, (lo // high + 1) * high)
            found.append(sums[lo // high, lo % high : lo % high + top - lo])
            lo = top
        return jnp.concatenate(found, axis=0) if len(found) > 1 else found[0]

    for k in range(3):
        first_t[:, 128 * k : 128 * (k + 1)] = rows_of(32 * k, 32 * (k + 1))
        wide = min(128, 288 - 128 * k)
        middle_t[:, 128 * k : 128 * k + wide] = rows_of(256 + 32 * k, 288 + 32 * k)[:, :wide]
    proj[...] = rows_of(96, 224)
    last[...] = rows_of(224, 256)


def stage10(lat_term, packed, n):
    depth, DS = n // INNER, pltpu.SemaphoreType.DMA
    packed = packed.reshape(INNER, -1, 128)
    chunk = packed.shape[1:]
    share = (lat_term.shape[0] // n, lat_term.shape[1])
    lat_grad, first_t, middle_t, last, proj = pl.pallas_call(
        functools.partial(body10, n),
        in_specs=[pl.BlockSpec(memory_space=pltpu.VMEM)] * 2,
        out_specs=[pl.BlockSpec(memory_space=pltpu.VMEM)] * 5,
        out_shape=[jax.ShapeDtypeStruct(shape, f32) for shape in (share, (32, 384), (32, 288), (32, 128), (128, 128))],
        scratch_shapes=[pltpu.VMEM((INNER,) + chunk, f32), pltpu.VMEM((INNER,) + chunk, f32), pltpu.VMEM((depth,) + chunk, f32), pltpu.VMEM(chunk, f32),
            pltpu.VMEM((INNER, depth) + share, bf16), pltpu.VMEM((depth,) + share, bf16), pltpu.VMEM((depth,) + share, bf16)]
        + [DS((INNER,)), DS((INNER,)), DS((depth,)), DS((depth,)), DS((INNER,)), DS((INNER,)), DS((INNER,)), DS((INNER,)), DS((depth,)), DS((depth,))],
        compiler_params=pltpu.CompilerParams(collective_id=10, has_side_effects=True),
    )(lat_term.reshape((depth, INNER) + share), packed)
    lat_grad, first_t, middle_t, last, proj = stage11((lat_grad, first_t, middle_t, last, proj))
    return lat_grad, (first_t.T, middle_t.T, last, proj)


def body11(*refs):
    half = len(refs) // 2
    for source, target in zip(refs[:half], refs[half:]):
        target[...] = source[...]


def stage11(arrays):
    VM = pl.BlockSpec(memory_space=pltpu.VMEM)
    return pl.pallas_call(
        body11,
        in_specs=[VM] * len(arrays),
        out_specs=[VM] * len(arrays),
        out_shape=[jax.ShapeDtypeStruct(v.shape, v.dtype) for v in arrays],
    )(*arrays)


def shards(slow_in, fast_in, clip_ids, lateral_weight, first_weight, middle_weight, last_weight, proj_weight,
           lat_norm, one_norm, two_norm, out_norm, proj_norm, fast_first, fast_middle, fast_last, fast_proj,
           fast_mid_norm, fast_out_norm, slow_cot, fast_cot):
    n = lax.axis_size("fsdp")
    side = slow_in.shape[1]
    count = slow_in.shape[0] * side * side * n
    lat, first, spair, band, fproj, fmid, flast, fpair, mask = stage0(
        lateral_weight.T, first_weight, (lat_norm, one_norm, two_norm, out_norm, proj_norm),
        (fast_first.T, fast_middle.T, fast_last, fast_proj, fast_mid_norm, fast_out_norm), clip_ids, n)
    lat = gathered(lat, n)

    def rows(v):
        return v.transpose(1, 2, 0, 3).reshape(-1, v.shape[3])
    def unrows(v):
        return v.reshape(side, side, -1, v.shape[1]).transpose(2, 0, 1, 3)
    def raw(v):
        return v.transpose(1, 2, 0, 3).reshape(side * side, -1, v.shape[3])
    def unraw(v):
        return v.reshape((side, side) + v.shape[1:]).transpose(2, 0, 1, 3)

    slow = rows(slow_in)
    fast4, lat_pre, fone_pre, n1, first, *held = stage1(
        raw(fast_in), lat, band, fproj, mask, spair, fpair, first, (middle_weight, last_weight), n)
    first = gathered(first, n).reshape(3, -1, first_weight.shape[1])
    lateral, one_pre, ftwo_pre, n2, middle, last, proj = stage2(
        slow, lat_pre, fone_pre, n1, first, fmid, mask, spair, fpair, held, proj_weight, side, n)
    middle = gathered(middle, n)
    two_pre, ftwo, n3, last, proj = stage3(one_pre, ftwo_pre, n2, middle, flast, spair, fpair, (last, proj), side, n)
    last, proj = gathered(last, n), gathered(proj, n)
    two, proj_pre, n4 = stage4(two_pre, slow, lateral, n3, last, proj, spair, n)
    slow_out, fast_out, delta, fdelta, local = stage5(
        two, proj_pre, rows(slow_cot), fast4, ftwo, raw(fast_cot), n1, n3, n4, last, fproj, flast)
    d_proj, d_fproj, last_term, proj_term, flast_term, e_two, e_ftwo, s6, s5 = stage6(
        count, two, two_pre, proj_pre, slow, lateral, delta, fast4, ftwo, ftwo_pre, fdelta, n1, n2, n3, n4, local, last, fproj, flast, n)
    middle_term, fmid_term, e_one, e_fone, s7, proj_grad = stage7(
        count, one_pre, two_pre, e_two, fone_pre, ftwo_pre, e_ftwo, n1, n2, n3, s6, middle, fmid, proj_term, side, n)
    first_term, pieces, middle_grad = stage8(count, slow, lateral, one_pre, e_one, n2, s7, mask, middle_term.reshape(-1, 256), n)
    slow_grad, e_lat, s8, last_grad, first_grad = stage8b(
        pieces, d_proj, lat_pre, n1, first, proj, last_term, first_term.reshape(-1, 256), n)
    lat_term, packed, fast_grad, slow_grad, *small = stage9(
        count, fast4, lat_pre, e_lat, fone_pre, e_fone, d_fproj, slow_grad, n1, s5, s6, s7, s8, lat, band, fproj, mask, flast_term, fmid_term,
        (first_grad, middle_grad, last_grad, proj_grad), n)
    lateral_grad, fast_grads = stage10(lat_term, packed, n)
    return (unrows(slow_out), unraw(fast_out), unrows(slow_grad), unraw(fast_grad),
            lateral_grad.T, *small[7:],
            *small[:5], *fast_grads, *small[5:7])


def solution(mesh):
    in_specs = (
        P("fsdp", None, None, None),
        P("fsdp", None, None, None),
        P("fsdp", None),
        P(None, "fsdp"),
        P("fsdp", None),
        P("fsdp", None),
        P("fsdp", None),
        P("fsdp", None),
        P(None, "fsdp"),
        P(None, "fsdp"),
        P(None, "fsdp"),
        P(None, "fsdp"),
        P(None, "fsdp"),
        P(),
        P(),
        P(),
        P(),
        P(),
        P(),
        P("fsdp", None, None, None),
        P("fsdp", None, None, None),
    )
    out_specs = (
        P("fsdp", None, None, None),
        P("fsdp", None, None, None),
        P("fsdp", None, None, None),
        P("fsdp", None, None, None),
        P(None, "fsdp"),
        P("fsdp", None),
        P("fsdp", None),
        P("fsdp", None),
        P("fsdp", None),
        P(None, "fsdp"),
        P(None, "fsdp"),
        P(None, "fsdp"),
        P(None, "fsdp"),
        P(None, "fsdp"),
        P(),
        P(),
        P(),
        P(),
        P(),
        P(),
    )
    return jax.shard_map(shards, mesh=mesh, in_specs=in_specs, out_specs=out_specs, check_vma=False)
```

```python
import functools

import jax
import jax.numpy as jnp
import numpy as np
from jax import lax
from jax.experimental import pallas as pl
from jax.experimental.pallas import tpu as pltpu
from jax.sharding import PartitionSpec as P

EPSILON = 1e-05


MESH = pl.DeviceIdType.MESH


f32 = jnp.float32
bf16 = jnp.bfloat16
STEPS = 7
STRIP = 32


def dot(a, b):
    return lax.dot_general(a, b, (((1,), (0,)), ((), ())), preferred_element_type=f32)


def dot_nt(a, b):
    return lax.dot_general(a, b, (((1,), (1,)), ((), ())), preferred_element_type=f32)


def dot_tn(a, b):
    return lax.dot_general(a, b, (((0,), (0,)), ((), ())), preferred_element_type=f32)


def shift(v, mask, by):
    rows = v.shape[0]
    moved = pltpu.roll(v, by % rows, 0)
    return masked(moved, mask)


def masked(v, mask):
    return (v.reshape(-1, mask.shape[0], v.shape[1]) * mask[None, :, : v.shape[1]]).reshape(v.shape)


def sigma(x):
    return 0.5 + 0.5 * jnp.tanh(0.5 * x)


def silu(x):
    return x * sigma(x)


def slope(x):
    s = sigma(x)
    return s * (1.0 + x * (1.0 - s))


def normed(z, n):
    return (z - n[0:1]) * n[1:2]


def scaled(hat, n):
    return hat * n[2:3] + n[3:4]


def acted(z, n):
    return scaled(normed(z, n), n)


def input_grad(e, hat, n, s_mean, s_cross):
    return ((n[2:3] * n[1:2]) * (e - s_mean - hat * s_cross)).astype(bf16)


def eighth(v):
    return jnp.sum(v.reshape(-1, 8, v.shape[1]), axis=0)


def clear_first(step, *refs):
    @pl.when(step == 0)
    def _():
        for ref in refs:
            ref[...] = jnp.zeros(ref.shape, ref.dtype)


def add_moments(step, acc, lo, z):
    hi = lo + z.shape[1]
    high = z.shape[0] // 8
    deep = z.reshape(high, 8, hi - lo)
    own = jnp.sum(deep, axis=0) * (1.0 / high)
    off = deep - own[None]
    spread_of = jnp.sum(off * off, axis=0)
    past = step.astype(f32)
    share = 1.0 / (past + 1.0)
    gap = own - acc[0, :, lo:hi]
    acc[0, :, lo:hi] += gap * share
    acc[1, :, lo:hi] += spread_of + gap * gap * (past * share * high)


def add_sums(step, acc, lo, parts):
    hi = lo + parts[0].shape[1]
    for k, part in enumerate(parts):
        acc[k, :, lo:hi] += part


def split_fours(raw, wide):
    rows = wide.shape[0]
    wide[...] = raw[...].astype(f32).reshape(rows, 128)
    return jnp.concatenate([wide[pl.ds(k, rows // 4, stride=4), :] for k in range(4)], axis=1)


def join_fours(value, wide, raw):
    rows = wide.shape[0]
    for k in range(4):
        wide[pl.ds(k, rows // 4, stride=4), :] = value[:, 128 * k : 128 * (k + 1)]
    raw[...] = wide[...].astype(bf16).reshape(raw.shape)


def clear(grid):
    grid[...] = jnp.zeros(grid.shape, grid.dtype)


def fill(grid, side, value, block):
    per = side // STEPS
    line = value.shape[0] // per
    frames = line // side
    for r in range(per):
        at = ((block * per + r + 1) * (side + 2) + 1) * frames
        grid[pl.ds(pl.multiple_of(at, 16), line), :] = value[r * line : (r + 1) * line]


def tap_columns(grid, side, step, rows, flip):
    per = side // STEPS
    line = rows // per
    frames = line // side
    lines = []
    for r in range(per):
        pieces = []
        for a in range(3):
            for b in range(3):
                ra, rb = (2 - a, 2 - b) if flip else (a, b)
                at = ((step * per + r + ra) * (side + 2) + rb) * frames
                pieces.append(grid[pl.ds(pl.multiple_of(at, 16), line), :])
        lines.append(jnp.concatenate(pieces, axis=1))
    return jnp.concatenate(lines, axis=0)


INNER = 8


def greet(n):
    me = lax.axis_index("fsdp")
    mi, mo, depth = lax.rem(me, INNER), lax.div(me, INNER), n // INNER
    barrier = pltpu.get_barrier_semaphore()
    for k in range(1, INNER):
        pl.semaphore_signal(barrier, inc=1, device_id=(mo * INNER + lax.rem(mi + k, INNER),), device_id_type=MESH)
    for k in range(1, depth):
        pl.semaphore_signal(barrier, inc=1, device_id=(lax.rem(mo + k, depth) * INNER + mi,), device_id_type=MESH)


def greeted(n):
    pl.semaphore_wait(pltpu.get_barrier_semaphore(), INNER - 1 + n // INNER - 1)


def total_of(n, centred, own, near, far, mid, near_send, near_recv, far_send, far_recv):
    me = lax.axis_index("fsdp")
    mi, mo, depth = lax.rem(me, INNER), lax.div(me, INNER), n // INNER

    def swap(src, slots, sends, recvs, mine, size, peer):
        copies = []
        for k in range(1, size):
            copy = pltpu.make_async_remote_copy(
                src_ref=src, dst_ref=slots.at[mine], send_sem=sends.at[k], recv_sem=recvs.at[k],
                device_id=(peer(k),), device_id_type=MESH)
            copy.start()
            copies.append(copy)
        slots[mine] = src[...]
        for copy in copies:
            copy.wait()

    def merge(slots, size):
        if not centred:
            return sum(slots[k] for k in range(1, size)) + slots[0]
        mean = sum(slots[k, 0:1] for k in range(size)) * (1.0 / size)
        off = [slots[k, 0:1] - mean for k in range(size)]
        return jnp.concatenate([mean, sum(slots[k, 1:2] + off[k] * off[k] for k in range(size)) * (1.0 / size)], axis=0)

    swap(own, near, near_send, near_recv, mi, INNER, lambda k: mo * INNER + lax.rem(mi + k, INNER))
    mid[...] = merge(near, INNER)
    if depth == 1:
        return mid[...]
    swap(mid, far, far_send, far_recv, mo, depth, lambda k: lax.rem(mo + k, depth) * INNER + mi)
    return merge(far, depth)


def over_groups(part, width):
    lanes = part.shape[1]
    if width < 128:
        wide = jnp.broadcast_to(part, (8, lanes))
        total = wide
        for k in range(1, lanes // width):
            total = total + pltpu.roll(wide, k * width, 1)
        return total[0:1]
    total = sum(part[:, k : k + width] for k in range(0, lanes, width))
    return jnp.concatenate([total] * (lanes // width), axis=1)


def norm_pack(total, pairs, out, folds):
    out[0:2] = total
    for lo, hi, width in folds:
        groups = width / (hi - lo)
        mean = over_groups(total[0:1, lo:hi], width) * groups
        off = total[0:1, lo:hi] - mean
        out[0:1, lo:hi] = mean
        out[1:2, lo:hi] = over_groups(total[1:2, lo:hi] + off * off, width) * groups
    out[1:2] = lax.rsqrt(out[1:2] + EPSILON)
    at = 0
    for pair, lo, hi in pairs:
        out[2:4, at : at + hi - lo] = pair[:, lo:hi]
        at += hi - lo


def sum_pack(total, out, folds):
    out[...] = total
    for lo, hi, width in folds:
        for k in range(out.shape[0]):
            out[k : k + 1, lo:hi] = over_groups(total[k : k + 1, lo:hi], width)


def swap_scratch(shape, n):
    DS, depth = pltpu.SemaphoreType.DMA, n // INNER
    return [pltpu.VMEM((INNER,) + shape, f32), pltpu.VMEM((depth,) + shape, f32), pltpu.VMEM(shape, f32),
        DS((INNER,)), DS((INNER,)), DS((depth,)), DS((depth,))]


def run(body, rows, ins, outs, scratch, n=1, swap=None, call=None, same=None):
    def spec(shape, how):
        if how == "any":
            return pl.BlockSpec(memory_space=pl.ANY)
        if how == "rows":
            return pl.BlockSpec((shape[0] // STEPS,) + tuple(shape[1:]), lambda i, d=len(shape): (i,) + (0,) * (d - 1))
        return pl.BlockSpec(tuple(shape), lambda i, d=len(shape): (0,) * d, pipeline_mode=pl.Buffered(1))
    def out_spec(shape, how):
        if how in ("rows", "any"):
            return spec(shape, how)
        return pl.BlockSpec(tuple(shape), lambda i, d=len(shape): (0,) * d)
    extra = {}
    if swap is not None:
        scratch = scratch + [pltpu.VMEM(swap, f32)]
    if n > 1 and swap is not None:
        scratch = scratch + swap_scratch(swap, n)
    if n > 1 and call is not None:
        extra = dict(collective_id=call, has_side_effects=True)
    return pl.pallas_call(
        body,
        grid=(STEPS,),
        in_specs=[spec(a.shape, how) for a, how in ins],
        out_specs=[out_spec(shape, how) for shape, _, how in outs],
        out_shape=[jax.ShapeDtypeStruct(shape, kind) for shape, kind, _ in outs],
        scratch_shapes=scratch,
        input_output_aliases=same or {},
        compiler_params=pltpu.CompilerParams(dimension_semantics=("arbitrary",), vmem_limit_bytes=58 * 1024 * 1024, **extra),
    )(*[a for a, _ in ins])


def close_moments(step, acc, pairs, out, count, folds, n, ticks, own, *links):
    @pl.when(step == STEPS - 1)
    def _():
        mean = jnp.mean(acc[0], axis=0, keepdims=True)
        off = acc[0] - mean
        own[0:1] = mean
        own[1:2] = jnp.sum(acc[1], axis=0, keepdims=True) * (1.0 / count) + jnp.mean(off * off, axis=0, keepdims=True)
        if n > 1:
            ticks[3]()
            norm_pack(total_of(n, True, own, *links), pairs, out, folds)
            ticks[4]()
        else:
            norm_pack(own[...], pairs, out, folds)


def close_sums(step, acc, out, folds, n, ticks, own, *links):
    if n > 1 and not ticks:
        @pl.when(step == 0)
        def _():
            greet(n)

    @pl.when(step == STEPS - 1)
    def _():
        for k in range(acc.shape[0]):
            own[k : k + 1] = jnp.sum(acc[k], axis=0, keepdims=True)
        if n > 1:
            if ticks:
                ticks[3]()
            else:
                greeted(n)
            sum_pack(total_of(n, False, own, *links), out, folds)
            if ticks:
                ticks[4]()
        else:
            sum_pack(own[...], out, folds)


def places():
    me = lax.axis_index("fsdp")
    return lax.div(me, 8), lax.rem(lax.div(me, 4), 2), lax.rem(lax.div(me, 2), 2), lax.rem(me, 2)


def flat(z, y, x, c):
    return ((z * 2 + y) * 2 + x) * 2 + c


def six(term, n):
    return term.reshape((n // 8, 2, 2, 2, term.shape[0] // n) + term.shape[1:])


def halves(width):
    if width < 256:
        return ((0, width),)
    middle = width // 256 * 128
    return ((0, middle), (middle, width))


def scatter_scratch(parts, n):
    depth, k, DS = n // 8, len(parts), pltpu.SemaphoreType.DMA
    def buf(lead):
        return [pltpu.VMEM(lead + part, bf16) for part in parts]
    return (buf((depth, 2, 2)) + buf((depth, 2, 2)) + buf((depth, 2)) + buf((depth,)) + buf((depth,))
        + [DS((k,)), DS((k, 2)), DS((k, 2, 2)), DS((k, 2, 2)), DS((k, depth)), DS((k, depth))])


def scatter_ticks(n, ins, outs, rest):
    k, depth = len(ins), n // 8
    half, r1, r2, r3, r4 = (rest[j * k : (j + 1) * k] for j in range(5))
    own_sem, c_sem, p_sem, q_sem, z_send, z_recv = rest[5 * k :]
    z, y, x, c = places()
    core, over_x, over_y = flat(z, y, x, 1 - c), flat(z, y, 1 - x, c), flat(z, 1 - y, x, c)
    line = [flat(lax.rem(z + s, depth), y, x, c) for s in range(depth)]
    spots = [lax.rem(z + s, depth) for s in range(depth)]

    def remote(src, dst, send, recv, peer):
        return pltpu.make_async_remote_copy(
            src_ref=src, dst_ref=dst, send_sem=send, recv_sem=recv, device_id=(peer,), device_id_type=MESH)
    def sides(i):
        return tuple(enumerate(halves(half[i].shape[-1])))
    def own(i):
        return pltpu.make_async_copy(ins[i].at[:, :, :, c], half[i], own_sem.at[i])
    def to_core(i):
        return remote(ins[i].at[:, :, :, 1 - c], r1[i], c_sem.at[i, 0], c_sem.at[i, 1], core)
    def to_first(i, t, lo, hi):
        src, peer = (half[i].at[:, :, 1 - x, :, lo:hi], over_x) if t == 0 else (half[i].at[:, 1 - y, :, :, lo:hi], over_y)
        return remote(src, r2[i].at[:, :, :, lo:hi], p_sem.at[i, t, 0], p_sem.at[i, t, 1], peer)
    def to_second(i, t, lo, hi):
        src, peer = (half[i].at[:, 1 - y, x, :, lo:hi], over_y) if t == 0 else (half[i].at[:, y, 1 - x, :, lo:hi], over_x)
        return remote(src, r3[i].at[:, :, lo:hi], q_sem.at[i, t, 0], q_sem.at[i, t, 1], peer)
    def to_line(i, s):
        return remote(half[i].at[spots[s], y, x], r4[i].at[s], z_send.at[i, s], z_recv.at[i, s], line[s])
    def add(target, other):
        target[...] = (target[...].astype(f32) + other[...].astype(f32)).astype(target.dtype)

    def begin():
        for i in range(k):
            own(i).start()
            to_core(i).start()
    def first():
        for i in range(k):
            own(i).wait()
            to_core(i).wait()
            @pl.loop(0, depth)
            def _(zz, i=i):
                for a in range(2):
                    for b in range(2):
                        add(half[i].at[zz, a, b], r1[i].at[zz, a, b])
            for t, (lo, hi) in sides(i):
                to_first(i, t, lo, hi).start()
    def second():
        for i in range(k):
            for t, (lo, hi) in sides(i):
                to_first(i, t, lo, hi).wait()
                @pl.loop(0, depth)
                def _(zz, i=i, t=t, lo=lo, hi=hi):
                    for o in range(2):
                        target = half[i].at[zz, o, x] if t == 0 else half[i].at[zz, y, o]
                        add(target.at[:, lo:hi], r2[i].at[zz, o, :, lo:hi])
                to_second(i, t, lo, hi).start()
    def third():
        for i in range(k):
            for t, (lo, hi) in sides(i):
                to_second(i, t, lo, hi).wait()
            @pl.loop(0, depth)
            def _(zz, i=i):
                add(half[i].at[zz, y, x], r3[i].at[zz])
            for s in range(1, depth):
                to_line(i, s).start()
    def finish():
        for i in range(k):
            outs[i][...] = half[i][z, y, x].astype(f32)
            for s in range(1, depth):
                to_line(i, s).wait()
                outs[i][...] += r4[i][s].astype(f32)
    return begin, first, second, third, finish


GATHER_SEMS = 9


def gather_scratch(k, n):
    DS, depth = pltpu.SemaphoreType.DMA, n // 8
    return [DS((1,)), DS((depth,)), DS((depth,)), DS((2, 2)), DS((2, 2)), DS((2, 3)), DS((2, 3)), DS((8,)), DS((8,))] * k


class Moves:
    def __init__(self, n, shard, whole, sems):
        self.n, self.shard, self.whole, self.sems = n, shard, whole, sems
        self.at = places()
        self.sides = tuple(enumerate(halves(whole.shape[-1])))

    def remote(self, src, dst, send, recv, *peer):
        return pltpu.make_async_remote_copy(
            src_ref=src, dst_ref=dst, send_sem=send, recv_sem=recv, device_id=(flat(*peer),), device_id_type=MESH)

    def part(self, name, t, lo, hi):
        z, y, x, c = self.at
        index = {
            "p": (slice(None), y, x, c),
            "q": (slice(None), y, slice(None), c) if t == 0 else (slice(None), slice(None), x, c),
            "c1": (slice(None), y, 1 - x, c) if t == 0 else (slice(None), 1 - y, x, c),
            "c2": (slice(None), 1 - y, slice(None), c) if t == 0 else (slice(None), slice(None), 1 - x, c),
        }["p" if name == "c0" else name]
        return self.whole.at[index + (slice(None), slice(lo, hi))]

    def copies(self, name):
        z, y, x, c = self.at
        own, z_send, z_recv, p, q, c_send, c_recv, d_send, d_recv = self.sems
        depth = self.n // 8
        if name == "z":
            mine = self.whole.at[z, y, x, c]
            return [pltpu.make_async_copy(self.shard, mine, own.at[0])] + [
                self.remote(self.shard, mine, z_send.at[s], z_recv.at[s], lax.rem(z + s, depth), y, x, c) for s in range(1, depth)]
        if name == "d":
            mine = self.whole.at[:, y, x, c]
            found = []
            for k in range(1, 8):
                other = lax.rem((y * 2 + x) * 2 + c + k, 8)
                found.append(self.remote(mine, mine, d_send.at[k], d_recv.at[k], z, 0, 0, other))
            return found
        found = []
        for t, (lo, hi) in self.sides:
            src = self.part(name, t, lo, hi)
            if name[0] == "c":
                j = int(name[1])
                found.append(self.remote(src, src, c_send.at[t, j], c_recv.at[t, j], z, y, x, 1 - c))
                continue
            sem = p if name == "p" else q
            peer = (z, y, 1 - x, c) if (t == 0) == (name == "p") else (z, 1 - y, x, c)
            found.append(self.remote(src, src, sem.at[t, 0], sem.at[t, 1], *peer))
        return found

    def start(self, *names):
        for name in names:
            for copy in self.copies(name):
                copy.start()

    def wait(self, *names):
        for name in names:
            for copy in self.copies(name):
                copy.wait()


def moves(n, shards, wholes, rest):
    return [Moves(n, shard, whole, rest[GATHER_SEMS * i : GATHER_SEMS * (i + 1)]) for i, (shard, whole) in enumerate(zip(shards, wholes))]


def spread_shapes(shards, n):
    return [((n // 8, 2, 2, 2) + v.shape, v.dtype, "any") for v in shards]


def whole_shapes(wholes):
    return [(v.shape, v.dtype, "any") for v in wholes]


def gathered(v, n):
    return v.reshape((n * v.shape[4],) + v.shape[5:])


def at_lanes(v, offset):
    rows, width = v.shape
    wide = v if width == 128 else jnp.concatenate([v, jnp.zeros((rows, 128 - width), v.dtype)], axis=1)
    return pltpu.roll(wide, offset, 1) if offset else wide


def build_fast(first_t, middle_t, last, skip, mid_norm, out_norm, ids, band, fproj, fmid, flast, fpair, mask, lanes):
    band[...] = jnp.zeros(band.shape, bf16)
    fproj[...] = jnp.zeros(fproj.shape, bf16)
    flast[...] = jnp.zeros(flast.shape, bf16)
    none = jnp.zeros((96, 128), f32)
    for tap in range(3):
        block = jnp.concatenate([first_t[:, 128 * tap : 128 * (tap + 1)].astype(f32), none], axis=0).T
        placed = [pltpu.roll(block, 32 * j, 1) if j else block for j in range(4)]
        for part in range(3):
            for k in range(4):
                here = [j for j in range(4) if (j + tap - 1) % 4 == k and part == (1 if j + tap < 1 else 2 if j + tap > 4 else 0)]
                if here:
                    (j,) = here
                    band[128 * k : 128 * (k + 1), 128 * part : 128 * (part + 1)] += placed[j].astype(bf16)
    lanes[...] = jnp.zeros(lanes.shape, f32)
    lanes[:, :288] = middle_t[...].astype(f32)
    for group in range(3):
        block = jnp.concatenate([lanes[:, 128 * group : 128 * (group + 1)], none], axis=0).T
        for tap in range(4 * group, min(4 * group + 4, 9)):
            part = block[32 * (tap % 4) : 32 * (tap % 4 + 1)]
            for k in range(4):
                fmid[128 * tap + 32 * k : 128 * tap + 32 * (k + 1)] = (pltpu.roll(part, 32 * k, 1) if k else part).astype(bf16)
    for k in range(4):
        flast[32 * k : 32 * (k + 1), 128 * k : 128 * (k + 1)] = last[...]
    for k in range(2):
        fproj[128 * k : 128 * (k + 1), 128 * k : 128 * (k + 1)] = skip[...]
        narrow = at_lanes(mid_norm[k].astype(f32), 0)
        wide = jnp.concatenate([narrow] * 4, axis=0)
        fpair[:, 128 * k : 128 * (k + 1)] = sum(pltpu.roll(wide, 32 * j, 1) for j in range(1, 4))[:2] + narrow
        for j in range(4):
            fpair[:, 256 + 512 * k + 128 * j : 384 + 512 * k + 128 * j] = out_norm[k].astype(f32)
    frames = mask.shape[1]
    row = lax.broadcasted_iota(jnp.int32, (frames, frames), 0)
    column = lax.broadcasted_iota(jnp.int32, (frames, frames), 1)
    spread_ids = jnp.broadcast_to(ids[...].astype(f32), (frames, frames))
    def pick(by):
        return jnp.sum(jnp.where(column == row + by, spread_ids, 0.0), axis=1, keepdims=True)
    at = lax.broadcasted_iota(jnp.int32, (frames, 1), 0)
    here = pick(0)
    prev = jnp.where((here == pick(-1)) & (at > 0), 1.0, 0.0)
    after = jnp.where((here == pick(1)) & (at < frames - 1), 1.0, 0.0)
    mask[0] = jnp.broadcast_to(prev, mask.shape[1:])
    mask[1] = jnp.broadcast_to(after, mask.shape[1:])


def pack_norms(pairs, out):
    total, offset = None, 0
    for pair in pairs:
        v = at_lanes(jnp.concatenate([pair[...].astype(f32)] * 4, axis=0), offset)
        total = v if total is None else total + v
        offset += pair.shape[1]
    out[...] = total


def join_norms(gathered_of, shares, out):
    n = gathered_of.shape[0]
    offset, lo = 0, 0
    for share in shares:
        wide = share * n
        pick = lax.broadcasted_iota(jnp.int32, (128, wide), 0) == offset + lax.broadcasted_iota(jnp.int32, (128, wide), 1) % share
        pick = jnp.where(pick, 1.0, 0.0).astype(bf16)
        mine = lax.broadcasted_iota(jnp.int32, (n, wide), 0) == lax.broadcasted_iota(jnp.int32, (n, wide), 1) // share
        for row in range(2):
            each = dot(gathered_of[:, row, :].astype(bf16), pick)
            out[row : row + 1, lo : lo + wide] = jnp.sum(jnp.where(mine, each, 0.0), axis=0, keepdims=True)
        offset += share
        lo += wide


def body0(n, lat_shard, first_shard, p_lat, p_one, p_two, p_out, p_proj, first_t, middle_t, last_w, skip, mid_norm, out_norm, ids,
          lat_whole, first_whole, spair, band, fproj, fmid, flast, fpair, mask, own, norms_whole, lanes, *sems):
    lat, norms, first = moves(n, (lat_shard, own, first_shard), (lat_whole, norms_whole, first_whole), sems)
    pairs = (p_lat, p_one, p_two, p_out, p_proj)
    greet(n)
    pack_norms(pairs, own)
    greeted(n)
    for m in (lat, norms, first):
        m.start("z")
    build_fast(first_t, middle_t, last_w, skip, mid_norm, out_norm, ids, band, fproj, fmid, flast, fpair, mask, lanes)
    for m in (lat, norms):
        m.wait("z")
        m.start("d")
    first.wait("z")
    lat.wait("d")
    norms.wait("d")
    join_norms(norms_whole[...].reshape(n, 8, 128), [p.shape[1] for p in pairs], spair)


def stage0(lat_shard, first_shard, pairs, fast, ids, n):
    VM, ANY = pl.BlockSpec(memory_space=pltpu.VMEM), pl.BlockSpec(memory_space=pl.ANY)
    shape_of = lambda shape, kind: jax.ShapeDtypeStruct(shape, kind)
    small = tuple(pairs) + tuple(fast) + (ids,)
    width = sum(p.shape[1] for p in pairs) * n
    return pl.pallas_call(
        functools.partial(body0, n),
        in_specs=[ANY, ANY] + [VM] * len(small),
        out_specs=[ANY, ANY] + [VM] * 7,
        out_shape=[shape_of(s, k) for s, k, _ in spread_shapes([lat_shard, first_shard], n)]
        + [shape_of((2, width), f32), shape_of((512, 384), bf16), shape_of((256, 256), bf16), shape_of((1152, 128), bf16),
           shape_of((128, 512), bf16), shape_of((2, 1280), f32), shape_of((2, ids.shape[1], 256), f32)],
        scratch_shapes=[pltpu.VMEM((8, 128), f32), pltpu.VMEM((n // 8, 2, 2, 2, 8, 128), f32), pltpu.VMEM((32, 384), f32)] + gather_scratch(3, n),
        compiler_params=pltpu.CompilerParams(collective_id=1, has_side_effects=True),
    )(lat_shard, first_shard, *small)


def run_ticks(step, n, ticks, at):
    @pl.when(step == 0)
    def _():
        greet(n)
    for j in range(3):
        @pl.when(step == at[j])
        def _(j=j):
            if j == 0:
                greeted(n)
            ticks[j]()


def strips(rows, width, body, init):
    return lax.fori_loop(0, rows // STRIP, lambda k, carry: body(pl.ds(pl.multiple_of(k * STRIP, STRIP), STRIP), carry), init, unroll=True)


FOLDS1 = ((256, 384, 32), (384, 896, 128))
FOLDS2 = ((256, 384, 32),)
FOLDS3 = ((256, 768, 128),)


def body1(n, raw, lat, band, fproj, mask, spair, fpair, held, *refs):
    shards, (fast4, lat_pre, fone_pre, n1), wholes, (wide, acc), rest = refs[:2], refs[2:6], refs[6:9], refs[9:11], refs[11:]
    step = pl.program_id(0)
    clear_first(step, acc)
    ticks, swap = (), rest
    if n > 1:
        first, *others = moves(n, (None,) + tuple(shards), wholes, rest)
        swap = rest[3 * GATHER_SEMS :]

        def begin():
            first.start("p", "c0")
            for m in others:
                m.start("z")
        def middle():
            first.wait("p")
            first.start("q", "c1")
        def late():
            first.wait("q")
            first.start("c2")
        def finish():
            first.wait("c0", "c1", "c2")
            for m in others:
                m.wait("z")
        ticks = (begin, middle, lambda: None, late, finish)
        run_ticks(step, n, ticks, (1, 4, 6))
    f = split_fours(raw, wide).astype(bf16)
    fast4[...] = f
    prev, nxt = mask[0], mask[1]
    z = dot_nt(f[:, :384], lat[:, 256:]) + shift(dot_nt(f[:, 256:], lat[:, :256]), prev, 1)
    lat_pre[...] = z
    add_moments(step, acc, 0, z)
    y = dot(f, band[...])
    z = y[:, :128] + shift(y[:, 128:256], prev, 1) + shift(y[:, 256:], nxt, -1)
    fone_pre[...] = z
    add_moments(step, acc, 256, z)
    z = jnp.concatenate([dot(f[:, :256], fproj[...]), dot(f[:, 256:], fproj[...])], axis=1)
    add_moments(step, acc, 384, z)
    close_moments(step, acc, ((spair, 0, 256), (fpair, 0, 128), (fpair, 768, 1280)), n1, f.shape[0] * STEPS, FOLDS1, n, ticks, *swap)


def stage1(raw, lat, band, fproj, mask, spair, fpair, held, shards_of, n):
    rows = raw.shape[0] * raw.shape[1] // 4
    return run(functools.partial(body1, n), rows,
        [(raw, "rows")] + [(v, "all") for v in (lat, band, fproj, mask, spair, fpair)] + [(v, "any") for v in (held,) + tuple(shards_of)],
        [((rows, 512), bf16, "rows"), ((rows, 256), f32, "rows"), ((rows, 128), f32, "rows"), ((4, 896), f32, "all")] + whole_shapes([held]) + spread_shapes(shards_of, n),
        [pltpu.VMEM((rows * 4 // STEPS, 128), f32), pltpu.VMEM((2, 8, 896), f32)] + (gather_scratch(3, n) if n > 1 else []), n, (2, 896), 2, {7: 4})


def body2(n, side, slow, lat_pre, fone_pre, n1, first, fmid, mask, spair, fpair, held_a, held_b, shard,
          lateral, one_pre, ftwo_pre, n2, whole_a, whole_b, whole_c, grid, acc, *rest):
    step = pl.program_id(0)
    rows = slow.shape[0]
    n_lat, n_fone = n1[:, :256], n1[:, 256:384]
    ticks, swap = (), rest
    if n > 1:
        middle, last, proj = moves(n, (None, None, shard), (whole_a, whole_b, whole_c), rest)
        swap = rest[3 * GATHER_SEMS :]

        def begin():
            middle.start("p", "c0")
            last.start("p", "c0")
            proj.start("z")
        def half():
            middle.wait("p")
            middle.start("q", "c1")
        def late():
            proj.wait("z")
            proj.start("p", "c0")
        def close():
            middle.wait("q")
            middle.start("c2")
        def finish():
            last.wait("p", "c0")
            proj.wait("p", "c0")
            middle.wait("c0", "c1", "c2")
        ticks = (begin, half, late, close, finish)
        run_ticks(step, n, ticks, (1, 3, 5))

    def put(block):
        part = fone_pre[pl.ds(pl.multiple_of(block * rows, 16), rows), :]
        fill(grid, side, silu(acted(part, n_fone)).astype(bf16), block)

    @pl.when(step == 0)
    def _():
        clear(grid)
        clear(acc)
        put(0)

    put(jnp.minimum(step + 1, STEPS - 1))
    lat = silu(acted(lat_pre[...], n_lat)).astype(bf16)
    lateral[...] = lat
    joined = jnp.concatenate([slow[...], lat], axis=1)
    z = dot(joined, first[1]) + shift(dot(joined, first[0]), mask[0], 1) + shift(dot(joined, first[2]), mask[1], -1)
    one_pre[...] = z
    add_moments(step, acc, 0, z)
    z = dot(tap_columns(grid, side, step, rows, False), fmid[...])
    ftwo_pre[...] = z
    add_moments(step, acc, 256, z)
    close_moments(step, acc, ((spair, 256, 512), (fpair, 128, 256)), n2, rows * STEPS, FOLDS2, n, ticks, *swap)


def stage2(slow, lat_pre, fone_pre, n1, first, fmid, mask, spair, fpair, held, shard, side, n):
    rows = slow.shape[0]
    frames = rows // side**2
    return run(functools.partial(body2, n, side), rows,
        [(slow, "rows"), (lat_pre, "rows")] + [(v, "all") for v in (fone_pre, n1, first, fmid, mask, spair, fpair)] + [(v, "any") for v in tuple(held) + (shard,)],
        [((rows, 256), bf16, "rows"), ((rows, 256), f32, "rows"), ((rows, 128), f32, "rows"), ((4, 384), f32, "all")] + whole_shapes(held) + spread_shapes([shard], n),
        [pltpu.VMEM(((side + 2) ** 2 * frames, 128), bf16), pltpu.VMEM((2, 8, 384), f32)] + (gather_scratch(3, n) if n > 1 else []), n, (2, 384), 3, {9: 4, 10: 5})


def body3(n, side, one_pre, ftwo_pre, n2, middle, flast, spair, fpair, held_a, held_b, two_pre, ftwo, n3, whole_a, whole_b, grid, acc, *rest):
    step = pl.program_id(0)
    rows = two_pre.shape[0]
    n_one, n_ftwo = n2[:, :256], n2[:, 256:]
    ticks, swap = (), rest
    if n > 1:
        both = moves(n, (None, None), (whole_a, whole_b), rest)
        swap = rest[2 * GATHER_SEMS :]

        def begin():
            for m in both:
                m.start("q", "c1")
        def half():
            for m in both:
                m.wait("q")
                m.start("c2")
        def finish():
            for m in both:
                m.wait("c1", "c2")
        ticks = (begin, half, lambda: None, lambda: None, finish)
        run_ticks(step, n, ticks, (1, 5, 6))

    def put(block):
        part = one_pre[pl.ds(pl.multiple_of(block * rows, 16), rows), :]
        fill(grid, side, silu(acted(part, n_one)).astype(bf16), block)

    @pl.when(step == 0)
    def _():
        clear(grid)
        clear(acc)
        put(0)

    put(jnp.minimum(step + 1, STEPS - 1))
    z = dot(tap_columns(grid, side, step, rows, False), middle[...])
    two_pre[...] = z
    add_moments(step, acc, 0, z)
    f = silu(acted(ftwo_pre[...], n_ftwo)).astype(bf16)
    ftwo[...] = f
    for k in range(2):
        add_moments(step, acc, 256 * (k + 1), dot(f, flast[:, 256 * k : 256 * (k + 1)]))
    close_moments(step, acc, ((spair, 512, 768), (fpair, 256, 768)), n3, rows * STEPS, FOLDS3, n, ticks, *swap)


def stage3(one_pre, ftwo_pre, n2, middle, flast, spair, fpair, held, side, n):
    rows = one_pre.shape[0]
    frames = rows // side**2
    return run(functools.partial(body3, n, side), rows,
        [(one_pre, "all"), (ftwo_pre, "rows")] + [(v, "all") for v in (n2, middle, flast, spair, fpair)] + [(v, "any") for v in held],
        [((rows, 256), f32, "rows"), ((rows, 128), bf16, "rows"), ((4, 768), f32, "all")] + whole_shapes(held),
        [pltpu.VMEM(((side + 2) ** 2 * frames, 256), bf16), pltpu.VMEM((2, 8, 768), f32)] + (gather_scratch(2, n) if n > 1 else []), n, (2, 768), 4, {7: 3, 8: 4})


def body4(n, two_pre, slow, lateral, n3, last, proj, spair, two, proj_pre, n4, acc, *swap):
    step = pl.program_id(0)
    clear_first(step, acc)
    v = silu(acted(two_pre[...], n3[:, :256])).astype(bf16)
    two[...] = v
    for k in range(4):
        add_moments(step, acc, 256 * k, dot(v, last[:, 256 * k : 256 * (k + 1)]))
    joined = jnp.concatenate([slow[...], lateral[...]], axis=1)
    for k in range(4):
        z = dot(joined, proj[:, 256 * k : 256 * (k + 1)])
        proj_pre[:, 256 * k : 256 * (k + 1)] = z.astype(proj_pre.dtype)
        add_moments(step, acc, 1024 + 256 * k, z)
    if n > 1:
        @pl.when(step == 0)
        def _():
            greet(n)
    close_moments(step, acc, ((spair, 768, 2816),), n4, v.shape[0] * STEPS, (), n,
        (None, None, None, lambda: greeted(n), lambda: None), *swap)


def stage4(two_pre, slow, lateral, n3, last, proj, spair, n):
    rows = two_pre.shape[0]
    return run(functools.partial(body4, n), rows,
        [(v, "rows") for v in (two_pre, slow, lateral)] + [(v, "all") for v in (n3, last, proj, spair)],
        [((rows, 256), bf16, "rows"), ((rows, 1024), f32, "rows"), ((4, 2048), f32, "all")], [pltpu.VMEM((2, 8, 2048), f32)], n, (2, 2048), 5)


def body5(two, proj_pre, cot, fast4, ftwo, fcot, n1, n3, n4, last, fproj, flast,
          slow_out, fast_out, delta, fdelta, sums, wide, three, fthree, fskip, fgrad, fout, acc):
    step = pl.program_id(0)
    rows = two.shape[0]
    clear_first(step, acc)
    fgrad[...] = split_fours(fcot, wide)
    three[...] = dot(two[...], last[...])
    fthree[...] = dot(ftwo[...], flast[...])
    for k in range(2):
        fskip[:, 256 * k : 256 * (k + 1)] = dot(fast4[:, 256 * k : 256 * (k + 1)], fproj[...])

    def side_of(za, zb, grad, na, nb, out, keep, lo, lanes):
        ga, gb, base = 0.5 * na[1:2] * na[2:3], 0.5 * nb[1:2] * nb[2:3], 0.5 * (na[3:4] + nb[3:4])
        ma, mb = na[0:1], nb[0:1]
        def one(at, carry):
            ha = za[at, lanes].astype(f32) - ma
            hb = zb[at, lanes].astype(f32) - mb
            h = ha * ga + hb * gb + base
            th = jnp.tanh(h)
            u = 1.0 + th
            out[at, lanes] = (h * u).astype(out.dtype)
            d = (0.5 * grad[at, lanes].astype(f32)) * (u * (1.0 + h * (1.0 - th)))
            keep[at, lanes] = d
            return carry[0] + eighth(d), carry[1] + eighth(d * ha), carry[2] + eighth(d * hb)
        zero = jnp.zeros((8, 256), f32)
        add_sums(step, acc, lo, strips(rows, 256, one, (zero, zero, zero)))

    for k in range(4):
        lanes = slice(256 * k, 256 * (k + 1))
        side_of(three, proj_pre, cot, n4[:, lanes], n4[:, 1024 + 256 * k : 1280 + 256 * k], slow_out, delta, 256 * k, lanes)
    for k in range(2):
        lanes = slice(256 * k, 256 * (k + 1))
        side_of(fthree, fskip, fgrad, n3[:, 256 + 256 * k : 512 + 256 * k], n1[:, 384 + 256 * k : 640 + 256 * k], fout, fdelta, 1024 + 256 * k, lanes)
    join_fours(fout[...], wide, fast_out)

    @pl.when(step == STEPS - 1)
    def _():
        scales = (1.0, jnp.concatenate([n4[1:2, :1024], n3[1:2, 256:]], axis=1), jnp.concatenate([n4[1:2, 1024:], n1[1:2, 384:]], axis=1))
        for k in range(3):
            sums[k : k + 1] = jnp.sum(acc[k], axis=0, keepdims=True) * scales[k]


def stage5(two, proj_pre, cot, fast4, ftwo, fcot, n1, n3, n4, last, fproj, flast):
    rows = two.shape[0]
    part = rows // STEPS
    return run(body5, rows,
        [(two, "rows"), (proj_pre, "rows"), (cot, "rows"), (fast4, "rows"), (ftwo, "rows"), (fcot, "rows"),
         (n1, "all"), (n3, "all"), (n4, "all"), (last, "all"), (fproj, "all"), (flast, "all")],
        [((rows, 1024), bf16, "rows"), (fcot.shape, bf16, "rows"), ((rows, 1024), f32, "rows"), ((rows, 512), f32, "rows"), ((3, 1536), f32, "all")],
        [pltpu.VMEM((part * 4, 128), f32), pltpu.VMEM((part, 1024), f32), pltpu.VMEM((part, 512), f32), pltpu.VMEM((part, 512), f32),
         pltpu.VMEM((part, 512), f32), pltpu.VMEM((part, 512), f32), pltpu.VMEM((3, 8, 1536), f32)])


def body5x(n, own, out, *links):
    greet(n)
    greeted(n)
    sum_pack(total_of(n, False, own, *links), out, ((1024, 1536, 128),))


def stage5x(sums, n):
    return pl.pallas_call(
        functools.partial(body5x, n),
        in_specs=[pl.BlockSpec(memory_space=pltpu.VMEM)],
        out_specs=pl.BlockSpec(memory_space=pltpu.VMEM),
        out_shape=jax.ShapeDtypeStruct(sums.shape, f32),
        scratch_shapes=swap_scratch(sums.shape, n),
        compiler_params=pltpu.CompilerParams(collective_id=6, has_side_effects=True),
    )(sums)


def body6(n, total, two, two_pre, proj_pre, slow, lateral, delta, fast4, ftwo, ftwo_pre, fdelta, n1, n2, n3, n4, s5, last, fproj, flast,
          d_proj, d_fproj, last_term, proj_term, flast_term, e_two, e_ftwo, sums,
          three, fthree, fskip, d_three, d_fthree, acc, last_acc, proj_acc, *swap):
    step = pl.program_id(0)
    rows = two.shape[0]
    clear_first(step, acc, last_acc, proj_acc, flast_term)
    three[...] = dot(two[...], last[...])
    fthree[...] = dot(ftwo[...], flast[...])
    for k in range(2):
        fskip[:, 256 * k : 256 * (k + 1)] = dot(fast4[:, 256 * k : 256 * (k + 1)], fproj[...])

    def side_of(za, zb, e, na, nb, s, da, db, lanes):
        pa, pb = na[2:3] * na[1:2], nb[2:3] * nb[1:2]
        qa, qb = pa * na[1:2] * s[1:2], pb * nb[1:2] * s[2:3]
        ma, mb, base = na[0:1], nb[0:1], s[0:1]
        def one(at, carry):
            d = e[at, lanes] - base
            da[at, lanes] = (d * pa - (za[at, lanes].astype(f32) - ma) * qa).astype(bf16)
            db[at, lanes] = (d * pb - (zb[at, lanes].astype(f32) - mb) * qb).astype(bf16)
            return carry
        strips(rows, 256, one, 0)

    for k in range(4):
        lanes = slice(256 * k, 256 * (k + 1))
        side_of(three, proj_pre, delta, n4[:, lanes], n4[:, 1024 + 256 * k : 1280 + 256 * k], s5[:, lanes] * (1.0 / total), d_three, d_proj, lanes)
    for k in range(2):
        lanes = slice(256 * k, 256 * (k + 1))
        side_of(fthree, fskip, fdelta, n3[:, 256 + 256 * k : 512 + 256 * k], n1[:, 384 + 256 * k : 640 + 256 * k],
                s5[:, 1024 + 256 * k : 1280 + 256 * k] * (0.25 / total), d_fthree, d_fproj, lanes)

    wide = slow.shape[1]
    last_acc[...] += dot_tn(two[...], d_three[...])
    proj_acc[:wide] += dot_tn(slow[...], d_proj[...])
    proj_acc[wide:] += dot_tn(lateral[...], d_proj[...])
    flast_term[...] += dot_tn(ftwo[...], d_fthree[...])
    h = normed(two_pre[...], n3[:, :256])
    e = dot_nt(d_three[...], last[...]) * slope(scaled(h, n3[:, :256]))
    e_two[...] = e
    add_sums(step, acc, 0, (eighth(e), eighth(e * h)))
    h = normed(ftwo_pre[...], n2[:, 256:])
    e = dot_nt(d_fthree[...], flast[...]) * slope(scaled(h, n2[:, 256:]))
    e_ftwo[...] = e
    add_sums(step, acc, 256, (eighth(e), eighth(e * h)))
    close_sums(step, acc, sums, ((256, 384, 32),), n, (), *swap)

    @pl.when(step == STEPS - 1)
    def _():
        last_term[...] = last_acc[...].astype(bf16)
        proj_term[...] = proj_acc[...].astype(bf16)


def stage6(total, two, two_pre, proj_pre, slow, lateral, delta, fast4, ftwo, ftwo_pre, fdelta, n1, n2, n3, n4, s5, last, fproj, flast, n):
    rows = two.shape[0]
    part = rows // STEPS
    return run(functools.partial(body6, n, total), rows,
        [(a, "rows") for a in (two, two_pre, proj_pre, slow, lateral, delta, fast4, ftwo, ftwo_pre, fdelta)]
        + [(a, "all") for a in (n1, n2, n3, n4, s5, last, fproj, flast)],
        [((rows, 1024), bf16, "rows"), ((rows, 512), bf16, "rows"), ((256, 1024), bf16, "all"), ((1280, 1024), bf16, "all"), ((128, 512), f32, "all"),
         ((rows, 256), f32, "rows"), ((rows, 128), f32, "rows"), ((2, 384), f32, "all")],
        [pltpu.VMEM((part, 1024), f32), pltpu.VMEM((part, 512), f32), pltpu.VMEM((part, 512), f32),
         pltpu.VMEM((part, 1024), bf16), pltpu.VMEM((part, 512), bf16), pltpu.VMEM((2, 8, 384), f32),
         pltpu.VMEM((256, 1024), f32), pltpu.VMEM((1280, 1024), f32)], n, (2, 384), 7)


def body7(n, side, total, one_pre, two_pre, e_two, fone_pre, ftwo_pre, e_ftwo, n1, n2, n3, s6, middle, fmid, proj_term,
          middleerm, fmid_term, e_one, e_fone, sums, proj_grad, grid, fgrid, acc, mid_acc, *rest):
    step = pl.program_id(0)
    ticks, swap = (), rest
    if n > 1:
        ticks = scatter_ticks(n, (proj_term,), (proj_grad,), rest[:11])
        swap = rest[11:]
        run_ticks(step, n, ticks, (1, 3, 5))
    rows = one_pre.shape[0]

    def put(block):
        at = pl.ds(pl.multiple_of(block * rows, 16), rows)
        p, s = n3[:, :256], s6[:, :256] * (1.0 / total)
        fill(grid, side, input_grad(e_two[at, :], normed(two_pre[at, :], p), p, s[0:1], s[1:2]), block)
        p, s = n2[:, 256:], s6[:, 256:] * (0.25 / total)
        fill(fgrid, side, input_grad(e_ftwo[at, :], normed(ftwo_pre[at, :], p), p, s[0:1], s[1:2]), block)

    @pl.when(step == 0)
    def _():
        clear(grid)
        clear(fgrid)
        clear(acc)
        put(0)
        mid_acc[...] = jnp.zeros_like(mid_acc)
        fmid_term[...] = jnp.zeros_like(fmid_term)

    put(jnp.minimum(step + 1, STEPS - 1))

    def one_side(pre, p, columns, weight, lo, term, e_out):
        h = normed(pre[...], p)
        act = scaled(h, p)
        s = sigma(act)
        mid = act * s
        term[...] += dot_tn(mid.astype(bf16), columns)
        width = weight.shape[1]
        turned = jnp.concatenate([weight[width * k : width * (k + 1)] for k in range(9)], axis=1)
        e = dot_nt(columns, turned) * (s + mid * (1.0 - s))
        e_out[...] = e
        add_sums(step, acc, lo, (eighth(e), eighth(e * h)))

    one_side(one_pre, n2[:, :256], tap_columns(grid, side, step, rows, True), middle, 0, mid_acc, e_one)
    one_side(fone_pre, n1[:, 256:384], tap_columns(fgrid, side, step, rows, True), fmid, 256, fmid_term, e_fone)
    close_sums(step, acc, sums, ((256, 384, 32),), n, ticks, *swap)

    @pl.when(step == STEPS - 1)
    def _():
        for k in range(9):
            middleerm[k] = mid_acc[:, 256 * k : 256 * (k + 1)].astype(bf16)


def stage7(total, one_pre, two_pre, e_two, fone_pre, ftwo_pre, e_ftwo, n1, n2, n3, s6, middle, fmid, proj_term, side, n):
    terms = [six(v, n) for v in (proj_term,)] if n > 1 else [proj_term]
    parts = [(v.shape[0] // n, v.shape[1]) for v in (proj_term,)]
    rows = one_pre.shape[0]
    frames = rows // side**2
    return run(functools.partial(body7, n, side, total), rows,
        [(one_pre, "rows"), (two_pre, "all"), (e_two, "all"), (fone_pre, "rows"), (ftwo_pre, "all"), (e_ftwo, "all")]
        + [(a, "all") for a in (n1, n2, n3, s6, middle, fmid)] + [(v, "any") for v in terms],
        [((9, 256, 256), bf16, "all"), ((128, 1152), f32, "all"), ((rows, 256), f32, "rows"), ((rows, 128), f32, "rows"), ((2, 384), f32, "all")] + [(part, f32, "all") for part in parts],
        [pltpu.VMEM(((side + 2) ** 2 * frames, 256), bf16), pltpu.VMEM(((side + 2) ** 2 * frames, 128), bf16),
         pltpu.VMEM((2, 8, 384), f32), pltpu.VMEM((256, 2304), f32)] + (scatter_scratch(parts, n) if n > 1 else []), n, (2, 384), 8)


def body8(n, total, slow, lateral, one_pre, e_one, n2, s7, mask, middleerm, first_term, pieces, middle_grad, first_acc, *rest):
    step = pl.program_id(0)
    if n > 1:
        ticks = scatter_ticks(n, (middleerm,), (middle_grad,), rest)
        run_ticks(step, n, ticks, (1, 2, 4))

        @pl.when(step == STEPS - 1)
        def _():
            ticks[3]()
    clear_first(step, first_acc)
    p, s = n2[:, :256], s7[:, :256] * (1.0 / total)
    d = input_grad(e_one[...], normed(one_pre[...], p), p, s[0:1], s[1:2])
    w = d.astype(f32)
    rows = w.shape[0]
    before = pltpu.roll(masked(w, mask[0]), rows - 1, 0).astype(bf16)
    after = pltpu.roll(masked(w, mask[1]), 1, 0).astype(bf16)
    columns = jnp.concatenate([before, d, after], axis=1)
    pieces[...] = columns
    wide = slow.shape[1]
    first_acc[:wide] += dot_tn(slow[...], columns)
    first_acc[wide:] += dot_tn(lateral[...], columns)

    @pl.when(step == STEPS - 1)
    def _():
        for k in range(3):
            first_term[k] = first_acc[:, 256 * k : 256 * (k + 1)].astype(bf16)
        if n > 1:
            ticks[4]()


def stage8(total, slow, lateral, one_pre, e_one, n2, s7, mask, middleerm, n):
    rows = slow.shape[0]
    part = (middleerm.shape[0] // n, middleerm.shape[1])
    return run(functools.partial(body8, n, total), rows,
        [(a, "rows") for a in (slow, lateral, one_pre, e_one)] + [(a, "all") for a in (n2, s7, mask)]
        + [(six(middleerm, n) if n > 1 else middleerm, "any")],
        [((3, 1280, 256), bf16, "all"), ((rows, 768), bf16, "rows"), (part, f32, "all")],
        [pltpu.VMEM((1280, 768), f32)] + (scatter_scratch([part], n) if n > 1 else []), n, None, 12)


def body8b(n, pieces, d_proj, lat_pre, n1, first, proj, last_term, first_term,
           slow_grad, e_lat, sums, last_grad, first_grad, acc, *rest):
    step = pl.program_id(0)
    ticks, swap = (), rest
    if n > 1:
        ticks = scatter_ticks(n, (last_term, first_term), (last_grad, first_grad), rest[:16])
        swap = rest[16:]
        run_ticks(step, n, ticks, (1, 3, 5))
    clear_first(step, acc)
    wide = proj.shape[0] - 256

    def back(lo, hi):
        part = dot_nt(d_proj[...], proj[lo:hi])
        for k in range(3):
            part += dot_nt(pieces[:, 256 * k : 256 * (k + 1)], first[k, lo:hi])
        return part

    for k in range(4):
        slow_grad[:, 256 * k : 256 * (k + 1)] = back(256 * k, 256 * (k + 1)).astype(bf16)
    h = normed(lat_pre[...], n1[:, :256])
    e = back(wide, wide + 256) * slope(scaled(h, n1[:, :256]))
    e_lat[...] = e
    add_sums(step, acc, 0, (eighth(e), eighth(e * h)))
    close_sums(step, acc, sums, (), n, ticks, *swap)


def stage8b(pieces, d_proj, lat_pre, n1, first, proj, last_term, first_term, n):
    rows = pieces.shape[0]
    terms = [six(v, n) if n > 1 else v for v in (last_term, first_term)]
    parts = [(v.shape[0] // n, v.shape[1]) for v in (last_term, first_term)]
    return run(functools.partial(body8b, n), rows,
        [(a, "rows") for a in (pieces, d_proj, lat_pre)] + [(a, "all") for a in (n1, first, proj)] + [(v, "any") for v in terms],
        [((rows, 1024), bf16, "rows"), ((rows, 256), f32, "rows"), ((2, 256), f32, "all")] + [(part, f32, "all") for part in parts],
        [pltpu.VMEM((2, 8, 256), f32)] + (scatter_scratch(parts, n) if n > 1 else []), n, (2, 256), 9)


def lanes_at(v, source, target):
    moved = pltpu.roll(v, (target - source) % 128, 1) if target != source else v
    lane = lax.broadcasted_iota(jnp.int32, v.shape, 1)
    return jnp.where((lane >= target) & (lane < target + 32), moved, 0.0)


def pack_fast(out, band, fproj, flast, fmid):
    places_of = (
        ((0, 0, 1), (0, 1, 2), (0, 2, 3), (1, 3, 0)),
        ((0, 0, 0), (0, 1, 1), (0, 2, 2), (0, 3, 3)),
        ((0, 1, 0), (0, 2, 1), (0, 3, 2), (2, 0, 3)),
    )
    for tap in range(3):
        out[32 * tap : 32 * (tap + 1)] = sum(
            band[128 * part + 32 * j : 128 * part + 32 * (j + 1), 128 * k : 128 * (k + 1)] for part, k, j in places_of[tap])
    out[96:224] = fproj[...]
    out[224:256] = sum(flast[32 * k : 32 * (k + 1), 128 * k : 128 * (k + 1)] for k in range(4))
    for group in range(3):
        total = None
        for tap in range(4 * group, min(4 * group + 4, 9)):
            for k in range(4):
                turned = fmid[:, 128 * tap : 128 * (tap + 1)].T
                v = lanes_at(turned[32 * k : 32 * (k + 1)], 32 * k, 32 * (tap % 4))
                total = v if total is None else total + v
        out[256 + 32 * group : 288 + 32 * group] = total
    out[352:384] = jnp.zeros((32, 128), f32)


def own_pair(out, sums, lo, hi, row):
    share = out.shape[1]
    back = lax.rem(hi - lo - lax.axis_index("fsdp") * share, hi - lo)
    for at, k in enumerate((row, 0)):
        wide = jnp.broadcast_to(sums[k : k + 1, lo:hi], (8, hi - lo))
        out[at : at + 1] = pltpu.roll(wide, back, 1)[0:1, :share]


def body9(n, total, fast4, lat_pre, e_lat, fone_pre, e_fone, d_fproj, ready, n1, s5, s6, s7, s8, lat, band, fproj, mask, flast_term, fmid_term,
          ready_first, ready_middle, ready_last, ready_proj, lat_term, packed, raw, slow_grad, lat_n, one_n, two_n, out_n, proj_n, mid_n, fout_n,
          first_grad, middle_grad, last_grad, proj_grad, wide, lat_acc, whole, band_term, fproj_term):
    step = pl.program_id(0)
    clear_first(step, lat_acc, band_term, fproj_term)
    slow_grad[...] = ready[...]
    rows = fast4.shape[0]
    def backward(e, pre, p, s):
        d = input_grad(e[...], normed(pre[...], p), p, s[0:1], s[1:2])
        w = d.astype(f32)
        return d, pltpu.roll(masked(w, mask[0]), rows - 1, 0).astype(bf16), pltpu.roll(masked(w, mask[1]), 1, 0).astype(bf16)
    d, before, _ = backward(e_lat, lat_pre, n1[:, :256], s8[...] * (1.0 / total))
    f, fbefore, fafter = backward(e_fone, fone_pre, n1[:, 256:384], s7[:, 256:] * (0.25 / total))
    narrow = jnp.concatenate([f, fbefore, fafter], axis=1)
    lat_acc[:, :256] += dot_tn(before, fast4[:, 256:])
    lat_acc[:, 256:] += dot_tn(d, fast4[:, :384])
    band_term[...] += dot_tn(narrow, fast4[...])
    for k in range(4):
        fproj_term[...] += dot_tn(fast4[:, 128 * k : 128 * (k + 1)], d_fproj[:, 128 * k : 128 * (k + 1)])
    base = dot_nt(narrow, band[...])
    skip = jnp.concatenate([dot_nt(d_fproj[:, 256 * k : 256 * (k + 1)], fproj[...]) for k in range(2)], axis=1)
    whole[...] = base + skip
    whole[:, :384] += dot(d, lat[:, 256:])
    whole[:, 256:] += dot(before, lat[:, :256])
    join_fours(whole[...], wide, raw)

    @pl.when(step == STEPS - 1)
    def _():
        lat_term[...] = lat_acc[...].astype(bf16)
        for grad, found in ((first_grad, ready_first), (middle_grad, ready_middle), (last_grad, ready_last), (proj_grad, ready_proj)):
            grad[...] = found[...]
        pack_fast(packed, band_term, fproj_term, flast_term, fmid_term)
        if n > 1:
            own_pair(lat_n, s8, 0, 256, 1)
            own_pair(one_n, s7, 0, 256, 1)
            own_pair(two_n, s6, 0, 256, 1)
            own_pair(out_n, s5, 0, 1024, 1)
            own_pair(proj_n, s5, 0, 1024, 2)
        for j, (sums, lo, row) in enumerate(((s7, 256, 1), (s6, 256, 1))):
            mid_n[j, 0:1] = sums[row : row + 1, lo : lo + 32]
            mid_n[j, 1:2] = sums[0:1, lo : lo + 32]
        for j in range(2):
            fout_n[j, 0:1] = s5[j + 1 : j + 2, 1024:1152]
            fout_n[j, 1:2] = s5[0:1, 1024:1152]


def stage9(total, fast4, lat_pre, e_lat, fone_pre, e_fone, d_fproj, ready, n1, s5, s6, s7, s8, lat, band, fproj, mask, flast_term, fmid_term, grads, n):
    rows = fast4.shape[0]
    part = rows // STEPS
    return run(functools.partial(body9, n, total), rows,
        [(a, "rows") for a in (fast4, lat_pre, e_lat, fone_pre, e_fone, d_fproj, ready)]
        + [(a, "all") for a in (n1, s5, s6, s7, s8, lat, band, fproj, mask, flast_term, fmid_term) + tuple(grads)],
        [((256, 640), bf16, "all"), ((384, 128), f32, "all"), ((rows // 16, 64, 128), bf16, "rows"), (ready.shape, bf16, "rows")]
        + [((2, 256 // n), f32, "all")] * 3 + [((2, 1024 // n), f32, "all")] * 2 + [((2, 2, 32), f32, "all"), ((2, 2, 128), f32, "all")] + [(v.shape, f32, "all") for v in grads],
        [pltpu.VMEM((part * 4, 128), f32), pltpu.VMEM((256, 640), f32), pltpu.VMEM((part, 512), f32),
         pltpu.VMEM((384, 512), f32), pltpu.VMEM((128, 128), f32)])


def body10(n, lat_term, packed, lat_grad, first_t, middle_t, last, proj, sums, slots, line, mine, lat_slots, lat_line, lat_mine,
           a_send, a_recv, b_send, b_recv, g_send, g_recv, l_send, l_recv, m_send, m_recv):
    me = lax.axis_index("fsdp")
    mi, mo, depth = lax.rem(me, INNER), lax.div(me, INNER), n // INNER
    peers = [mo * INNER + lax.rem(mi + k, INNER) for k in range(INNER)]
    spots = [lax.rem(mi + k, INNER) for k in range(INNER)]
    beyond = [lax.rem(mo + k, depth) for k in range(depth)]

    def remote(src, dst, send, recv, peer):
        copy = pltpu.make_async_remote_copy(
            src_ref=src, dst_ref=dst, send_sem=send, recv_sem=recv, device_id=(peer,), device_id_type=MESH)
        copy.start()
        return copy

    greet(n)
    greeted(n)
    fast = [remote(packed.at[spots[k]], slots.at[mi], a_send.at[k], a_recv.at[k], peers[k]) for k in range(1, INNER)]
    slow = [remote(lat_term.at[:, spots[k]], lat_slots.at[mi], l_send.at[k], l_recv.at[k], peers[k]) for k in range(1, INNER)]
    slots[mi] = packed[mi]
    lat_slots[mi] = lat_term[:, mi]
    for copy in fast:
        copy.wait()
    mine[...] = sum(slots[k] for k in range(1, INNER)) + slots[0]
    fast = [remote(mine, line.at[mo], b_send.at[k], b_recv.at[k], beyond[k] * INNER + mi) for k in range(1, depth)]
    line[mo] = mine[...]
    for copy in slow:
        copy.wait()
    lat_mine[...] = sum(lat_slots[k].astype(f32) for k in range(INNER)).astype(bf16)
    slow = [remote(lat_mine.at[beyond[k]], lat_line.at[mo], m_send.at[k], m_recv.at[k], beyond[k] * INNER + mi) for k in range(1, depth)]
    lat_line[mo] = lat_mine[mo]
    for copy in fast:
        copy.wait()
    sums[mi] = sum((line[k] for k in range(1, depth)), line[0])
    fast = [remote(sums.at[mi], sums.at[mi], g_send.at[k], g_recv.at[k], peers[k]) for k in range(1, INNER)]
    for copy in slow:
        copy.wait()
    lat_grad[...] = sum(lat_line[k].astype(f32) for k in range(depth))
    for copy in fast:
        copy.wait()

    high = sums.shape[1]
    def rows_of(lo, hi):
        found = []
        while lo < hi:
            top = min(hi, (lo // high + 1) * high)
            found.append(sums[lo // high, lo % high : lo % high + top - lo])
            lo = top
        return jnp.concatenate(found, axis=0) if len(found) > 1 else found[0]

    for k in range(3):
        first_t[:, 128 * k : 128 * (k + 1)] = rows_of(32 * k, 32 * (k + 1))
        wide = min(128, 288 - 128 * k)
        middle_t[:, 128 * k : 128 * k + wide] = rows_of(256 + 32 * k, 288 + 32 * k)[:, :wide]
    proj[...] = rows_of(96, 224)
    last[...] = rows_of(224, 256)


def stage10(lat_term, packed, n):
    depth, DS = n // INNER, pltpu.SemaphoreType.DMA
    packed = packed.reshape(INNER, -1, 128)
    chunk = packed.shape[1:]
    share = (lat_term.shape[0] // n, lat_term.shape[1])
    lat_grad, first_t, middle_t, last, proj = pl.pallas_call(
        functools.partial(body10, n),
        in_specs=[pl.BlockSpec(memory_space=pltpu.VMEM)] * 2,
        out_specs=[pl.BlockSpec(memory_space=pltpu.VMEM)] * 5,
        out_shape=[jax.ShapeDtypeStruct(shape, f32) for shape in (share, (32, 384), (32, 288), (32, 128), (128, 128))],
        scratch_shapes=[pltpu.VMEM((INNER,) + chunk, f32), pltpu.VMEM((INNER,) + chunk, f32), pltpu.VMEM((depth,) + chunk, f32), pltpu.VMEM(chunk, f32),
            pltpu.VMEM((INNER, depth) + share, bf16), pltpu.VMEM((depth,) + share, bf16), pltpu.VMEM((depth,) + share, bf16)]
        + [DS((INNER,)), DS((INNER,)), DS((depth,)), DS((depth,)), DS((INNER,)), DS((INNER,)), DS((INNER,)), DS((INNER,)), DS((depth,)), DS((depth,))],
        compiler_params=pltpu.CompilerParams(collective_id=10, has_side_effects=True),
    )(lat_term.reshape((depth, INNER) + share), packed)
    lat_grad, first_t, middle_t, last, proj = stage11((lat_grad, first_t, middle_t, last, proj))
    return lat_grad, (first_t.T, middle_t.T, last, proj)


def body11(*refs):
    half = len(refs) // 2
    for source, target in zip(refs[:half], refs[half:]):
        target[...] = source[...]


def stage11(arrays):
    VM = pl.BlockSpec(memory_space=pltpu.VMEM)
    return pl.pallas_call(
        body11,
        in_specs=[VM] * len(arrays),
        out_specs=[VM] * len(arrays),
        out_shape=[jax.ShapeDtypeStruct(v.shape, v.dtype) for v in arrays],
    )(*arrays)


def shards(slow_in, fast_in, clip_ids, lateral_weight, first_weight, middle_weight, last_weight, proj_weight,
           lat_norm, one_norm, two_norm, out_norm, proj_norm, fast_first, fast_middle, fast_last, fast_proj,
           fast_mid_norm, fast_out_norm, slow_cot, fast_cot):
    n = lax.axis_size("fsdp")
    side = slow_in.shape[1]
    count = slow_in.shape[0] * side * side * n
    lat, first, spair, band, fproj, fmid, flast, fpair, mask = stage0(
        lateral_weight.T, first_weight, (lat_norm, one_norm, two_norm, out_norm, proj_norm),
        (fast_first.T, fast_middle.T, fast_last, fast_proj, fast_mid_norm, fast_out_norm), clip_ids, n)
    lat = gathered(lat, n)

    def rows(v):
        return v.transpose(1, 2, 0, 3).reshape(-1, v.shape[3])
    def unrows(v):
        return v.reshape(side, side, -1, v.shape[1]).transpose(2, 0, 1, 3)
    def raw(v):
        return v.transpose(1, 2, 0, 3).reshape(side * side, -1, v.shape[3])
    def unraw(v):
        return v.reshape((side, side) + v.shape[1:]).transpose(2, 0, 1, 3)

    slow = rows(slow_in)
    fast4, lat_pre, fone_pre, n1, first, *held = stage1(
        raw(fast_in), lat, band, fproj, mask, spair, fpair, first, (middle_weight, last_weight), n)
    first = gathered(first, n).reshape(3, -1, first_weight.shape[1])
    lateral, one_pre, ftwo_pre, n2, middle, last, proj = stage2(
        slow, lat_pre, fone_pre, n1, first, fmid, mask, spair, fpair, held, proj_weight, side, n)
    middle = gathered(middle, n)
    two_pre, ftwo, n3, last, proj = stage3(one_pre, ftwo_pre, n2, middle, flast, spair, fpair, (last, proj), side, n)
    last, proj = gathered(last, n), gathered(proj, n)
    two, proj_pre, n4 = stage4(two_pre, slow, lateral, n3, last, proj, spair, n)
    slow_out, fast_out, delta, fdelta, local = stage5(
        two, proj_pre, rows(slow_cot), fast4, ftwo, raw(fast_cot), n1, n3, n4, last, fproj, flast)
    s5 = stage5x(local, n)
    d_proj, d_fproj, last_term, proj_term, flast_term, e_two, e_ftwo, s6 = stage6(
        count, two, two_pre, proj_pre, slow, lateral, delta, fast4, ftwo, ftwo_pre, fdelta, n1, n2, n3, n4, s5, last, fproj, flast, n)
    middle_term, fmid_term, e_one, e_fone, s7, proj_grad = stage7(
        count, one_pre, two_pre, e_two, fone_pre, ftwo_pre, e_ftwo, n1, n2, n3, s6, middle, fmid, proj_term, side, n)
    first_term, pieces, middle_grad = stage8(count, slow, lateral, one_pre, e_one, n2, s7, mask, middle_term.reshape(-1, 256), n)
    slow_grad, e_lat, s8, last_grad, first_grad = stage8b(
        pieces, d_proj, lat_pre, n1, first, proj, last_term, first_term.reshape(-1, 256), n)
    lat_term, packed, fast_grad, slow_grad, *small = stage9(
        count, fast4, lat_pre, e_lat, fone_pre, e_fone, d_fproj, slow_grad, n1, s5, s6, s7, s8, lat, band, fproj, mask, flast_term, fmid_term,
        (first_grad, middle_grad, last_grad, proj_grad), n)
    lateral_grad, fast_grads = stage10(lat_term, packed, n)
    return (unrows(slow_out), unraw(fast_out), unrows(slow_grad), unraw(fast_grad),
            lateral_grad.T, *small[7:],
            *small[:5], *fast_grads, *small[5:7])


def solution(mesh):
    in_specs = (
        P("fsdp", None, None, None),
        P("fsdp", None, None, None),
        P("fsdp", None),
        P(None, "fsdp"),
        P("fsdp", None),
        P("fsdp", None),
        P("fsdp", None),
        P("fsdp", None),
        P(None, "fsdp"),
        P(None, "fsdp"),
        P(None, "fsdp"),
        P(None, "fsdp"),
        P(None, "fsdp"),
        P(),
        P(),
        P(),
        P(),
        P(),
        P(),
        P("fsdp", None, None, None),
        P("fsdp", None, None, None),
    )
    out_specs = (
        P("fsdp", None, None, None),
        P("fsdp", None, None, None),
        P("fsdp", None, None, None),
        P("fsdp", None, None, None),
        P(None, "fsdp"),
        P("fsdp", None),
        P("fsdp", None),
        P("fsdp", None),
        P("fsdp", None),
        P(None, "fsdp"),
        P(None, "fsdp"),
        P(None, "fsdp"),
        P(None, "fsdp"),
        P(None, "fsdp"),
        P(),
        P(),
        P(),
        P(),
        P(),
        P(),
    )
    return jax.shard_map(shards, mesh=mesh, in_specs=in_specs, out_specs=out_specs, check_vma=False)
```
